32 devices in a mesh: group: 2 (over y), ctx: 4 (over z), section: 2 (over x), rep: 2 (over core).
Axes of the slice: x: 2, y: 2, z: 4, core: 2. Of those that a mesh axis runs over, the one named last changes fastest.
Arguments:
- stream: bfloat16 [1024, 4096], P(('group', 'ctx'), ('section', 'rep')), parts along dimension 0, may hold values from -12 to 12
- query_proj: bfloat16 [1024, 4096], P(('group', 'ctx'), ('section', 'rep')), parts along dimension 0, may hold values from -105 to 105
- key_proj: bfloat16 [1024, 256], P(('group', 'ctx')), parts along dimension 0, may hold values from -4 to 4
- value_projected: bfloat16 [1024, 256], P(('group', 'ctx')), parts along dimension 0, may hold values from -6 to 6
- expert_ids: int32 [1024, 2], P(('group', 'ctx')), parts along dimension 0, may hold values from 0 to 3, all different within a row; in each aligned block of 128 rows (0 to 127, 128 to 255, ...) at most 80 rows name the same one
- expert_home: int32 [4], replicated, may hold values from 0 to 3, each once
- router: bfloat16 [4096, 4], P(('section', 'rep')), may hold values from -0.09375 to 0.09375
- norm_gain: bfloat16 [4096], P(('section', 'rep')), may hold values from 0.25 to 1.75
- w_gate: bfloat16 [4, 4096, 768], P('ctx', ('section', 'rep')), may hold values from -0.09375 to 0.09375
- w_up: bfloat16 [4, 4096, 768], P('ctx', ('section', 'rep')), may hold values from -0.09375 to 0.09375
- w_down: bfloat16 [4, 768, 4096], P('ctx', None, ('section', 'rep')), may hold values from -0.21875 to 0.21875
Outputs:
- result: bfloat16 [1024, 4096], P(('group', 'ctx'), ('section', 'rep')), parts along dimension 0
The draws below stay inside these ranges and needn't reach their ends.
There are 2 independent parts, one for each index of `group`. The reference program is written for one: setup_inputs(seed, part) draws one part's arguments, and reference() takes and returns one part's arrays. A program takes and returns all parts, laid end to end along the dimension named above; an argument that names none is the same for every part. Nothing has to cross between parts.
Inputs may be any that keep to these rules, and one draw needn't show every extreme that they name: `expert_ids`: in each token's row the 2 experts differ; within the 128 tokens of one index of ctx no expert is chosen more than 80 times. `expert_home`: each index of ctx holds exactly one expert.
All inputs are finite; a program needn't handle non-finite values.
Results may differ from the reference program's by a relative error of at most 0.0085.
Values may be sent and summed in bfloat16 or wider, within the bound.
No kernel may reach another device: no remote copies, remote signals or barrier semaphores. Data moves between devices by JAX's collectives and lax.ppermute only.
A program may use at most 64 MiB of HBM per device.

```python
import math
import jax
import jax.numpy as jnp
import numpy as np
from jax import lax

D = 4096
HEAD_SIZE = 128
QUERY_HEADS = 32
KEY_VALUE_HEADS = 2
HID = 768
TOK_DEV = 128
EXPERTS = 4
TOP = 2
BLOCK_TOKENS = 512
CAP = 80
N_SECTION = 2
N_REP = 2


def drawn_pair(key):
    start_offset = jax.random.fold_in(key, 4242)
    key_sample = jnp.clip(jax.random.normal(jax.random.fold_in(start_offset, 1), (BLOCK_TOKENS, KEY_VALUE_HEADS, HEAD_SIZE), jnp.float32), -4.0, 4.0)
    query_sample = jnp.clip(jax.random.normal(jax.random.fold_in(start_offset, 2), (BLOCK_TOKENS, KEY_VALUE_HEADS, QUERY_HEADS // KEY_VALUE_HEADS, HEAD_SIZE), jnp.float32), -4.0, 4.0)
    return (query_sample.reshape(BLOCK_TOKENS, QUERY_HEADS * HEAD_SIZE), key_sample.reshape(BLOCK_TOKENS, KEY_VALUE_HEADS * HEAD_SIZE))


def draw_query_proj(key, part):
    return drawn_pair(key)[0].astype(jnp.bfloat16)


def draw_key_proj(key, part):
    return drawn_pair(key)[1].astype(jnp.bfloat16)


def draw_stream(key, part):
    start_offset = jax.random.fold_in(key, 777)
    column_scale = jnp.linspace(0.5, 1.5, D)
    values = jnp.clip(jax.random.normal(jax.random.fold_in(start_offset, 3), (BLOCK_TOKENS, D), jnp.float32), -6.0, 6.0)
    return (values * column_scale[None, :]).astype(jnp.bfloat16)


def level_of(own_key, extent, split, smallest, largest):
    def one(dim, shards_of):
        heights = jax.random.uniform(jax.random.fold_in(jax.random.fold_in(own_key, 6), dim), (shards_of,), jnp.float32, smallest / len(split), largest / len(split))
        return jnp.repeat(jnp.exp(heights), extent[dim] // shards_of).reshape((-1,) + (1,) * (len(extent) - dim - 1))

    factor_of = one(*split[0])
    for cut in split[1:]:
        factor_of = factor_of * one(*cut)
    return factor_of


def deal_out(rng, own, number, rows, number_of, top, most, slope):
    sequence = jax.random.permutation(rng, number_of)
    crowded, usual = load_shares(number_of, rows * top, most, slope, True), load_shares(number_of, rows * top, most, slope, False)
    places = jnp.arange(number_of)

    def named(sizes, offset_by):
        used = int((sizes > 0).sum())
        fixed = max(1, used // 4)
        passed = fixed + (places - fixed + offset_by * (used - fixed)) % max(1, number_of - fixed)
        return jnp.zeros((number_of,), jnp.int32).at[sequence[jnp.where(places < fixed, places, passed)]].set(jnp.asarray(sizes, jnp.int32))

    sizes = jnp.where(number % 4 == 0, named(crowded, number // 4), named(usual, number - number // 4 - 1))
    mixed = jax.random.permutation(jax.random.fold_in(own, 3), number_of)
    giver, receiver = mixed[0:number_of // 2 * 2:2], mixed[1:number_of // 2 * 2:2]
    margin = jnp.minimum(sizes[giver] - 1, most - sizes[receiver]) // 2
    margin = jnp.where((giver == sequence[0]) | (receiver == sequence[0]) | (sizes[receiver] == 0), 0, jnp.maximum(margin, 0))
    passed = jax.random.randint(jax.random.fold_in(own, 4), (number_of // 2,), 0, 1 << 20) % (margin + 1)
    sizes = sizes.at[giver].add(-passed).at[receiver].add(passed)
    labels = jnp.searchsorted(jnp.cumsum(sizes), jnp.arange(rows * top), side="right").astype(jnp.int32)
    table = labels.reshape(top, rows).T
    table = table[jax.random.permutation(jax.random.fold_in(own, 1), rows)]
    offset_by = jax.random.randint(jax.random.fold_in(own, 2), (rows, 1), 0, top)
    return jnp.take_along_axis(table, (jnp.arange(top)[None, :] + offset_by) % top, axis=1)


def load_shares(amount, total, bound, skew, full):
    portions = [(1 << 20) // math.isqrt(rank ** skew) + 1 for rank in range(1, amount + 1)]
    largest = bound if full else min(bound, max(-(-total // amount), total * portions[0] // sum(portions)))
    least = 1 if total - largest >= amount - 1 else 0
    counts, spare = [largest] + [least] * (amount - 1), total - largest - least * (amount - 1)
    while spare > 0:
        candidates = [i for i in range(1, amount) if counts[i] < largest] or [i for i in range(1, amount) if counts[i] < bound]
        whole, left = sum([portions[i] for i in candidates]), spare
        for i in candidates:
            addition = min(bound - counts[i], max(1, left * portions[i] // whole), spare)
            counts[i] = counts[i] + addition
            spare = spare - addition
    return np.array(counts)


def centred(stream_key, extent, deviation, most, cuts=(), kind=jnp.bfloat16):
    factor_of = level_of(stream_key, extent, cuts, -0.22, 0.18) if cuts else 1.0
    result = jax.random.normal(stream_key, extent, jnp.float32) * deviation * factor_of
    return jnp.minimum(jnp.maximum(result, -most), most).astype(kind)


def setup_inputs(seed: int = 0, part: int = 0) -> dict:
    key_list = jax.random.split(jax.random.key(seed), 12)
    own_keys = jax.random.split(jax.random.fold_in(key_list[11], part), 12)
    stream = draw_stream(jax.random.fold_in(jax.random.fold_in(key_list[11], part), 71), part)
    query_proj = draw_query_proj(jax.random.fold_in(jax.random.fold_in(key_list[11], part), 71), part)
    key_proj = draw_key_proj(jax.random.fold_in(jax.random.fold_in(key_list[11], part), 71), part)
    value_projected = centred(own_keys[3], (BLOCK_TOKENS, KEY_VALUE_HEADS * HEAD_SIZE), 1.0, 6.0, ((0, 4),))
    expert_ids_keys = jax.random.split(jax.random.fold_in(own_keys[4], 1), BLOCK_TOKENS // TOK_DEV)
    expert_ids_turns = jax.random.permutation(jax.random.fold_in(own_keys[4], 3), BLOCK_TOKENS // TOK_DEV)
    expert_ids = jax.vmap(lambda own, number: deal_out(jax.random.fold_in(own_keys[4], 2), own, number, TOK_DEV, EXPERTS, TOP, CAP, 2))(expert_ids_keys, expert_ids_turns).reshape((BLOCK_TOKENS, TOP))
    expert_home = jax.random.permutation(key_list[5], EXPERTS).astype(jnp.int32)
    router = centred(key_list[6], (D, EXPERTS), D ** -0.5, 0.09375, ((0, 4),))
    norm_gain = jnp.clip(1.0 + 0.15 * jax.random.normal(key_list[7], (D,), jnp.float32), 0.25, 1.75).astype(jnp.bfloat16)
    w_gate = centred(key_list[8], (EXPERTS, D, HID), D ** -0.5, 0.09375, ((0, 4), (1, 4)))
    w_up = centred(key_list[9], (EXPERTS, D, HID), D ** -0.5, 0.09375, ((0, 4), (1, 4)))
    w_down = centred(key_list[10], (EXPERTS, HID, D), HID ** -0.5, 0.21875, ((0, 4), (2, 4)))
    return dict(stream=stream, query_proj=query_proj, key_proj=key_proj, value_projected=value_projected, expert_ids=expert_ids, expert_home=expert_home, router=router, norm_gain=norm_gain, w_gate=w_gate, w_up=w_up, w_down=w_down)


epsilon = 1e-06

def attention_rows(query_block_rows, first_row, key_gathered, value_gathered):
    block_length_rows = query_block_rows.shape[0]
    query_matrix = query_block_rows.astype(jnp.float32).reshape(block_length_rows, KEY_VALUE_HEADS, QUERY_HEADS // KEY_VALUE_HEADS, HEAD_SIZE)
    key_subset = key_gathered.astype(jnp.float32).reshape(BLOCK_TOKENS, KEY_VALUE_HEADS, HEAD_SIZE)
    value_subset = value_gathered.astype(jnp.float32).reshape(BLOCK_TOKENS, KEY_VALUE_HEADS, HEAD_SIZE)
    scores = jnp.einsum('tgha,pga->ghtp', query_matrix, key_subset) * (1.0 / math.sqrt(HEAD_SIZE))
    query_pos = first_row + jnp.arange(block_length_rows, dtype=jnp.int32)
    key_pos = jnp.arange(BLOCK_TOKENS, dtype=jnp.int32)
    visible = query_pos[:, None] >= key_pos[None, :]
    scores = jnp.where(visible, scores, -1e+30)
    top_score = lax.optimization_barrier(jnp.max(scores, axis=-1, keepdims=True))
    expo = jnp.where(visible, jnp.exp(scores - top_score), 0.0)
    total = lax.optimization_barrier(jnp.sum(expo, axis=-1))
    rounded = lax.optimization_barrier(expo.astype(jnp.bfloat16))
    mixed = jnp.einsum('ghtp,pga->ghta', rounded.astype(jnp.float32), value_subset) / total[..., None]
    return jnp.transpose(mixed, (2, 0, 1, 3)).reshape(block_length_rows, QUERY_HEADS * HEAD_SIZE)

def block_attention(queries, key_gathered, value_gathered):
    blocks = BLOCK_TOKENS // TOK_DEV
    query_blocks = queries.reshape(blocks, TOK_DEV, QUERY_HEADS * HEAD_SIZE)
    firsts = jnp.arange(blocks, dtype=jnp.int32) * TOK_DEV

    def one_block(packed):
        return attention_rows(packed[0], packed[1], key_gathered, value_gathered)
    return lax.map(one_block, (query_blocks, firsts)).reshape(BLOCK_TOKENS, QUERY_HEADS * HEAD_SIZE)

def split_product(row_block, weight):
    shards = N_SECTION * N_REP
    width = D // shards
    rows = row_block.astype(jnp.float32).reshape(row_block.shape[0], shards, width)
    parts = weight.astype(jnp.float32).reshape(shards, width, HID)
    partial_value = jnp.einsum('rsd,sdh->srh', rows, parts)
    rounded = lax.optimization_barrier(partial_value.astype(jnp.bfloat16))
    return lax.optimization_barrier(jnp.sum(rounded.astype(jnp.float32), axis=0))

def expert_mix(normed, chosen, gates, home_row, gate_set, up_set, down_set):
    flat_ids = chosen.reshape(-1).astype(jnp.int32)
    flat_tok = (jnp.arange(BLOCK_TOKENS * TOP, dtype=jnp.int32) // TOP).astype(jnp.int32)
    flat_gate = gates.reshape(-1)
    limit = EXPERTS * CAP

    def visit(total, expert):
        member = flat_ids == expert
        row_index = jnp.nonzero(member, size=limit, fill_value=0)[0].astype(jnp.int32)
        live = (jnp.arange(limit, dtype=jnp.int32) < jnp.sum(member.astype(jnp.int32))).astype(jnp.float32)
        token_index = flat_tok[row_index]
        row_block = normed[token_index]
        device_slot = home_row[expert]
        gate_act = split_product(row_block, gate_set[device_slot])
        up_act = split_product(row_block, up_set[device_slot])
        product = (jax.nn.silu(gate_act) * up_act).astype(jnp.bfloat16)
        answer = jnp.dot(product, down_set[device_slot], preferred_element_type=jnp.float32).astype(jnp.bfloat16)
        answer = lax.optimization_barrier(answer)
        weight_col = flat_gate[row_index] * live
        total = total.at[token_index].add(weight_col[:, None] * answer.astype(jnp.float32))
        return (total, None)
    total, ignored = lax.scan(visit, jnp.zeros((BLOCK_TOKENS, D), jnp.float32), jnp.arange(EXPERTS, dtype=jnp.int32))
    return total

def reference(stream, query_proj, key_proj, value_projected, expert_ids, expert_home, router, norm_gain, w_gate, w_up, w_down):
    attended = block_attention(query_proj, key_proj, value_projected)
    hidden = stream.astype(jnp.float32) + attended
    mean_sq = lax.optimization_barrier(jnp.mean(hidden * hidden, axis=-1, keepdims=True))
    normed = (hidden * lax.rsqrt(mean_sq + epsilon) * norm_gain.astype(jnp.float32)).astype(jnp.bfloat16)
    logits = jnp.dot(normed, router, preferred_element_type=jnp.float32)
    picked = jnp.take_along_axis(logits, expert_ids.astype(jnp.int32), axis=1)
    squashed = jax.nn.sigmoid(picked)
    gates = squashed / lax.optimization_barrier(jnp.sum(squashed, axis=-1, keepdims=True))
    mixed = expert_mix(normed, expert_ids, gates, expert_home.astype(jnp.int32), w_gate, w_up, w_down)
    return (hidden + mixed).astype(jnp.bfloat16)
```

```python
import functools
import math

import jax
import jax.numpy as jnp
from jax import lax
from jax.experimental import pallas as pl
from jax.experimental.pallas import tpu as pltpu
from jax.sharding import PartitionSpec as P

HEAD_SIZE = 128
LANES = 128
EPSILON = 1e-06
HIDDEN_MASK = -1e30
VMEM_LIMIT = 48 * 1024 * 1024

F32 = jnp.float32
BF16 = jnp.bfloat16
NT = (((1,), (1,)), ((), ()))


def dot(a, b):
    return jnp.dot(a, b, preferred_element_type=F32)


def dot_nt(a, b):
    return lax.dot_general(a, b, NT, preferred_element_type=F32)


def vmem_call(body, out_shape, n_scalar, n_in, scratch=(), flops=0, bytes_accessed=0):
    multi = isinstance(out_shape, (tuple, list))
    n_out = len(out_shape) if multi else 1
    whole = pl.BlockSpec(memory_space=pltpu.VMEM)
    return pl.pallas_call(
        body,
        out_shape=out_shape,
        in_specs=[pl.BlockSpec(memory_space=pltpu.SMEM)] * n_scalar + [whole] * n_in,
        out_specs=[whole] * n_out if multi else whole,
        scratch_shapes=list(scratch),
        compiler_params=pltpu.CompilerParams(vmem_limit_bytes=VMEM_LIMIT),
        cost_estimate=pl.CostEstimate(
            flops=flops, bytes_accessed=bytes_accessed, transcendentals=0
        ),
    )


def attend_kernel(n, cap, place_ref, q_ref, stream_ref, gain_ref, router_ref, target_ref, *rest):
    kv_refs, (hidden_ref, stats_ref), row_refs, (k_all, v_all, gained) = (
        rest[:n],
        rest[n : n + 2],
        rest[n + 2 : 2 * n + 2],
        rest[2 * n + 2 :],
    )
    place = place_ref[0]
    tokens = q_ref.shape[0]
    heads = q_ref.shape[1] // HEAD_SIZE
    for back in range(n):
        rows = slice(back * tokens, (back + 1) * tokens)
        k_all[rows, :] = kv_refs[back][:, :HEAD_SIZE]
        v_all[rows, :] = kv_refs[back][:, HEAD_SIZE:]
    row = lax.broadcasted_iota(jnp.int32, (tokens, n * tokens), 0)
    col = lax.broadcasted_iota(jnp.int32, (tokens, n * tokens), 1)
    visible = jnp.logical_and(col <= jnp.where(col < tokens, row, n * tokens), col < (place + 1) * tokens)
    squares = jnp.zeros((tokens, 1), F32)
    for head in range(heads):
        cols = slice(head * HEAD_SIZE, (head + 1) * HEAD_SIZE)
        scores = dot_nt(q_ref[:, cols], k_all[...]) * (1.0 / math.sqrt(HEAD_SIZE))
        scores = jnp.where(visible, scores, HIDDEN_MASK)
        expo = jnp.exp(scores - jnp.max(scores, axis=-1, keepdims=True))
        total = jnp.sum(expo, axis=-1, keepdims=True)
        attended = dot(expo.astype(BF16), v_all[...]) / total
        hidden = stream_ref[:, cols].astype(F32) + attended
        hidden_ref[:, cols] = hidden
        squares = squares + jnp.sum(hidden * hidden, axis=-1, keepdims=True)
        gained[:, cols] = (hidden * gain_ref[:, cols].astype(F32)).astype(BF16)
    values = gained[...]
    stats = dot_nt(router_ref[...], values)
    stat_row = lax.broadcasted_iota(jnp.int32, stats.shape, 0)
    squares_row = jnp.transpose(jnp.broadcast_to(squares, (tokens, LANES)))[0:1, :]
    stats_ref[...] = jnp.where(stat_row == stats.shape[0] - 1, squares_row, stats)
    earlier = (
        lax.broadcasted_iota(jnp.int32, (tokens, tokens), 0)
        < lax.broadcasted_iota(jnp.int32, (tokens, tokens), 1)
    ).astype(BF16)
    slot = lax.broadcasted_iota(jnp.int32, (cap, tokens), 0)
    for j in range(n):
        member = jnp.sum(
            (target_ref[...] == jnp.bitwise_xor(place, j)).astype(F32), axis=0, keepdims=True
        )
        rank = dot(jnp.broadcast_to(member, (8, tokens)).astype(BF16), earlier)[0:1, :]
        rank = jnp.where(member > 0.5, rank, -1.0).astype(jnp.int32)
        placing = (slot == rank).astype(F32).astype(BF16)
        row_refs[j][...] = dot(placing, values).astype(BF16)


def up_kernel(n_blocks, rep_ref, gate_ref, up_ref, gain_ref, *rest):
    blocks, (keep_ref, send_ref) = rest[:n_blocks], rest[n_blocks:]
    half = gate_ref.shape[1] // 2
    cap = blocks[0].shape[0]
    mine = pl.multiple_of(rep_ref[0] * half, LANES)
    other = pl.multiple_of((1 - rep_ref[0]) * half, LANES)
    rows = (
        blocks[0][...] if n_blocks == 1 else jnp.concatenate([b[...] for b in blocks], axis=0)
    )
    plain = rows.astype(F32) / gain_ref[...].astype(F32)
    squares = jnp.sum(plain * plain, axis=-1, keepdims=True)
    high = squares.astype(BF16)
    low = (squares - high.astype(F32)).astype(BF16)
    lane = lax.broadcasted_iota(jnp.int32, (rows.shape[0], LANES), 1)
    send_ref[:, :half] = dot(rows, gate_ref[:, pl.ds(other, half)]).astype(BF16)
    send_ref[:, half : 2 * half] = dot(rows, up_ref[:, pl.ds(other, half)]).astype(BF16)
    send_ref[:, 2 * half :] = jnp.where(lane < LANES // 2, high.astype(F32), low.astype(F32)).astype(BF16)
    keep_ref[:, :half] = dot(rows, gate_ref[:, pl.ds(mine, half)])
    keep_ref[:, half : 2 * half] = dot(rows, up_ref[:, pl.ds(mine, half)])
    keep_ref[:, 2 * half :] = jnp.broadcast_to(squares, lane.shape)


def received_squares(ref, start):
    return jnp.sum(ref[:, start:].astype(F32), axis=-1, keepdims=True) * (2.0 / LANES)


def add_kernel(keep_ref, got_ref, sum_ref, send_ref):
    wide = keep_ref.shape[1] - LANES
    both = keep_ref[:, :wide] + got_ref[:, :wide].astype(F32)
    sum_ref[:, :wide] = both
    send_ref[:, :wide] = both.astype(BF16)
    squares = keep_ref[:, wide:] + received_squares(got_ref, wide)
    sum_ref[:, wide:] = squares
    high = squares.astype(BF16).astype(F32)
    lane = lax.broadcasted_iota(jnp.int32, squares.shape, 1)
    send_ref[:, wide:] = jnp.where(lane < LANES // 2, high, squares - high).astype(BF16)


def inner_kernel(features, sum_ref, got_ref, inner_ref):
    wide = sum_ref.shape[1] - LANES
    half = wide // 2
    squares = sum_ref[:, wide : wide + 1] + received_squares(got_ref, wide)
    scale = lax.rsqrt(squares * (1.0 / features) + EPSILON)
    gate = (sum_ref[:, :half] + got_ref[:, :half].astype(F32)) * scale
    up = (sum_ref[:, half:wide] + got_ref[:, half:wide].astype(F32)) * scale
    inner_ref[...] = (gate * jax.nn.sigmoid(gate) * up).astype(BF16)


def down_kernel(rep_ref, down_ref, mine_ref, other_ref, *out_refs):
    half = mine_ref.shape[1]
    mine = pl.multiple_of(rep_ref[0] * half, LANES)
    other = pl.multiple_of((1 - rep_ref[0]) * half, LANES)
    answer = dot(mine_ref[...], down_ref[pl.ds(mine, half), :]) + dot(
        other_ref[...], down_ref[pl.ds(other, half), :]
    )
    cap = out_refs[0].shape[0]
    for i, out_ref in enumerate(out_refs):
        out_ref[...] = answer[i * cap : (i + 1) * cap].astype(BF16)


def mix_kernel(n, features, experts, place_ref, hidden_ref, stats_ref, ids_ref, target_ref, *rest):
    answers, (out_ref, stacked) = rest[:n], rest[n:]
    place = place_ref[0]
    tokens = hidden_ref.shape[0]
    top = ids_ref.shape[1]
    cap = answers[0].shape[0]
    for j in range(n):
        stacked[j * cap : (j + 1) * cap, :] = answers[j][...]
    stats = jnp.transpose(stats_ref[...])
    last = stats.shape[1] - 1
    scale = lax.rsqrt(stats[:, last : last + 1] * (1.0 / features) + EPSILON)
    logits = stats * scale
    kinds = lax.broadcasted_iota(jnp.int32, stats.shape, 1)
    squashed = [
        jax.nn.sigmoid(
            jnp.sum(jnp.where(kinds == ids_ref[:, k : k + 1], logits, 0.0), axis=-1, keepdims=True)
        )
        for k in range(top)
    ]
    whole = functools.reduce(lambda a, b: a + b, squashed)
    blocks = jnp.bitwise_xor(lax.broadcasted_iota(jnp.int32, (tokens, LANES), 1), place)
    named = [target_ref[:, k : k + 1] == blocks for k in range(top)]
    member = functools.reduce(lambda a, b: a + b, [x.astype(F32) for x in named])
    later = (
        lax.broadcasted_iota(jnp.int32, (tokens, tokens), 0)
        > lax.broadcasted_iota(jnp.int32, (tokens, tokens), 1)
    ).astype(F32).astype(BF16)
    rank = dot(later, member.astype(BF16))
    rank = rank + lax.broadcasted_iota(jnp.int32, rank.shape, 1).astype(F32) * float(cap)
    slot = lax.broadcasted_iota(jnp.int32, (tokens, n * cap), 1)
    weights = jnp.zeros((tokens, n * cap), F32)
    for k in range(top):
        at = jnp.sum(jnp.where(named[k], rank, 0.0), axis=-1, keepdims=True).astype(jnp.int32)
        weights = weights + jnp.where(slot == at, squashed[k] / whole, 0.0)
    high = weights.astype(BF16)
    low = (weights - high.astype(F32)).astype(BF16)
    mixed = dot(high, stacked[...]) + dot(low, stacked[...])
    out_ref[...] = (hidden_ref[...] + mixed).astype(out_ref.dtype)


def swap(x, axis):
    return lax.ppermute(x, axis, [(0, 1), (1, 0)])


def direct(
    stream,
    query_proj,
    key_proj,
    value_projected,
    expert_ids,
    expert_home,
    router,
    norm_gain,
    w_gate,
    w_up,
    w_down,
):
    tokens, width = stream.shape
    top = expert_ids.shape[1]
    n = lax.axis_size("ctx")
    features = width * lax.axis_size(("section", "rep"))
    experts = router.shape[1]
    hid = w_gate.shape[2]
    cap = capacity_of(tokens, top, n)
    place = lax.axis_index("ctx").astype(jnp.int32)
    rep = lax.axis_index("rep").astype(jnp.int32)
    where = place.reshape(1)
    side = rep.reshape(1)
    heads = width // HEAD_SIZE
    group_width = features // key_proj.shape[1]
    kv_head = lax.axis_index(("section", "rep")) * heads // group_width

    def exchange(x, j):
        return lax.ppermute(x, "ctx", [(i, i ^ j) for i in range(n)])

    own_kv = jnp.concatenate(
        [
            lax.dynamic_slice_in_dim(a, kv_head * HEAD_SIZE, HEAD_SIZE, 1)
            for a in (key_proj, value_projected)
        ],
        axis=1,
    )
    kvs = [own_kv] + [
        lax.ppermute(own_kv, "ctx", [(i, i + back) for i in range(n - back)])
        for back in range(1, n)
    ]
    one_hot = expert_ids[:, :, None] == jnp.arange(experts, dtype=jnp.int32)[None, None, :]
    target = jnp.sum(jnp.where(one_hot, expert_home[None, None, :], 0), axis=-1)
    gain = norm_gain.reshape(1, width)
    stat_rows = -(-(experts + 1) // 8) * 8
    router_rows = jnp.pad(router.T, ((0, stat_rows - experts), (0, 0)))

    hidden, stats, *rows = vmem_call(
        functools.partial(attend_kernel, n, cap),
        [
            jax.ShapeDtypeStruct((tokens, width), F32),
            jax.ShapeDtypeStruct((stat_rows, tokens), F32),
        ]
        + [jax.ShapeDtypeStruct((cap, width), BF16)] * n,
        1,
        5 + n,
        scratch=[
            pltpu.VMEM((n * tokens, HEAD_SIZE), BF16),
            pltpu.VMEM((n * tokens, HEAD_SIZE), BF16),
            pltpu.VMEM((tokens, width), BF16),
        ],
        flops=4 * tokens * n * tokens * width,
        bytes_accessed=10 * tokens * width,
    )(where, query_proj, stream, gain, router_rows, target.T, *kvs)

    order = sorted(range(1, n), key=lambda j: (j < n // 2, j))
    arrived = {j: exchange(rows[j], j) for j in order}
    arrived[0] = rows[0]

    stats = stats + swap(stats, "rep")
    stats = stats + swap(stats, "section")

    far = [(j,) for j in order if j >= n // 2]
    near = tuple(j for j in range(n // 2))
    answers = {}
    for chain in far + [near]:
        count = len(chain) * cap
        wide = hid + LANES
        keep, send = vmem_call(
            functools.partial(up_kernel, len(chain)),
            [jax.ShapeDtypeStruct((count, wide), F32), jax.ShapeDtypeStruct((count, wide), BF16)],
            1,
            3 + len(chain),
            flops=4 * count * width * hid,
            bytes_accessed=4 * width * hid,
        )(side, w_gate[0], w_up[0], gain, *[arrived[j] for j in chain])
        both, send = vmem_call(
            add_kernel,
            [jax.ShapeDtypeStruct((count, wide), F32), jax.ShapeDtypeStruct((count, wide), BF16)],
            0,
            2,
            flops=count * wide,
            bytes_accessed=10 * count * wide,
        )(keep, swap(send, "rep"))
        inner = vmem_call(
            functools.partial(inner_kernel, features),
            jax.ShapeDtypeStruct((count, hid // 2), BF16),
            0,
            2,
            flops=4 * count * wide,
            bytes_accessed=6 * count * wide,
        )(both, swap(send, "section"))
        outs = vmem_call(
            down_kernel,
            [jax.ShapeDtypeStruct((cap, width), BF16)] * len(chain),
            1,
            3,
            flops=2 * count * hid * width,
            bytes_accessed=2 * hid * width,
        )(side, w_down[0], inner, swap(inner, "rep"))
        for j, out in zip(chain, outs):
            answers[j] = exchange(out, j) if j else out

    return vmem_call(
        functools.partial(mix_kernel, n, features, experts),
        jax.ShapeDtypeStruct((tokens, width), BF16),
        1,
        4 + n,
        scratch=[pltpu.VMEM((n * cap, width), BF16)],
        flops=4 * tokens * n * cap * width,
        bytes_accessed=6 * tokens * width + 2 * n * cap * width,
    )(where, hidden, stats, expert_ids, target, *[answers[j] for j in range(n)])


def capacity_of(tokens, top, n):
    return min(tokens, max(2, 5 * tokens * top // (4 * n)))


def score_update(running, query_matrix, query_pos, key_block, value_block, key_anchor):
    run_max, run_sum, run_acc = running
    key_len = key_block.shape[0]
    scores = jnp.einsum(
        "tha,pa->htp", query_matrix, key_block, preferred_element_type=jnp.float32
    ) * (1.0 / math.sqrt(HEAD_SIZE))
    key_pos = key_anchor + jnp.arange(key_len, dtype=jnp.int32)
    visible = query_pos[:, None] >= key_pos[None, :]
    scores = jnp.where(visible, scores, HIDDEN_MASK)
    new_max = jnp.maximum(run_max, jnp.max(scores, axis=-1))
    expo = jnp.where(visible, jnp.exp(scores - new_max[..., None]), 0.0)
    factor = jnp.exp(run_max - new_max)
    new_sum = run_sum * factor + jnp.sum(expo, axis=-1)
    weights = expo.astype(jnp.bfloat16)
    new_acc = run_acc * factor[..., None] + jnp.einsum(
        "htp,pa->hta", weights, value_block, preferred_element_type=jnp.float32
    )
    return (new_max, new_sum, new_acc)


def absorb_rows(running, query_matrix, query_pos, key_rows, value_rows, anchor):
    piece_len = key_rows.shape[0]
    if piece_len > 512 and piece_len % 512 == 0:
        blocks = piece_len // 512
        key_tiles = key_rows.reshape(blocks, 512, key_rows.shape[1])
        value_tiles = value_rows.reshape(blocks, 512, value_rows.shape[1])
        anchors = anchor + 512 * jnp.arange(blocks, dtype=jnp.int32)

        def advance(state_now, tile):
            return (
                score_update(state_now, query_matrix, query_pos, tile[0], tile[1], tile[2]),
                None,
            )

        running, ignored = lax.scan(advance, running, (key_tiles, value_tiles, anchors))
        return running
    return score_update(running, query_matrix, query_pos, key_rows, value_rows, anchor)


def general(
    stream,
    query_proj,
    key_proj,
    value_projected,
    expert_ids,
    expert_home,
    router,
    norm_gain,
    w_gate,
    w_up,
    w_down,
):
    tok_rows, local_width = stream.shape
    top_count = expert_ids.shape[1]
    columns = lax.axis_size("ctx")
    features = local_width * lax.axis_size(("section", "rep"))
    capacity = capacity_of(tok_rows, top_count, columns)
    place = lax.axis_index("ctx")
    feature_index = lax.axis_index(("section", "rep"))
    heads_dev = local_width // HEAD_SIZE
    group_width = features // key_proj.shape[1]
    kv_head = feature_index * heads_dev // group_width
    query_matrix = query_proj.reshape(tok_rows, heads_dev, HEAD_SIZE)
    query_pos = place * tok_rows + jnp.arange(tok_rows, dtype=jnp.int32)
    initial = (
        jnp.full((heads_dev, tok_rows), HIDDEN_MASK, jnp.float32),
        jnp.zeros((heads_dev, tok_rows), jnp.float32),
        jnp.zeros((heads_dev, tok_rows, HEAD_SIZE), jnp.float32),
    )
    key_single = lax.dynamic_slice_in_dim(key_proj, kv_head * HEAD_SIZE, HEAD_SIZE, 1)
    value_single = lax.dynamic_slice_in_dim(value_projected, kv_head * HEAD_SIZE, HEAD_SIZE, 1)
    run_max, run_sum, run_acc = absorb_rows(
        initial,
        query_matrix,
        query_pos,
        lax.all_gather(key_single, "ctx", axis=0, tiled=True),
        lax.all_gather(value_single, "ctx", axis=0, tiled=True),
        jnp.int32(0),
    )
    attended = jnp.transpose(run_acc / run_sum[..., None], (1, 0, 2)).reshape(tok_rows, local_width)
    hidden = stream.astype(jnp.float32) + attended
    total_sq = lax.psum(jnp.sum(hidden * hidden, axis=-1), ("section", "rep"))
    scale_rows = lax.rsqrt(total_sq / features + EPSILON)
    normed = (hidden * scale_rows[:, None] * norm_gain.astype(jnp.float32)[None, :]).astype(
        jnp.bfloat16
    )
    logits = lax.psum(dot(normed, router), ("section", "rep"))
    experts_all = logits.shape[1]
    one_hot = expert_ids[:, :, None] == jnp.arange(experts_all, dtype=jnp.int32)[None, None, :]
    picked = jnp.sum(jnp.where(one_hot, logits[:, None, :], 0.0), axis=-1)
    squashed = jax.nn.sigmoid(picked)
    gates = squashed / jnp.sum(squashed, axis=-1, keepdims=True)
    target = jnp.sum(jnp.where(one_hot, expert_home[None, None, :], 0), axis=-1)
    named = target[:, :, None] == jnp.arange(columns, dtype=jnp.int32)[None, None, :]
    member = jnp.any(named, axis=1).astype(jnp.bfloat16)
    before = jnp.tril(jnp.ones((tok_rows, tok_rows), jnp.bfloat16), -1)
    rank = dot(before, member).astype(jnp.int32)
    rank = jnp.sum(jnp.where(named, rank[:, None, :], 0), axis=-1)
    slot_index = (target * capacity + rank).reshape(-1)
    placing = slot_index[None, :] == jnp.arange(columns * capacity, dtype=jnp.int32)[:, None]
    placing = jnp.any(placing.reshape(columns * capacity, tok_rows, top_count), axis=-1).astype(
        jnp.bfloat16
    )
    outgoing = dot(placing, normed).astype(jnp.bfloat16)
    outgoing = outgoing.reshape(columns, capacity, local_width)
    received = lax.all_to_all(outgoing, "ctx", split_axis=0, concat_axis=0, tiled=True)
    flat_rows = received.reshape(-1, local_width)
    gate_part = dot(flat_rows, w_gate[0])
    up_part = dot(flat_rows, w_up[0])
    gate_full = lax.psum(gate_part.astype(jnp.bfloat16), ("section", "rep")).astype(jnp.float32)
    up_full = lax.psum(up_part.astype(jnp.bfloat16), ("section", "rep")).astype(jnp.float32)
    inner = (jax.nn.silu(gate_full) * up_full).astype(jnp.bfloat16)
    answer = dot(inner, w_down[0]).astype(jnp.bfloat16)
    returned = lax.all_to_all(
        answer.reshape(received.shape), "ctx", split_axis=0, concat_axis=0, tiled=True
    )
    flat_back = returned.reshape(columns * capacity, local_width)
    picked_rows = flat_back[slot_index].reshape(tok_rows, top_count, local_width)
    mixed = jnp.sum(gates[:, :, None] * picked_rows.astype(jnp.float32), axis=1)
    return (hidden + mixed).astype(jnp.bfloat16)


def solution(mesh):
    size = dict(mesh.shape)
    pairs = size["section"] == 2 and size["rep"] == 2
    short = size["ctx"] in (2, 4)
    placed = (
        P(("group", "ctx"), ("section", "rep")),
        P(("group", "ctx"), ("section", "rep")),
        P(("group", "ctx"), None),
        P(("group", "ctx"), None),
        P(("group", "ctx"), None),
        P(),
        P(("section", "rep"), None),
        P(("section", "rep")),
        P("ctx", ("section", "rep"), None),
        P("ctx", ("section", "rep"), None),
        P("ctx", None, ("section", "rep")),
    )
    return jax.shard_map(
        direct if pairs and short else general,
        mesh=mesh,
        in_specs=placed,
        out_specs=P(("group", "ctx"), ("section", "rep")),
        check_vma=False,
    )
```

```python
import functools
import math

import jax
import jax.numpy as jnp
from jax import lax
from jax.experimental import pallas as pl
from jax.experimental.pallas import tpu as pltpu
from jax.sharding import PartitionSpec as P

HEAD_SIZE = 128
LANES = 128
EPSILON = 1e-06
HIDDEN_MASK = -1e30
VMEM_LIMIT = 16 * 1024 * 1024

F32 = jnp.float32
BF16 = jnp.bfloat16
NT = (((1,), (1,)), ((), ()))


def dot(a, b):
    return jnp.dot(a, b, preferred_element_type=F32)


def dot_nt(a, b):
    return lax.dot_general(a, b, NT, preferred_element_type=F32)


def vmem_call(body, out_shape, scalars, arrays, after=(), scratch=(), remote=(), held=True):
    multi = isinstance(out_shape, (tuple, list))
    n_out = len(out_shape) if multi else 1
    n_given = len(scalars) + len(remote) + len(arrays)
    whole = pl.BlockSpec(memory_space=pltpu.VMEM)
    anywhere = pl.BlockSpec(memory_space=pl.ANY)

    def placed(x):
        return pltpu.VMEM(x.shape, x.dtype) if held else x

    def kernel(*refs):
        body(*refs[:n_given], *refs[n_given + len(after) :])

    kernel.__name__ = getattr(body, "func", body).__name__
    return pl.pallas_call(
        kernel,
        out_shape=[placed(x) for x in out_shape] if multi else placed(out_shape),
        in_specs=[pl.BlockSpec(memory_space=pltpu.SMEM)] * len(scalars)
        + [pl.BlockSpec(memory_space=pltpu.HBM)] * len(remote)
        + [whole] * len(arrays)
        + [anywhere] * len(after),
        out_specs=[whole] * n_out if multi else whole,
        scratch_shapes=list(scratch),
        compiler_params=pltpu.CompilerParams(vmem_limit_bytes=VMEM_LIMIT),
        cost_estimate=pl.CostEstimate(flops=1, bytes_accessed=1, transcendentals=0),
    )(
        *scalars,
        *[pltpu.with_memory_space_constraint(x, pltpu.HBM) for x in remote],
        *[pltpu.with_memory_space_constraint(x, pltpu.VMEM) for x in arrays],
        *after,
    )


def carry(copies):
    for copy in copies:
        copy.start()
    for copy in copies:
        copy.wait()


def prepare_kernel(experts, head_ref, rep_ref, key_in, value_in, q_in, stream_in, gain_in, router_in, ids_in, home_in, *rest):
    part_ref, key_ref, value_ref, q_ref, stream_ref, gain_ref, router_ref, ids_ref, target_ref = rest[:9]
    home_ref, sems = rest[9:]
    columns = pl.ds(pl.multiple_of(head_ref[0] * HEAD_SIZE, HEAD_SIZE), HEAD_SIZE)
    pairs = [
        (key_in.at[:, columns], key_ref),
        (value_in.at[:, columns], value_ref),
        (ids_in, ids_ref),
        (home_in, home_ref),
        (gain_in, gain_ref),
        (router_in, router_ref),
        (q_in, q_ref),
        (stream_in, stream_ref),
    ]
    carry([pltpu.make_async_copy(a, b, sems.at[i]) for i, (a, b) in enumerate(pairs)])
    ids = ids_ref[...]
    target = jnp.zeros(ids.shape, jnp.int32)
    for expert in range(experts):
        target = jnp.where(ids == expert, home_ref[0:1, expert : expert + 1], target)
    target_ref[...] = target

    @pl.when(rep_ref[0] == 0)
    def _():
        part_ref[...] = key_ref[...]

    @pl.when(rep_ref[0] == 1)
    def _():
        part_ref[...] = value_ref[...]


def attend_kernel(n, cap, place_ref, rep_ref, gate_in, up_in, down_in, q_ref, stream_ref, gain_ref, router_ref, target_ref, key_ref, value_ref, *rest):
    mine, theirs, rest = rest[: n - 1], rest[n - 1 : 2 * n - 2], rest[2 * n - 2 :]
    (hidden_ref, stats_ref), row_refs, weight_refs, (k_all, v_all, gained, sems) = (
        rest[:2],
        rest[2 : n + 2],
        rest[n + 2 : n + 5],
        rest[n + 5 :],
    )
    pairs = zip((gate_in, up_in, down_in), weight_refs)
    copies = [pltpu.make_async_copy(a, b, sems.at[i]) for i, (a, b) in enumerate(pairs)]
    for copy in copies:
        copy.start()
    place = place_ref[0]
    tokens = q_ref.shape[0]
    heads = q_ref.shape[1] // HEAD_SIZE
    row = lax.broadcasted_iota(jnp.int32, (tokens, tokens), 0)
    col = lax.broadcasted_iota(jnp.int32, (tokens, tokens), 1)
    pieces = [jnp.where(row >= col, 0.0, HIDDEN_MASK)]
    k_all[:tokens, :] = key_ref[...]
    v_all[:tokens, :] = value_ref[...]
    for i in range(n - 1):
        rows = slice((i + 1) * tokens, (i + 2) * tokens)
        seen = jnp.where(jnp.bitwise_xor(place, i + 1) < place, 0.0, HIDDEN_MASK)
        pieces.append(jnp.full((tokens, tokens), seen, F32))

        @pl.when(rep_ref[0] == 0)
        def _():
            k_all[rows, :] = mine[i][...]
            v_all[rows, :] = theirs[i][...]

        @pl.when(rep_ref[0] == 1)
        def _():
            k_all[rows, :] = theirs[i][...]
            v_all[rows, :] = mine[i][...]

    bias = jnp.concatenate(pieces, axis=1)
    squares = jnp.zeros((tokens, 1), F32)
    for head in range(heads):
        cols = slice(head * HEAD_SIZE, (head + 1) * HEAD_SIZE)
        scores = dot_nt(q_ref[:, cols], k_all[...]) * (1.0 / math.sqrt(HEAD_SIZE)) + bias
        expo = jnp.exp(scores - jnp.max(scores, axis=-1, keepdims=True))
        total = jnp.sum(expo, axis=-1, keepdims=True)
        attended = dot(expo.astype(BF16), v_all[...]) / total
        hidden = stream_ref[:, cols].astype(F32) + attended
        hidden_ref[:, cols] = hidden
        squares = squares + jnp.sum(hidden * hidden, axis=-1, keepdims=True)
        gained[:, cols] = (hidden * gain_ref[head : head + 1, :].astype(F32)).astype(BF16)
    values = gained[...]
    earlier = (row < col).astype(F32).astype(BF16)
    slot = lax.broadcasted_iota(jnp.int32, (cap, tokens), 0)
    for j in range(n):
        member = jnp.sum((target_ref[...] == jnp.bitwise_xor(place, j)).astype(F32), axis=0, keepdims=True)
        rank = dot(jnp.broadcast_to(member, (8, tokens)).astype(BF16), earlier)[0:1, :]
        rank = jnp.where(member > 0.5, rank, -1.0).astype(jnp.int32)
        placing = (slot == rank).astype(F32).astype(BF16)
        row_refs[j][...] = dot(placing, values).astype(BF16)
    squares_row = jnp.transpose(jnp.broadcast_to(squares, (tokens, LANES)))
    height = stats_ref.shape[0]
    stats_ref[...] = jnp.concatenate(
        [dot_nt(router_ref[...], values), squares_row[: height - router_ref.shape[0], :]], axis=0
    )
    for copy in copies:
        copy.wait()


def split_pair(x):
    high = x.astype(BF16).astype(F32)
    lane = lax.broadcasted_iota(jnp.int32, x.shape, 1)
    return jnp.where(lane < LANES // 2, high, x - high).astype(BF16)


def join_pair(ref, rows, start):
    return jnp.sum(ref[rows, start:].astype(F32), axis=-1, keepdims=True) * (2.0 / LANES)


def put_stats(ref, base, stats):
    height, tokens = stats.shape
    ref[base:, :] = jnp.zeros((ref.shape[0] - base, ref.shape[1]), BF16)
    terms = []
    for i in range(3):
        term = stats.astype(BF16)
        stats = stats - term.astype(F32)
        terms.append(term.astype(F32))
    pad = jnp.zeros((ref.shape[0] - base - height, 3 * tokens), F32)
    ref[base:, : 3 * tokens] = jnp.concatenate(
        [jnp.concatenate(terms, axis=1), pad], axis=0
    ).astype(BF16)


def get_stats(ref, base, like):
    height, tokens = like.shape
    parts = ref[base:, : 3 * tokens].astype(F32)[:height]
    return parts[:, :tokens] + parts[:, tokens : 2 * tokens] + parts[:, 2 * tokens :]


def up_kernel(with_stats, rep_ref, gate_ref, up_ref, gain_ref, *rest):
    rows_ref, keep_ref, first_ref, second_ref = rest[-4:]
    count = rows_ref.shape[0]
    half = gate_ref.shape[1] // 2
    mine = pl.multiple_of(rep_ref[0] * half, LANES)
    other = pl.multiple_of((1 - rep_ref[0]) * half, LANES)
    rows = rows_ref[...]
    squares = jnp.zeros((count, LANES), F32)
    for i in range(gain_ref.shape[0]):
        plain = rows[:, i * LANES : (i + 1) * LANES].astype(F32) / gain_ref[i : i + 1, :].astype(F32)
        squares = squares + plain * plain
    squares = jnp.broadcast_to(jnp.sum(squares, axis=-1, keepdims=True), (count, LANES))
    first_ref[...] = dot(rows, gate_ref[:, pl.ds(other, half)]).astype(BF16)
    second_ref[:count, :half] = dot(rows, up_ref[:, pl.ds(other, half)]).astype(BF16)
    second_ref[:count, half:] = split_pair(squares)
    keep_ref[:, :half] = dot(rows, gate_ref[:, pl.ds(mine, half)])
    keep_ref[:, half : 2 * half] = dot(rows, up_ref[:, pl.ds(mine, half)])
    keep_ref[:, 2 * half :] = squares
    if with_stats:
        put_stats(second_ref, count, rest[0][...])


def add_kernel(with_stats, *refs):
    keep_ref, first_ref, second_ref, sum_ref, send_ref = refs[with_stats : with_stats + 5]
    count = keep_ref.shape[0]
    wide = keep_ref.shape[1] - LANES
    half = first_ref.shape[1]
    for start, ref in ((0, first_ref), (half, second_ref)):
        both = keep_ref[:, start : start + half] + ref[:count, :half].astype(F32)
        sum_ref[:, start : start + half] = both
        send_ref[:count, start : start + half] = both.astype(BF16)
    squares = keep_ref[:, wide:] + join_pair(second_ref, slice(0, count), half)
    sum_ref[:, wide:] = squares
    send_ref[:count, wide:] = split_pair(squares)
    if with_stats:
        stats_ref, total_ref = refs[0], refs[-1]
        stats = stats_ref[...] + get_stats(second_ref, count, stats_ref)
        total_ref[...] = stats
        put_stats(send_ref, count, stats)


def inner_kernel(features, with_stats, *refs):
    sum_ref, got_ref, inner_ref = refs[with_stats : with_stats + 3]
    count = sum_ref.shape[0]
    wide = sum_ref.shape[1] - LANES
    half = wide // 2
    squares = sum_ref[:, wide : wide + 1] + join_pair(got_ref, slice(0, count), wide)
    scale = lax.rsqrt(squares * (1.0 / features) + EPSILON)
    gate = (sum_ref[:, :half] + got_ref[:count, :half].astype(F32)) * scale
    up = (sum_ref[:, half:wide] + got_ref[:count, half:wide].astype(F32)) * scale
    inner_ref[...] = (gate * jax.nn.sigmoid(gate) * up).astype(BF16)
    if with_stats:
        stats_ref, total_ref = refs[0], refs[-1]
        total_ref[...] = stats_ref[...] + get_stats(got_ref, count, stats_ref)


def down_kernel(rep_ref, down_ref, mine_ref, other_ref, out_ref):
    half = mine_ref.shape[1]
    mine = pl.multiple_of(rep_ref[0] * half, LANES)
    other = pl.multiple_of((1 - rep_ref[0]) * half, LANES)
    out_ref[...] = (
        dot(mine_ref[...], down_ref[pl.ds(mine, half), :])
        + dot(other_ref[...], down_ref[pl.ds(other, half), :])
    ).astype(BF16)


def gates_kernel(cap, features, place_ref, stats_ref, ids_ref, target_ref, *weight_refs):
    place = place_ref[0]
    top, tokens = ids_ref.shape
    stats = jnp.transpose(stats_ref[...])
    height = stats.shape[1]
    scale = lax.rsqrt(stats[:, height - 1 :] * (1.0 / features) + EPSILON)
    logits = stats * scale
    both = jnp.concatenate(
        [ids_ref[...], target_ref[...], jnp.zeros((8 - 2 * top, tokens), jnp.int32)], axis=0
    )
    both = jnp.transpose(both.astype(F32)).astype(jnp.int32)
    kinds = lax.broadcasted_iota(jnp.int32, stats.shape, 1)
    squashed = [
        jax.nn.sigmoid(
            jnp.sum(jnp.where(kinds == both[:, k : k + 1], logits, 0.0), axis=-1, keepdims=True)
        )
        for k in range(top)
    ]
    whole = functools.reduce(lambda a, b: a + b, squashed)
    blocks = jnp.bitwise_xor(lax.broadcasted_iota(jnp.int32, (tokens, LANES), 1), place)
    named = [both[:, top + k : top + k + 1] == blocks for k in range(top)]
    member = functools.reduce(lambda a, b: a + b, [x.astype(F32) for x in named])
    later = (
        lax.broadcasted_iota(jnp.int32, (tokens, tokens), 0)
        > lax.broadcasted_iota(jnp.int32, (tokens, tokens), 1)
    ).astype(F32).astype(BF16)
    rank = dot(later, member.astype(BF16))
    slot = lax.broadcasted_iota(jnp.int32, (tokens, cap), 1)
    for j, weights_ref in enumerate(weight_refs):
        weights = jnp.zeros((tokens, cap), F32)
        for k in range(top):
            at = jnp.where(named[k][:, j : j + 1], rank[:, j : j + 1], -1.0).astype(jnp.int32)
            weights = weights + jnp.where(slot == at, squashed[k] / whole, 0.0)
        high = weights.astype(BF16)
        weights_ref[:tokens, :] = high
        weights_ref[tokens:, :] = (weights - high.astype(F32)).astype(BF16)


def mix_kernel(count, partial_ref, *rest):
    weights, answers, out_ref = rest[:count], rest[count : 2 * count], rest[-1]
    tokens = partial_ref.shape[0]
    total = partial_ref[...]
    for weights_ref, answer_ref in zip(weights, answers):
        mixed = dot(weights_ref[...], answer_ref[...])
        total = total + (mixed[:tokens] + mixed[tokens:])
    out_ref[...] = total.astype(out_ref.dtype)


def swap(x, axis):
    return lax.ppermute(x, axis, [(0, 1), (1, 0)])


def direct(
    stream,
    query_proj,
    key_proj,
    value_projected,
    expert_ids,
    expert_home,
    router,
    norm_gain,
    w_gate,
    w_up,
    w_down,
):
    tokens, width = stream.shape
    top = expert_ids.shape[1]
    n = lax.axis_size("ctx")
    features = width * lax.axis_size(("section", "rep"))
    experts = router.shape[1]
    hid = w_gate.shape[2]
    wide = hid + LANES
    cap = capacity_of(tokens, top, n)
    where = lax.axis_index("ctx").astype(jnp.int32).reshape(1)
    side = lax.axis_index("rep").astype(jnp.int32).reshape(1)
    heads = width // HEAD_SIZE
    group_width = features // key_proj.shape[1]
    kv_head = (lax.axis_index(("section", "rep")) * heads // group_width).astype(jnp.int32).reshape(1)

    def exchange(x, j):
        return lax.ppermute(x, "ctx", [(i, i ^ j) for i in range(n)])

    def like(x):
        return jax.ShapeDtypeStruct(x.shape, x.dtype)

    gain = norm_gain.reshape(width // LANES, LANES)
    part, own_key, own_value, queries, stream, gain, router_rows, ids_rows, target = vmem_call(
        functools.partial(prepare_kernel, experts),
        [jax.ShapeDtypeStruct((tokens, HEAD_SIZE), BF16)] * 3
        + [like(x) for x in (query_proj, stream, gain, router.T)]
        + [jax.ShapeDtypeStruct((top, tokens), jnp.int32)] * 2,
        [kv_head, side],
        [],
        remote=[key_proj, value_projected, query_proj, stream, gain, router.T, expert_ids.T]
        + [expert_home.reshape(1, experts)],
        scratch=[pltpu.VMEM((1, experts), jnp.int32), pltpu.SemaphoreType.DMA((8,))],
    )
    distance = sorted(range(1, n), key=lambda j: (j < n // 2, j))
    mine = {j: exchange(part, j) for j in distance}
    theirs = {j: swap(mine[j], "rep") for j in distance}
    stat_rows = -(-(experts + 1) // 8) * 8

    weights = [w_gate[0], w_up[0], w_down[0]]
    hidden, stats, *rows = vmem_call(
        functools.partial(attend_kernel, n, cap),
        [
            jax.ShapeDtypeStruct((tokens, width), F32),
            jax.ShapeDtypeStruct((stat_rows, tokens), F32),
        ]
        + [jax.ShapeDtypeStruct((cap, width), BF16)] * n
        + [like(x) for x in weights],
        [where, side],
        [queries, stream, gain, router_rows, target, own_key, own_value]
        + [kept[j] for kept in (mine, theirs) for j in range(1, n)],
        remote=weights,
        scratch=[
            pltpu.VMEM((n * tokens, HEAD_SIZE), BF16),
            pltpu.VMEM((n * tokens, HEAD_SIZE), BF16),
            pltpu.VMEM((tokens, width), BF16),
            pltpu.SemaphoreType.DMA((3,)),
        ],
    )
    rows, (gate, up, down) = rows[:n], rows[n:]
    arrived = {j: exchange(rows[j], j) for j in distance}
    arrived[0] = rows[0]

    extra = -(-stat_rows // 16) * 16
    state = {}
    made = {"last": hidden, "stats": stats, "partial": hidden}

    def run(body, out_shape, scalars, arrays, held=True):
        outs = vmem_call(body, out_shape, scalars, arrays, after=[made["last"]], held=held)
        made["last"] = outs[0] if isinstance(outs, (tuple, list)) else outs
        return outs

    def stat_part(j):
        return (1, [made["stats"]], [like(stats)], extra) if j == 1 else (0, [], [], 0)

    def up_step(j):
        flag, given, made_too, more = stat_part(j)
        keep, first, second = run(
            functools.partial(up_kernel, flag),
            [
                jax.ShapeDtypeStruct((cap, wide), F32),
                jax.ShapeDtypeStruct((cap, hid // 2), BF16),
                jax.ShapeDtypeStruct((cap + more, hid // 2 + LANES), BF16),
            ],
            [side],
            [gate, up, gain] + given + [arrived[j]],
        )
        state[j] = (keep, swap(first, "rep"), swap(second, "rep"))

    def add_step(j):
        flag, given, made_too, more = stat_part(j)
        both, send, *rest = run(
            functools.partial(add_kernel, flag),
            [jax.ShapeDtypeStruct((cap, wide), F32), jax.ShapeDtypeStruct((cap + more, wide), BF16)]
            + made_too,
            [],
            given + list(state[j]),
        )
        if rest:
            made["stats"] = rest[0]
        state[j] = (both, swap(send, "section"))

    def inner_step(j):
        flag, given, made_too, more = stat_part(j)
        inner, *rest = run(
            functools.partial(inner_kernel, features, flag),
            [jax.ShapeDtypeStruct((cap, hid // 2), BF16)] + made_too,
            [],
            given + list(state[j]),
        )
        if rest:
            made["stats"] = rest[0]
        state[j] = (inner, swap(inner, "rep"))

    def down_step(j):
        answer = run(down_kernel, jax.ShapeDtypeStruct((cap, width), BF16), [side], [down, *state[j]])
        state[j] = exchange(answer, j) if j else answer

    def gates_step():
        made["weights"] = run(
            functools.partial(gates_kernel, cap, features),
            [jax.ShapeDtypeStruct((2 * tokens, cap), BF16)] * n,
            [where],
            [made["stats"], ids_rows, target],
        )

    def mix_step(blocks, dtype=F32, held=True):
        made["partial"] = run(
            functools.partial(mix_kernel, len(blocks)),
            jax.ShapeDtypeStruct((tokens, width), dtype),
            [],
            [made["partial"]] + [made["weights"][j] for j in blocks] + [state[j] for j in blocks],
            held=held,
        )

    steps = dict(u=up_step, a=add_step, i=inner_step, d=down_step, m=lambda j: mix_step([j]))
    chain = [0] + [distance[0], *distance[:0:-1]]
    plan = (
        *("u0", "a0", "u1", "u2", "i0", "a1", "a2", "u3", "i1", "d0", "d1"),
        *("a3", "i2", "g", "d2", "m0", "i3", "m1", "d3"),
    )
    for name in plan:
        if name == "g":
            gates_step()
        elif int(name[1]) < n - (name[0] == "m"):
            steps[name[0]](chain[int(name[1])])
    mix_step(chain[2:] if n > 2 else chain[1:], BF16, held=False)
    return made["partial"]


def capacity_of(tokens, top, n):
    return min(tokens, max(2, 5 * tokens * top // (4 * n)))


def score_update(running, query_matrix, query_pos, key_block, value_block, key_anchor):
    run_max, run_sum, run_acc = running
    key_len = key_block.shape[0]
    scores = jnp.einsum(
        "tha,pa->htp", query_matrix, key_block, preferred_element_type=jnp.float32
    ) * (1.0 / math.sqrt(HEAD_SIZE))
    key_pos = key_anchor + jnp.arange(key_len, dtype=jnp.int32)
    visible = query_pos[:, None] >= key_pos[None, :]
    scores = jnp.where(visible, scores, HIDDEN_MASK)
    new_max = jnp.maximum(run_max, jnp.max(scores, axis=-1))
    expo = jnp.where(visible, jnp.exp(scores - new_max[..., None]), 0.0)
    factor = jnp.exp(run_max - new_max)
    new_sum = run_sum * factor + jnp.sum(expo, axis=-1)
    weights = expo.astype(jnp.bfloat16)
    new_acc = run_acc * factor[..., None] + jnp.einsum(
        "htp,pa->hta", weights, value_block, preferred_element_type=jnp.float32
    )
    return (new_max, new_sum, new_acc)


def absorb_rows(running, query_matrix, query_pos, key_rows, value_rows, anchor):
    piece_len = key_rows.shape[0]
    if piece_len > 512 and piece_len % 512 == 0:
        blocks = piece_len // 512
        key_tiles = key_rows.reshape(blocks, 512, key_rows.shape[1])
        value_tiles = value_rows.reshape(blocks, 512, value_rows.shape[1])
        anchors = anchor + 512 * jnp.arange(blocks, dtype=jnp.int32)

        def advance(state_now, tile):
            return (
                score_update(state_now, query_matrix, query_pos, tile[0], tile[1], tile[2]),
                None,
            )

        running, ignored = lax.scan(advance, running, (key_tiles, value_tiles, anchors))
        return running
    return score_update(running, query_matrix, query_pos, key_rows, value_rows, anchor)


def general(
    stream,
    query_proj,
    key_proj,
    value_projected,
    expert_ids,
    expert_home,
    router,
    norm_gain,
    w_gate,
    w_up,
    w_down,
):
    tok_rows, local_width = stream.shape
    top_count = expert_ids.shape[1]
    columns = lax.axis_size("ctx")
    features = local_width * lax.axis_size(("section", "rep"))
    capacity = capacity_of(tok_rows, top_count, columns)
    place = lax.axis_index("ctx")
    feature_index = lax.axis_index(("section", "rep"))
    heads_dev = local_width // HEAD_SIZE
    group_width = features // key_proj.shape[1]
    kv_head = feature_index * heads_dev // group_width
    query_matrix = query_proj.reshape(tok_rows, heads_dev, HEAD_SIZE)
    query_pos = place * tok_rows + jnp.arange(tok_rows, dtype=jnp.int32)
    initial = (
        jnp.full((heads_dev, tok_rows), HIDDEN_MASK, jnp.float32),
        jnp.zeros((heads_dev, tok_rows), jnp.float32),
        jnp.zeros((heads_dev, tok_rows, HEAD_SIZE), jnp.float32),
    )
    key_single = lax.dynamic_slice_in_dim(key_proj, kv_head * HEAD_SIZE, HEAD_SIZE, 1)
    value_single = lax.dynamic_slice_in_dim(value_projected, kv_head * HEAD_SIZE, HEAD_SIZE, 1)
    run_max, run_sum, run_acc = absorb_rows(
        initial,
        query_matrix,
        query_pos,
        lax.all_gather(key_single, "ctx", axis=0, tiled=True),
        lax.all_gather(value_single, "ctx", axis=0, tiled=True),
        jnp.int32(0),
    )
    attended = jnp.transpose(run_acc / run_sum[..., None], (1, 0, 2)).reshape(tok_rows, local_width)
    hidden = stream.astype(jnp.float32) + attended
    total_sq = lax.psum(jnp.sum(hidden * hidden, axis=-1), ("section", "rep"))
    scale_rows = lax.rsqrt(total_sq / features + EPSILON)
    normed = (hidden * scale_rows[:, None] * norm_gain.astype(jnp.float32)[None, :]).astype(
        jnp.bfloat16
    )
    logits = lax.psum(dot(normed, router), ("section", "rep"))
    experts_all = logits.shape[1]
    one_hot = expert_ids[:, :, None] == jnp.arange(experts_all, dtype=jnp.int32)[None, None, :]
    picked = jnp.sum(jnp.where(one_hot, logits[:, None, :], 0.0), axis=-1)
    squashed = jax.nn.sigmoid(picked)
    gates = squashed / jnp.sum(squashed, axis=-1, keepdims=True)
    target = jnp.sum(jnp.where(one_hot, expert_home[None, None, :], 0), axis=-1)
    named = target[:, :, None] == jnp.arange(columns, dtype=jnp.int32)[None, None, :]
    member = jnp.any(named, axis=1).astype(jnp.bfloat16)
    before = jnp.tril(jnp.ones((tok_rows, tok_rows), jnp.bfloat16), -1)
    rank = dot(before, member).astype(jnp.int32)
    rank = jnp.sum(jnp.where(named, rank[:, None, :], 0), axis=-1)
    slot_index = (target * capacity + rank).reshape(-1)
    placing = slot_index[None, :] == jnp.arange(columns * capacity, dtype=jnp.int32)[:, None]
    placing = jnp.any(placing.reshape(columns * capacity, tok_rows, top_count), axis=-1).astype(
        jnp.bfloat16
    )
    outgoing = dot(placing, normed).astype(jnp.bfloat16)
    outgoing = outgoing.reshape(columns, capacity, local_width)
    received = lax.all_to_all(outgoing, "ctx", split_axis=0, concat_axis=0, tiled=True)
    flat_rows = received.reshape(-1, local_width)
    gate_part = dot(flat_rows, w_gate[0])
    up_part = dot(flat_rows, w_up[0])
    gate_full = lax.psum(gate_part.astype(jnp.bfloat16), ("section", "rep")).astype(jnp.float32)
    up_full = lax.psum(up_part.astype(jnp.bfloat16), ("section", "rep")).astype(jnp.float32)
    inner = (jax.nn.silu(gate_full) * up_full).astype(jnp.bfloat16)
    answer = dot(inner, w_down[0]).astype(jnp.bfloat16)
    returned = lax.all_to_all(
        answer.reshape(received.shape), "ctx", split_axis=0, concat_axis=0, tiled=True
    )
    flat_back = returned.reshape(columns * capacity, local_width)
    picked_rows = flat_back[slot_index].reshape(tok_rows, top_count, local_width)
    mixed = jnp.sum(gates[:, :, None] * picked_rows.astype(jnp.float32), axis=1)
    return (hidden + mixed).astype(jnp.bfloat16)


def solution(mesh):
    size = dict(mesh.shape)
    pairs = size["section"] == 2 and size["rep"] == 2
    short = size["ctx"] in (2, 4)
    placed = (
        P(("group", "ctx"), ("section", "rep")),
        P(("group", "ctx"), ("section", "rep")),
        P(("group", "ctx"), None),
        P(("group", "ctx"), None),
        P(("group", "ctx"), None),
        P(),
        P(("section", "rep"), None),
        P(("section", "rep")),
        P("ctx", ("section", "rep"), None),
        P("ctx", ("section", "rep"), None),
        P("ctx", None, ("section", "rep")),
    )
    return jax.shard_map(
        direct if pairs and short else general,
        mesh=mesh,
        in_specs=placed,
        out_specs=P(("group", "ctx"), ("section", "rep")),
        check_vma=False,
    )
```

```python
import functools
import math

import jax
import jax.numpy as jnp
from jax import lax
from jax.experimental import pallas as pl
from jax.experimental.pallas import tpu as pltpu
from jax.sharding import PartitionSpec as P

HEAD_SIZE = 128
LANES = 128
EPSILON = 1e-06
HIDDEN_MASK = -1e30
VMEM_LIMIT = 16 * 1024 * 1024

F32 = jnp.float32
BF16 = jnp.bfloat16
NT = (((1,), (1,)), ((), ()))


def dot(a, b):
    return jnp.dot(a, b, preferred_element_type=F32)


def dot_nt(a, b):
    return lax.dot_general(a, b, NT, preferred_element_type=F32)


def vmem_call(body, out_shape, scalars, arrays, after=(), scratch=(), remote=(), held=True):
    multi = isinstance(out_shape, (tuple, list))
    n_out = len(out_shape) if multi else 1
    n_given = len(scalars) + len(remote) + len(arrays)
    whole = pl.BlockSpec(memory_space=pltpu.VMEM)
    anywhere = pl.BlockSpec(memory_space=pl.ANY)

    def placed(x):
        return pltpu.VMEM(x.shape, x.dtype) if held else x

    def kernel(*refs):
        body(*refs[:n_given], *refs[n_given + len(after) :])

    kernel.__name__ = getattr(body, "func", body).__name__
    return pl.pallas_call(
        kernel,
        out_shape=[placed(x) for x in out_shape] if multi else placed(out_shape),
        in_specs=[pl.BlockSpec(memory_space=pltpu.SMEM)] * len(scalars)
        + [pl.BlockSpec(memory_space=pltpu.HBM)] * len(remote)
        + [whole] * len(arrays)
        + [anywhere] * len(after),
        out_specs=[whole] * n_out if multi else whole,
        scratch_shapes=list(scratch),
        compiler_params=pltpu.CompilerParams(vmem_limit_bytes=VMEM_LIMIT),
        cost_estimate=pl.CostEstimate(flops=1, bytes_accessed=1, transcendentals=0),
    )(
        *scalars,
        *[pltpu.with_memory_space_constraint(x, pltpu.HBM) for x in remote],
        *[pltpu.with_memory_space_constraint(x, pltpu.VMEM) for x in arrays],
        *after,
    )


def carry(copies):
    for copy in copies:
        copy.start()
    for copy in copies:
        copy.wait()


def prepare_kernel(head_ref, rep_ref, key_in, value_in, kv_ref, part_ref, sems):
    columns = pl.ds(pl.multiple_of(head_ref[0] * HEAD_SIZE, HEAD_SIZE), HEAD_SIZE)
    carry(
        [
            pltpu.make_async_copy(
                ref.at[:, columns], kv_ref.at[:, pl.ds(i * HEAD_SIZE, HEAD_SIZE)], sems.at[i]
            )
            for i, ref in enumerate((key_in, value_in))
        ]
    )
    for i in range(2):

        @pl.when(rep_ref[0] == i)
        def _():
            part_ref[...] = kv_ref[:, i * HEAD_SIZE : (i + 1) * HEAD_SIZE]


def fetch_kernel(experts, *refs):
    count = (len(refs) - 4) // 2
    sources, home_in, targets, (target_ref, home_ref, sems) = (
        refs[:count],
        refs[count],
        refs[count + 1 : 2 * count + 1],
        refs[2 * count + 1 :],
    )
    pairs = [(home_in, home_ref), *zip(sources, targets)]
    carry([pltpu.make_async_copy(a, b, sems.at[i]) for i, (a, b) in enumerate(pairs)])
    ids = targets[-1][...]
    target = jnp.zeros(ids.shape, jnp.int32)
    for expert in range(experts):
        target = jnp.where(ids == expert, home_ref[0:1, expert : expert + 1], target)
    target_ref[...] = target


def attend_kernel(n, cap, place_ref, rep_ref, gate_in, up_in, down_in, q_ref, stream_ref, gain_ref, router_ref, target_ref, kv_ref, *rest):
    (near_mine, near_theirs, far_mine, far_theirs), rest = rest[:4], rest[4:]
    (hidden_ref, stats_ref), row_refs, weight_refs, (k_all, v_all, gained, sems) = (
        rest[:2],
        rest[2 : n + 2],
        rest[n + 2 : n + 5],
        rest[n + 5 :],
    )
    pairs = zip((gate_in, up_in, down_in), weight_refs)
    copies = [pltpu.make_async_copy(a, b, sems.at[i]) for i, (a, b) in enumerate(pairs)]
    for copy in copies:
        copy.start()
    place = place_ref[0]
    tokens = q_ref.shape[0]
    heads = q_ref.shape[1] // HEAD_SIZE
    row = lax.broadcasted_iota(jnp.int32, (tokens, tokens), 0)
    col = lax.broadcasted_iota(jnp.int32, (tokens, tokens), 1)
    pieces = [jnp.where(row >= col, 0.0, HIDDEN_MASK)]
    rep = rep_ref[0]
    for block, (ref, offset) in enumerate(
        ((kv_ref, 0), (None, 1), (far_mine, 2 + rep), (far_theirs, 3 - rep))
    ):
        rows = slice(block * tokens, (block + 1) * tokens)
        if ref is not None:
            k_all[rows, :] = ref[:, :HEAD_SIZE]
            v_all[rows, :] = ref[:, HEAD_SIZE:]
        if block:
            seen = jnp.where(jnp.bitwise_xor(place, offset) < place, 0.0, HIDDEN_MASK)
            pieces.append(jnp.full((tokens, tokens), seen, F32))

    @pl.when(rep == 0)
    def _():
        k_all[tokens : 2 * tokens, :] = near_mine[...]
        v_all[tokens : 2 * tokens, :] = near_theirs[...]

    @pl.when(rep == 1)
    def _():
        k_all[tokens : 2 * tokens, :] = near_theirs[...]
        v_all[tokens : 2 * tokens, :] = near_mine[...]

    bias = jnp.concatenate(pieces, axis=1)
    stacked = jnp.concatenate(
        [q_ref[:, h * HEAD_SIZE : (h + 1) * HEAD_SIZE] for h in range(heads)], axis=0
    )
    scored = dot_nt(stacked, k_all[...])
    squares = jnp.zeros((tokens, 1), F32)
    for head in range(heads):
        cols = slice(head * HEAD_SIZE, (head + 1) * HEAD_SIZE)
        scores = scored[head * tokens : (head + 1) * tokens, :] * (1.0 / math.sqrt(HEAD_SIZE)) + bias
        expo = jnp.exp(scores - jnp.max(scores, axis=-1, keepdims=True))
        total = jnp.sum(expo, axis=-1, keepdims=True)
        attended = dot(expo.astype(BF16), v_all[...]) / total
        hidden = stream_ref[:, cols].astype(F32) + attended
        hidden_ref[:, cols] = hidden
        squares = squares + jnp.sum(hidden * hidden, axis=-1, keepdims=True)
        gained[:, cols] = (hidden * gain_ref[head : head + 1, :].astype(F32)).astype(BF16)
    values = gained[...]
    earlier = (row < col).astype(F32).astype(BF16)
    slot = lax.broadcasted_iota(jnp.int32, (cap, tokens), 0)
    for j in range(n):
        member = jnp.sum((target_ref[...] == jnp.bitwise_xor(place, j)).astype(F32), axis=0, keepdims=True)
        rank = dot(jnp.broadcast_to(member, (8, tokens)).astype(BF16), earlier)[0:1, :]
        rank = jnp.where(member > 0.5, rank, -1.0).astype(jnp.int32)
        placing = (slot == rank).astype(F32).astype(BF16)
        row_refs[j][...] = dot(placing, values).astype(BF16)
    squares_row = jnp.transpose(jnp.broadcast_to(squares, (tokens, LANES)))
    height = stats_ref.shape[0]
    stats_ref[...] = jnp.concatenate(
        [dot_nt(router_ref[...], values), squares_row[: height - router_ref.shape[0], :]], axis=0
    )
    for copy in copies:
        copy.wait()


def split_pair(x):
    high = x.astype(BF16).astype(F32)
    lane = lax.broadcasted_iota(jnp.int32, x.shape, 1)
    return jnp.where(lane < LANES // 2, high, x - high).astype(BF16)


def join_pair(ref, rows, start):
    return jnp.sum(ref[rows, start:].astype(F32), axis=-1, keepdims=True) * (2.0 / LANES)


def put_stats(ref, base, stats):
    height, tokens = stats.shape
    ref[base:, :] = jnp.zeros((ref.shape[0] - base, ref.shape[1]), BF16)
    terms = []
    for i in range(3):
        term = stats.astype(BF16)
        stats = stats - term.astype(F32)
        terms.append(term.astype(F32))
    pad = jnp.zeros((ref.shape[0] - base - height, 3 * tokens), F32)
    ref[base:, : 3 * tokens] = jnp.concatenate(
        [jnp.concatenate(terms, axis=1), pad], axis=0
    ).astype(BF16)


def get_stats(ref, base, like):
    height, tokens = like.shape
    parts = ref[base:, : 3 * tokens].astype(F32)[:height]
    return parts[:, :tokens] + parts[:, tokens : 2 * tokens] + parts[:, 2 * tokens :]


def up_kernel(with_stats, rep_ref, gate_ref, up_ref, gain_ref, *rest):
    rows_ref, keep_ref, first_ref, second_ref = rest[-4:]
    count = rows_ref.shape[0]
    half = gate_ref.shape[1] // 2
    mine = pl.multiple_of(rep_ref[0] * half, LANES)
    other = pl.multiple_of((1 - rep_ref[0]) * half, LANES)
    rows = rows_ref[...]
    squares = jnp.zeros((count, LANES), F32)
    for i in range(gain_ref.shape[0]):
        plain = rows[:, i * LANES : (i + 1) * LANES].astype(F32) / gain_ref[i : i + 1, :].astype(F32)
        squares = squares + plain * plain
    squares = jnp.broadcast_to(jnp.sum(squares, axis=-1, keepdims=True), (count, LANES))
    first_ref[...] = dot(rows, gate_ref[:, pl.ds(other, half)]).astype(BF16)
    second_ref[:count, :half] = dot(rows, up_ref[:, pl.ds(other, half)]).astype(BF16)
    second_ref[:count, half:] = split_pair(squares)
    keep_ref[:, :half] = dot(rows, gate_ref[:, pl.ds(mine, half)])
    keep_ref[:, half : 2 * half] = dot(rows, up_ref[:, pl.ds(mine, half)])
    keep_ref[:, 2 * half :] = squares
    if with_stats:
        put_stats(second_ref, count, rest[0][...])


def add_kernel(with_stats, *refs):
    keep_ref, first_ref, second_ref, sum_ref, send_ref = refs[with_stats : with_stats + 5]
    count = keep_ref.shape[0]
    wide = keep_ref.shape[1] - LANES
    half = first_ref.shape[1]
    for start, ref in ((0, first_ref), (half, second_ref)):
        both = keep_ref[:, start : start + half] + ref[:count, :half].astype(F32)
        sum_ref[:, start : start + half] = both
        send_ref[:count, start : start + half] = both.astype(BF16)
    squares = keep_ref[:, wide:] + join_pair(second_ref, slice(0, count), half)
    sum_ref[:, wide:] = squares
    send_ref[:count, wide:] = split_pair(squares)
    if with_stats:
        stats_ref, total_ref = refs[0], refs[-1]
        stats = stats_ref[...] + get_stats(second_ref, count, stats_ref)
        total_ref[...] = stats
        put_stats(send_ref, count, stats)


def inner_kernel(features, with_stats, *refs):
    sum_ref, got_ref, inner_ref = refs[with_stats : with_stats + 3]
    count = sum_ref.shape[0]
    wide = sum_ref.shape[1] - LANES
    half = wide // 2
    squares = sum_ref[:, wide : wide + 1] + join_pair(got_ref, slice(0, count), wide)
    scale = lax.rsqrt(squares * (1.0 / features) + EPSILON)
    gate = (sum_ref[:, :half] + got_ref[:count, :half].astype(F32)) * scale
    up = (sum_ref[:, half:wide] + got_ref[:count, half:wide].astype(F32)) * scale
    inner_ref[...] = (gate * jax.nn.sigmoid(gate) * up).astype(BF16)
    if with_stats:
        stats_ref, total_ref = refs[0], refs[-1]
        total_ref[...] = stats_ref[...] + get_stats(got_ref, count, stats_ref)


def down_kernel(rep_ref, down_ref, mine_ref, other_ref, out_ref):
    half = mine_ref.shape[1]
    mine = pl.multiple_of(rep_ref[0] * half, LANES)
    other = pl.multiple_of((1 - rep_ref[0]) * half, LANES)
    out_ref[...] = (
        dot(mine_ref[...], down_ref[pl.ds(mine, half), :])
        + dot(other_ref[...], down_ref[pl.ds(other, half), :])
    ).astype(BF16)


def gates_kernel(cap, features, place_ref, stats_ref, ids_ref, target_ref, *weight_refs):
    place = place_ref[0]
    top, tokens = ids_ref.shape
    stats = jnp.transpose(stats_ref[...])
    height = stats.shape[1]
    scale = lax.rsqrt(stats[:, height - 1 :] * (1.0 / features) + EPSILON)
    logits = stats * scale
    both = jnp.concatenate(
        [ids_ref[...], target_ref[...], jnp.zeros((8 - 2 * top, tokens), jnp.int32)], axis=0
    )
    both = jnp.transpose(both.astype(F32)).astype(jnp.int32)
    kinds = lax.broadcasted_iota(jnp.int32, stats.shape, 1)
    squashed = [
        jax.nn.sigmoid(
            jnp.sum(jnp.where(kinds == both[:, k : k + 1], logits, 0.0), axis=-1, keepdims=True)
        )
        for k in range(top)
    ]
    whole = functools.reduce(lambda a, b: a + b, squashed)
    blocks = jnp.bitwise_xor(lax.broadcasted_iota(jnp.int32, (tokens, LANES), 1), place)
    named = [both[:, top + k : top + k + 1] == blocks for k in range(top)]
    member = functools.reduce(lambda a, b: a + b, [x.astype(F32) for x in named])
    later = (
        lax.broadcasted_iota(jnp.int32, (tokens, tokens), 0)
        > lax.broadcasted_iota(jnp.int32, (tokens, tokens), 1)
    ).astype(F32).astype(BF16)
    rank = dot(later, member.astype(BF16))
    slot = lax.broadcasted_iota(jnp.int32, (tokens, cap), 1)
    for j, weights_ref in enumerate(weight_refs):
        weights = jnp.zeros((tokens, cap), F32)
        for k in range(top):
            at = jnp.where(named[k][:, j : j + 1], rank[:, j : j + 1], -1.0).astype(jnp.int32)
            weights = weights + jnp.where(slot == at, squashed[k] / whole, 0.0)
        high = weights.astype(BF16)
        weights_ref[:tokens, :] = high
        weights_ref[tokens:, :] = (weights - high.astype(F32)).astype(BF16)


def mix_kernel(count, partial_ref, *rest):
    weights, answers, out_ref = rest[:count], rest[count : 2 * count], rest[-1]
    tokens = partial_ref.shape[0]
    total = partial_ref[...]
    for weights_ref, answer_ref in zip(weights, answers):
        mixed = dot(weights_ref[...], answer_ref[...])
        total = total + (mixed[:tokens] + mixed[tokens:])
    out_ref[...] = total.astype(out_ref.dtype)


def swap(x, axis):
    return lax.ppermute(x, axis, [(0, 1), (1, 0)])


def direct(
    stream,
    query_proj,
    key_proj,
    value_projected,
    expert_ids,
    expert_home,
    router,
    norm_gain,
    w_gate,
    w_up,
    w_down,
):
    tokens, width = stream.shape
    top = expert_ids.shape[1]
    n = lax.axis_size("ctx")
    features = width * lax.axis_size(("section", "rep"))
    experts = router.shape[1]
    hid = w_gate.shape[2]
    wide = hid + LANES
    cap = capacity_of(tokens, top, n)
    where = lax.axis_index("ctx").astype(jnp.int32).reshape(1)
    side = lax.axis_index("rep").astype(jnp.int32).reshape(1)
    heads = width // HEAD_SIZE
    group_width = features // key_proj.shape[1]
    kv_head = (lax.axis_index(("section", "rep")) * heads // group_width).astype(jnp.int32).reshape(1)

    def exchange(x, j):
        return lax.ppermute(x, "ctx", [(i, i ^ j) for i in range(n)])

    def like(x):
        return jax.ShapeDtypeStruct(x.shape, x.dtype)

    own_kv, part = vmem_call(
        prepare_kernel,
        [jax.ShapeDtypeStruct((tokens, w * HEAD_SIZE), BF16) for w in (2, 1)],
        [kv_head, side],
        [],
        remote=[key_proj, value_projected],
        scratch=[pltpu.SemaphoreType.DMA((2,))],
    )
    sources = [query_proj, stream, norm_gain.reshape(width // LANES, LANES), router.T, expert_ids.T]
    queries, stream, gain, router_rows, ids_rows, target = vmem_call(
        functools.partial(fetch_kernel, experts),
        [like(x) for x in sources] + [jax.ShapeDtypeStruct((top, tokens), jnp.int32)],
        [],
        [],
        remote=[*sources, expert_home.reshape(1, experts)],
        after=[part],
        scratch=[pltpu.VMEM((1, experts), jnp.int32), pltpu.SemaphoreType.DMA((6,))],
    )
    distance = sorted(range(1, n), key=lambda j: (j < n // 2, j))
    near_kv = exchange(part, 1)
    far_kv = lax.ppermute(
        own_kv, ("ctx", "rep"), [(2 * i + r, 2 * (i ^ (2 + r)) + r) for i in range(n) for r in range(2)]
    )
    stat_rows = -(-(experts + 1) // 8) * 8

    weights = [w_gate[0], w_up[0], w_down[0]]
    hidden, stats, *rows = vmem_call(
        functools.partial(attend_kernel, n, cap),
        [
            jax.ShapeDtypeStruct((tokens, width), F32),
            jax.ShapeDtypeStruct((stat_rows, tokens), F32),
        ]
        + [jax.ShapeDtypeStruct((cap, width), BF16)] * n
        + [like(x) for x in weights],
        [where, side],
        [queries, stream, gain, router_rows, target, own_kv, near_kv, swap(near_kv, "rep")]
        + [far_kv, swap(far_kv, "rep")],
        remote=weights,
        scratch=[
            pltpu.VMEM((n * tokens, HEAD_SIZE), BF16),
            pltpu.VMEM((n * tokens, HEAD_SIZE), BF16),
            pltpu.VMEM((tokens, width), BF16),
            pltpu.SemaphoreType.DMA((3,)),
        ],
    )
    rows, (gate, up, down) = rows[:n], rows[n:]
    arrived = {j: exchange(rows[j], j) for j in distance}
    arrived[0] = rows[0]

    extra = -(-stat_rows // 16) * 16
    state = {}
    made = {"last": hidden, "stats": stats, "partial": hidden}

    def run(body, out_shape, scalars, arrays, held=True):
        outs = vmem_call(body, out_shape, scalars, arrays, after=[made["last"]], held=held)
        made["last"] = outs[0] if isinstance(outs, (tuple, list)) else outs
        return outs

    def stat_part(j):
        return (1, [made["stats"]], [like(stats)], extra) if j == 1 else (0, [], [], 0)

    def up_step(j):
        flag, given, made_too, more = stat_part(j)
        keep, first, second = run(
            functools.partial(up_kernel, flag),
            [
                jax.ShapeDtypeStruct((cap, wide), F32),
                jax.ShapeDtypeStruct((cap, hid // 2), BF16),
                jax.ShapeDtypeStruct((cap + more, hid // 2 + LANES), BF16),
            ],
            [side],
            [gate, up, gain] + given + [arrived[j]],
        )
        state[j] = (keep, swap(first, "rep"), swap(second, "rep"))

    def add_step(j):
        flag, given, made_too, more = stat_part(j)
        both, send, *rest = run(
            functools.partial(add_kernel, flag),
            [jax.ShapeDtypeStruct((cap, wide), F32), jax.ShapeDtypeStruct((cap + more, wide), BF16)]
            + made_too,
            [],
            given + list(state[j]),
        )
        if rest:
            made["stats"] = rest[0]
        state[j] = (both, swap(send, "section"))

    def inner_step(j):
        flag, given, made_too, more = stat_part(j)
        inner, *rest = run(
            functools.partial(inner_kernel, features, flag),
            [jax.ShapeDtypeStruct((cap, hid // 2), BF16)] + made_too,
            [],
            given + list(state[j]),
        )
        if rest:
            made["stats"] = rest[0]
        state[j] = (inner, swap(inner, "rep"))

    def down_step(j):
        answer = run(down_kernel, jax.ShapeDtypeStruct((cap, width), BF16), [side], [down, *state[j]])
        state[j] = exchange(answer, j) if j else answer

    def gates_step():
        made["weights"] = run(
            functools.partial(gates_kernel, cap, features),
            [jax.ShapeDtypeStruct((2 * tokens, cap), BF16)] * n,
            [where],
            [made["stats"], ids_rows, target],
        )

    def mix_step(blocks, dtype=F32, held=True):
        made["partial"] = run(
            functools.partial(mix_kernel, len(blocks)),
            jax.ShapeDtypeStruct((tokens, width), dtype),
            [],
            [made["partial"]] + [made["weights"][j] for j in blocks] + [state[j] for j in blocks],
            held=held,
        )

    steps = dict(u=up_step, a=add_step, i=inner_step, d=down_step, m=lambda j: mix_step([j]))
    chain = [0] + [distance[0], *distance[:0:-1]]
    plan = (
        *("u0", "a0", "u1", "u2", "i0", "a1", "a2", "u3", "i1", "d0", "d1"),
        *("a3", "i2", "g", "d2", "m0", "i3", "m1", "d3"),
    )
    for name in plan:
        if name == "g":
            gates_step()
        elif int(name[1]) < n - (name[0] == "m"):
            steps[name[0]](chain[int(name[1])])
    early = [chain[int(name[1])] for name in plan if name[0] == "m" and int(name[1]) < n - 1]
    mix_step([j for j in chain if j not in early], BF16, held=False)
    return made["partial"]


def capacity_of(tokens, top, n):
    return min(tokens, max(2, 5 * tokens * top // (4 * n)))


def score_update(running, query_matrix, query_pos, key_block, value_block, key_anchor):
    run_max, run_sum, run_acc = running
    key_len = key_block.shape[0]
    scores = jnp.einsum(
        "tha,pa->htp", query_matrix, key_block, preferred_element_type=jnp.float32
    ) * (1.0 / math.sqrt(HEAD_SIZE))
    key_pos = key_anchor + jnp.arange(key_len, dtype=jnp.int32)
    visible = query_pos[:, None] >= key_pos[None, :]
    scores = jnp.where(visible, scores, HIDDEN_MASK)
    new_max = jnp.maximum(run_max, jnp.max(scores, axis=-1))
    expo = jnp.where(visible, jnp.exp(scores - new_max[..., None]), 0.0)
    factor = jnp.exp(run_max - new_max)
    new_sum = run_sum * factor + jnp.sum(expo, axis=-1)
    weights = expo.astype(jnp.bfloat16)
    new_acc = run_acc * factor[..., None] + jnp.einsum(
        "htp,pa->hta", weights, value_block, preferred_element_type=jnp.float32
    )
    return (new_max, new_sum, new_acc)


def absorb_rows(running, query_matrix, query_pos, key_rows, value_rows, anchor):
    piece_len = key_rows.shape[0]
    if piece_len > 512 and piece_len % 512 == 0:
        blocks = piece_len // 512
        key_tiles = key_rows.reshape(blocks, 512, key_rows.shape[1])
        value_tiles = value_rows.reshape(blocks, 512, value_rows.shape[1])
        anchors = anchor + 512 * jnp.arange(blocks, dtype=jnp.int32)

        def advance(state_now, tile):
            return (
                score_update(state_now, query_matrix, query_pos, tile[0], tile[1], tile[2]),
                None,
            )

        running, ignored = lax.scan(advance, running, (key_tiles, value_tiles, anchors))
        return running
    return score_update(running, query_matrix, query_pos, key_rows, value_rows, anchor)


def general(
    stream,
    query_proj,
    key_proj,
    value_projected,
    expert_ids,
    expert_home,
    router,
    norm_gain,
    w_gate,
    w_up,
    w_down,
):
    tok_rows, local_width = stream.shape
    top_count = expert_ids.shape[1]
    columns = lax.axis_size("ctx")
    features = local_width * lax.axis_size(("section", "rep"))
    capacity = capacity_of(tok_rows, top_count, columns)
    place = lax.axis_index("ctx")
    feature_index = lax.axis_index(("section", "rep"))
    heads_dev = local_width // HEAD_SIZE
    group_width = features // key_proj.shape[1]
    kv_head = feature_index * heads_dev // group_width
    query_matrix = query_proj.reshape(tok_rows, heads_dev, HEAD_SIZE)
    query_pos = place * tok_rows + jnp.arange(tok_rows, dtype=jnp.int32)
    initial = (
        jnp.full((heads_dev, tok_rows), HIDDEN_MASK, jnp.float32),
        jnp.zeros((heads_dev, tok_rows), jnp.float32),
        jnp.zeros((heads_dev, tok_rows, HEAD_SIZE), jnp.float32),
    )
    key_single = lax.dynamic_slice_in_dim(key_proj, kv_head * HEAD_SIZE, HEAD_SIZE, 1)
    value_single = lax.dynamic_slice_in_dim(value_projected, kv_head * HEAD_SIZE, HEAD_SIZE, 1)
    run_max, run_sum, run_acc = absorb_rows(
        initial,
        query_matrix,
        query_pos,
        lax.all_gather(key_single, "ctx", axis=0, tiled=True),
        lax.all_gather(value_single, "ctx", axis=0, tiled=True),
        jnp.int32(0),
    )
    attended = jnp.transpose(run_acc / run_sum[..., None], (1, 0, 2)).reshape(tok_rows, local_width)
    hidden = stream.astype(jnp.float32) + attended
    total_sq = lax.psum(jnp.sum(hidden * hidden, axis=-1), ("section", "rep"))
    scale_rows = lax.rsqrt(total_sq / features + EPSILON)
    normed = (hidden * scale_rows[:, None] * norm_gain.astype(jnp.float32)[None, :]).astype(
        jnp.bfloat16
    )
    logits = lax.psum(dot(normed, router), ("section", "rep"))
    experts_all = logits.shape[1]
    one_hot = expert_ids[:, :, None] == jnp.arange(experts_all, dtype=jnp.int32)[None, None, :]
    picked = jnp.sum(jnp.where(one_hot, logits[:, None, :], 0.0), axis=-1)
    squashed = jax.nn.sigmoid(picked)
    gates = squashed / jnp.sum(squashed, axis=-1, keepdims=True)
    target = jnp.sum(jnp.where(one_hot, expert_home[None, None, :], 0), axis=-1)
    named = target[:, :, None] == jnp.arange(columns, dtype=jnp.int32)[None, None, :]
    member = jnp.any(named, axis=1).astype(jnp.bfloat16)
    before = jnp.tril(jnp.ones((tok_rows, tok_rows), jnp.bfloat16), -1)
    rank = dot(before, member).astype(jnp.int32)
    rank = jnp.sum(jnp.where(named, rank[:, None, :], 0), axis=-1)
    slot_index = (target * capacity + rank).reshape(-1)
    placing = slot_index[None, :] == jnp.arange(columns * capacity, dtype=jnp.int32)[:, None]
    placing = jnp.any(placing.reshape(columns * capacity, tok_rows, top_count), axis=-1).astype(
        jnp.bfloat16
    )
    outgoing = dot(placing, normed).astype(jnp.bfloat16)
    outgoing = outgoing.reshape(columns, capacity, local_width)
    received = lax.all_to_all(outgoing, "ctx", split_axis=0, concat_axis=0, tiled=True)
    flat_rows = received.reshape(-1, local_width)
    gate_part = dot(flat_rows, w_gate[0])
    up_part = dot(flat_rows, w_up[0])
    gate_full = lax.psum(gate_part.astype(jnp.bfloat16), ("section", "rep")).astype(jnp.float32)
    up_full = lax.psum(up_part.astype(jnp.bfloat16), ("section", "rep")).astype(jnp.float32)
    inner = (jax.nn.silu(gate_full) * up_full).astype(jnp.bfloat16)
    answer = dot(inner, w_down[0]).astype(jnp.bfloat16)
    returned = lax.all_to_all(
        answer.reshape(received.shape), "ctx", split_axis=0, concat_axis=0, tiled=True
    )
    flat_back = returned.reshape(columns * capacity, local_width)
    picked_rows = flat_back[slot_index].reshape(tok_rows, top_count, local_width)
    mixed = jnp.sum(gates[:, :, None] * picked_rows.astype(jnp.float32), axis=1)
    return (hidden + mixed).astype(jnp.bfloat16)


def solution(mesh):
    size = dict(mesh.shape)
    pairs = size["section"] == 2 and size["rep"] == 2
    short = size["ctx"] == 4
    placed = (
        P(("group", "ctx"), ("section", "rep")),
        P(("group", "ctx"), ("section", "rep")),
        P(("group", "ctx"), None),
        P(("group", "ctx"), None),
        P(("group", "ctx"), None),
        P(),
        P(("section", "rep"), None),
        P(("section", "rep")),
        P("ctx", ("section", "rep"), None),
        P("ctx", ("section", "rep"), None),
        P("ctx", None, ("section", "rep")),
    )
    return jax.shard_map(
        direct if pairs and short else general,
        mesh=mesh,
        in_specs=placed,
        out_specs=P(("group", "ctx"), ("section", "rep")),
        check_vma=False,
    )
```

```python
import functools
import math

import jax
import jax.numpy as jnp
from jax import lax
from jax.experimental import pallas as pl
from jax.experimental.pallas import tpu as pltpu
from jax.sharding import PartitionSpec as P

HEAD_SIZE = 128
LANES = 128
EPSILON = 1e-06
HIDDEN_MASK = -1e30
VMEM_LIMIT = 16 * 1024 * 1024

F32 = jnp.float32
BF16 = jnp.bfloat16
NT = (((1,), (1,)), ((), ()))


def dot(a, b):
    return jnp.dot(a, b, preferred_element_type=F32)


def dot_nt(a, b):
    return lax.dot_general(a, b, NT, preferred_element_type=F32)


def vmem_call(body, out_shape, scalars, arrays, after=(), scratch=(), remote=(), held=True):
    multi = isinstance(out_shape, (tuple, list))
    n_out = len(out_shape) if multi else 1
    n_given = len(scalars) + len(remote) + len(arrays)
    whole = pl.BlockSpec(memory_space=pltpu.VMEM)
    anywhere = pl.BlockSpec(memory_space=pl.ANY)

    def placed(x):
        return pltpu.VMEM(x.shape, x.dtype) if held else x

    def kernel(*refs):
        body(*refs[:n_given], *refs[n_given + len(after) :])

    kernel.__name__ = getattr(body, "func", body).__name__
    return pl.pallas_call(
        kernel,
        out_shape=[placed(x) for x in out_shape] if multi else placed(out_shape),
        in_specs=[pl.BlockSpec(memory_space=pltpu.SMEM)] * len(scalars)
        + [pl.BlockSpec(memory_space=pltpu.HBM)] * len(remote)
        + [whole] * len(arrays)
        + [anywhere] * len(after),
        out_specs=[whole] * n_out if multi else whole,
        scratch_shapes=list(scratch),
        compiler_params=pltpu.CompilerParams(vmem_limit_bytes=VMEM_LIMIT),
        cost_estimate=pl.CostEstimate(flops=1, bytes_accessed=1, transcendentals=0),
    )(
        *scalars,
        *[pltpu.with_memory_space_constraint(x, pltpu.HBM) for x in remote],
        *[pltpu.with_memory_space_constraint(x, pltpu.VMEM) for x in arrays],
        *after,
    )


def carry(copies):
    for copy in copies:
        copy.start()
    for copy in copies:
        copy.wait()


def prepare_kernel(head_ref, rep_ref, key_in, value_in, kv_ref, part_ref, sems):
    columns = pl.ds(pl.multiple_of(head_ref[0] * HEAD_SIZE, HEAD_SIZE), HEAD_SIZE)
    carry(
        [
            pltpu.make_async_copy(
                ref.at[:, columns], kv_ref.at[:, pl.ds(i * HEAD_SIZE, HEAD_SIZE)], sems.at[i]
            )
            for i, ref in enumerate((key_in, value_in))
        ]
    )
    for i in range(2):

        @pl.when(rep_ref[0] == i)
        def _():
            part_ref[...] = kv_ref[:, i * HEAD_SIZE : (i + 1) * HEAD_SIZE]


def fetch_kernel(experts, *refs):
    count = (len(refs) - 4) // 2
    sources, home_in, targets, (target_ref, home_ref, sems) = (
        refs[:count],
        refs[count],
        refs[count + 1 : 2 * count + 1],
        refs[2 * count + 1 :],
    )
    pairs = [(home_in, home_ref), *zip(sources, targets)]
    carry([pltpu.make_async_copy(a, b, sems.at[i]) for i, (a, b) in enumerate(pairs)])
    ids = targets[-1][...]
    target = jnp.zeros(ids.shape, jnp.int32)
    for expert in range(experts):
        target = jnp.where(ids == expert, home_ref[0:1, expert : expert + 1], target)
    target_ref[...] = target


def attend_kernel(n, first, place_ref, rep_ref, gate_in, up_in, q_ref, stream_ref, gain_ref, target_ref, kv_ref, *rest):
    (near_mine, near_theirs, far_mine, far_theirs), rest = rest[:4], rest[4:]
    hidden_ref, gained, squares_ref, first_ref, *weight_refs, k_all, v_all, sems = rest
    pairs = zip((gate_in, up_in), weight_refs)
    copies = [pltpu.make_async_copy(a, b, sems.at[i]) for i, (a, b) in enumerate(pairs)]
    for copy in copies:
        copy.start()
    place = place_ref[0]
    tokens = q_ref.shape[0]
    heads = q_ref.shape[1] // HEAD_SIZE
    row = lax.broadcasted_iota(jnp.int32, (tokens, tokens), 0)
    col = lax.broadcasted_iota(jnp.int32, (tokens, tokens), 1)
    pieces = [jnp.where(row >= col, 0.0, HIDDEN_MASK)]
    rep = rep_ref[0]
    for block, (ref, offset) in enumerate(
        ((kv_ref, 0), (None, 1), (far_mine, 2 + rep), (far_theirs, 3 - rep))
    ):
        rows = slice(block * tokens, (block + 1) * tokens)
        if ref is not None:
            k_all[rows, :] = ref[:, :HEAD_SIZE]
            v_all[rows, :] = ref[:, HEAD_SIZE:]
        if block:
            seen = jnp.where(jnp.bitwise_xor(place, offset) < place, 0.0, HIDDEN_MASK)
            pieces.append(jnp.full((tokens, tokens), seen, F32))

    @pl.when(rep == 0)
    def _():
        k_all[tokens : 2 * tokens, :] = near_mine[...]
        v_all[tokens : 2 * tokens, :] = near_theirs[...]

    @pl.when(rep == 1)
    def _():
        k_all[tokens : 2 * tokens, :] = near_theirs[...]
        v_all[tokens : 2 * tokens, :] = near_mine[...]

    bias = jnp.concatenate(pieces, axis=1)
    stacked = jnp.concatenate(
        [q_ref[:, h * HEAD_SIZE : (h + 1) * HEAD_SIZE] for h in range(heads)], axis=0
    )
    scored = dot_nt(stacked, k_all[...])
    squares = jnp.zeros((tokens, 1), F32)
    for head in range(heads):
        cols = slice(head * HEAD_SIZE, (head + 1) * HEAD_SIZE)
        scores = scored[head * tokens : (head + 1) * tokens, :] * (1.0 / math.sqrt(HEAD_SIZE)) + bias
        expo = jnp.exp(scores - jnp.max(scores, axis=-1, keepdims=True))
        total = jnp.sum(expo, axis=-1, keepdims=True)
        attended = dot(expo.astype(BF16), v_all[...]) / total
        hidden = stream_ref[:, cols].astype(F32) + attended
        hidden_ref[:, cols] = hidden
        squares = squares + jnp.sum(hidden * hidden, axis=-1, keepdims=True)
        gained[:, cols] = (hidden * gain_ref[head : head + 1, :].astype(F32)).astype(BF16)
    squares_ref[...] = jnp.broadcast_to(squares, squares_ref.shape)
    place_rows(place, target_ref, gained[...], [first], [first_ref])
    for copy in copies:
        copy.wait()


def place_rows(place, target_ref, values, blocks, row_refs):
    tokens = values.shape[0]
    earlier = (
        lax.broadcasted_iota(jnp.int32, (tokens, tokens), 0)
        < lax.broadcasted_iota(jnp.int32, (tokens, tokens), 1)
    ).astype(F32).astype(BF16)
    slot = lax.broadcasted_iota(jnp.int32, (row_refs[0].shape[0], tokens), 0)
    for j, row_ref in zip(blocks, row_refs):
        member = jnp.sum((target_ref[...] == jnp.bitwise_xor(place, j)).astype(F32), axis=0, keepdims=True)
        rank = dot(jnp.broadcast_to(member, (8, tokens)).astype(BF16), earlier)[0:1, :]
        rank = jnp.where(member > 0.5, rank, -1.0).astype(jnp.int32)
        placing = (slot == rank).astype(F32).astype(BF16)
        row_ref[...] = dot(placing, values).astype(BF16)


def rows_kernel(blocks, place_ref, down_in, gained_ref, squares_ref, router_ref, target_ref, *refs):
    row_refs, (stats_ref, down_ref, sem) = refs[: len(blocks)], refs[len(blocks) :]
    copy = pltpu.make_async_copy(down_in, down_ref, sem)
    copy.start()
    values = gained_ref[...]
    place_rows(place_ref[0], target_ref, values, blocks, row_refs)
    squares_row = jnp.transpose(squares_ref[...])
    height = stats_ref.shape[0]
    stats_ref[...] = jnp.concatenate(
        [dot_nt(router_ref[...], values), squares_row[: height - router_ref.shape[0], :]], axis=0
    )
    copy.wait()


def split_pair(x):
    high = x.astype(BF16).astype(F32)
    lane = lax.broadcasted_iota(jnp.int32, x.shape, 1)
    return jnp.where(lane < LANES // 2, high, x - high).astype(BF16)


def join_pair(ref, rows, start):
    return jnp.sum(ref[rows, start:].astype(F32), axis=-1, keepdims=True) * (2.0 / LANES)


def put_stats(ref, base, stats):
    height, tokens = stats.shape
    ref[base:, :] = jnp.zeros((ref.shape[0] - base, ref.shape[1]), BF16)
    terms = []
    for i in range(3):
        term = stats.astype(BF16)
        stats = stats - term.astype(F32)
        terms.append(term.astype(F32))
    pad = jnp.zeros((ref.shape[0] - base - height, 3 * tokens), F32)
    ref[base:, : 3 * tokens] = jnp.concatenate(
        [jnp.concatenate(terms, axis=1), pad], axis=0
    ).astype(BF16)


def get_stats(ref, base, like):
    height, tokens = like.shape
    parts = ref[base:, : 3 * tokens].astype(F32)[:height]
    return parts[:, :tokens] + parts[:, tokens : 2 * tokens] + parts[:, 2 * tokens :]


def up_kernel(with_stats, rep_ref, gate_ref, up_ref, gain_ref, *rest):
    rows_ref, keep_ref, first_ref, second_ref = rest[-4:]
    count = rows_ref.shape[0]
    half = gate_ref.shape[1] // 2
    mine = pl.multiple_of(rep_ref[0] * half, LANES)
    other = pl.multiple_of((1 - rep_ref[0]) * half, LANES)
    rows = rows_ref[...]
    squares = jnp.zeros((count, LANES), F32)
    for i in range(gain_ref.shape[0]):
        plain = rows[:, i * LANES : (i + 1) * LANES].astype(F32) / gain_ref[i : i + 1, :].astype(F32)
        squares = squares + plain * plain
    squares = jnp.broadcast_to(jnp.sum(squares, axis=-1, keepdims=True), (count, LANES))
    first_ref[...] = dot(rows, gate_ref[:, pl.ds(other, half)]).astype(BF16)
    second_ref[:count, :half] = dot(rows, up_ref[:, pl.ds(other, half)]).astype(BF16)
    second_ref[:count, half:] = split_pair(squares)
    keep_ref[:, :half] = dot(rows, gate_ref[:, pl.ds(mine, half)])
    keep_ref[:, half : 2 * half] = dot(rows, up_ref[:, pl.ds(mine, half)])
    keep_ref[:, 2 * half :] = squares
    if with_stats:
        put_stats(second_ref, count, rest[0][...])


def add_kernel(with_stats, *refs):
    keep_ref, first_ref, second_ref, sum_ref, send_ref = refs[with_stats : with_stats + 5]
    count = keep_ref.shape[0]
    wide = keep_ref.shape[1] - LANES
    half = first_ref.shape[1]
    for start, ref in ((0, first_ref), (half, second_ref)):
        both = keep_ref[:, start : start + half] + ref[:count, :half].astype(F32)
        sum_ref[:, start : start + half] = both
        send_ref[:count, start : start + half] = both.astype(BF16)
    squares = keep_ref[:, wide:] + join_pair(second_ref, slice(0, count), half)
    sum_ref[:, wide:] = squares
    send_ref[:count, wide:] = split_pair(squares)
    if with_stats:
        stats_ref, total_ref = refs[0], refs[-1]
        stats = stats_ref[...] + get_stats(second_ref, count, stats_ref)
        total_ref[...] = stats
        put_stats(send_ref, count, stats)


def inner_kernel(features, with_stats, *refs):
    sum_ref, got_ref, inner_ref = refs[with_stats : with_stats + 3]
    count = sum_ref.shape[0]
    wide = sum_ref.shape[1] - LANES
    half = wide // 2
    squares = sum_ref[:, wide : wide + 1] + join_pair(got_ref, slice(0, count), wide)
    scale = lax.rsqrt(squares * (1.0 / features) + EPSILON)
    gate = (sum_ref[:, :half] + got_ref[:count, :half].astype(F32)) * scale
    up = (sum_ref[:, half:wide] + got_ref[:count, half:wide].astype(F32)) * scale
    inner_ref[...] = (gate * jax.nn.sigmoid(gate) * up).astype(BF16)
    if with_stats:
        stats_ref, total_ref = refs[0], refs[-1]
        total_ref[...] = stats_ref[...] + get_stats(got_ref, count, stats_ref)


def down_kernel(rep_ref, down_ref, mine_ref, other_ref, out_ref):
    half = mine_ref.shape[1]
    mine = pl.multiple_of(rep_ref[0] * half, LANES)
    other = pl.multiple_of((1 - rep_ref[0]) * half, LANES)
    out_ref[...] = (
        dot(mine_ref[...], down_ref[pl.ds(mine, half), :])
        + dot(other_ref[...], down_ref[pl.ds(other, half), :])
    ).astype(BF16)


def gates_kernel(cap, features, place_ref, stats_ref, ids_ref, target_ref, *weight_refs):
    place = place_ref[0]
    top, tokens = ids_ref.shape
    stats = jnp.transpose(stats_ref[...])
    height = stats.shape[1]
    scale = lax.rsqrt(stats[:, height - 1 :] * (1.0 / features) + EPSILON)
    logits = stats * scale
    both = jnp.concatenate(
        [ids_ref[...], target_ref[...], jnp.zeros((8 - 2 * top, tokens), jnp.int32)], axis=0
    )
    both = jnp.transpose(both.astype(F32)).astype(jnp.int32)
    kinds = lax.broadcasted_iota(jnp.int32, stats.shape, 1)
    squashed = [
        jax.nn.sigmoid(
            jnp.sum(jnp.where(kinds == both[:, k : k + 1], logits, 0.0), axis=-1, keepdims=True)
        )
        for k in range(top)
    ]
    whole = functools.reduce(lambda a, b: a + b, squashed)
    blocks = jnp.bitwise_xor(lax.broadcasted_iota(jnp.int32, (tokens, LANES), 1), place)
    named = [both[:, top + k : top + k + 1] == blocks for k in range(top)]
    member = functools.reduce(lambda a, b: a + b, [x.astype(F32) for x in named])
    later = (
        lax.broadcasted_iota(jnp.int32, (tokens, tokens), 0)
        > lax.broadcasted_iota(jnp.int32, (tokens, tokens), 1)
    ).astype(F32).astype(BF16)
    rank = dot(later, member.astype(BF16))
    slot = lax.broadcasted_iota(jnp.int32, (tokens, cap), 1)
    for j, weights_ref in enumerate(weight_refs):
        weights = jnp.zeros((tokens, cap), F32)
        for k in range(top):
            at = jnp.where(named[k][:, j : j + 1], rank[:, j : j + 1], -1.0).astype(jnp.int32)
            weights = weights + jnp.where(slot == at, squashed[k] / whole, 0.0)
        high = weights.astype(BF16)
        weights_ref[:tokens, :] = high
        weights_ref[tokens:, :] = (weights - high.astype(F32)).astype(BF16)


def mix_kernel(count, partial_ref, *rest):
    weights, answers, out_ref = rest[:count], rest[count : 2 * count], rest[-1]
    tokens = partial_ref.shape[0]
    total = partial_ref[...]
    for weights_ref, answer_ref in zip(weights, answers):
        mixed = dot(weights_ref[...], answer_ref[...])
        total = total + (mixed[:tokens] + mixed[tokens:])
    out_ref[...] = total.astype(out_ref.dtype)


def swap(x, axis):
    return lax.ppermute(x, axis, [(0, 1), (1, 0)])


def direct(
    stream,
    query_proj,
    key_proj,
    value_projected,
    expert_ids,
    expert_home,
    router,
    norm_gain,
    w_gate,
    w_up,
    w_down,
):
    tokens, width = stream.shape
    top = expert_ids.shape[1]
    n = lax.axis_size("ctx")
    features = width * lax.axis_size(("section", "rep"))
    experts = router.shape[1]
    hid = w_gate.shape[2]
    wide = hid + LANES
    cap = capacity_of(tokens, top, n)
    where = lax.axis_index("ctx").astype(jnp.int32).reshape(1)
    side = lax.axis_index("rep").astype(jnp.int32).reshape(1)
    heads = width // HEAD_SIZE
    group_width = features // key_proj.shape[1]
    kv_head = (lax.axis_index(("section", "rep")) * heads // group_width).astype(jnp.int32).reshape(1)

    def exchange(x, j):
        return lax.ppermute(x, "ctx", [(i, i ^ j) for i in range(n)])

    def like(x):
        return jax.ShapeDtypeStruct(x.shape, x.dtype)

    own_kv, part = vmem_call(
        prepare_kernel,
        [jax.ShapeDtypeStruct((tokens, w * HEAD_SIZE), BF16) for w in (2, 1)],
        [kv_head, side],
        [],
        remote=[key_proj, value_projected],
        scratch=[pltpu.SemaphoreType.DMA((2,))],
    )
    sources = [query_proj, stream, norm_gain.reshape(width // LANES, LANES), router.T, expert_ids.T]
    queries, stream, gain, router_rows, ids_rows, target = vmem_call(
        functools.partial(fetch_kernel, experts),
        [like(x) for x in sources] + [jax.ShapeDtypeStruct((top, tokens), jnp.int32)],
        [],
        [],
        remote=[*sources, expert_home.reshape(1, experts)],
        after=[part],
        scratch=[pltpu.VMEM((1, experts), jnp.int32), pltpu.SemaphoreType.DMA((6,))],
    )
    distance = sorted(range(1, n), key=lambda j: (j < n // 2, j))
    near_kv = exchange(part, 1)
    far_kv = lax.ppermute(
        own_kv, ("ctx", "rep"), [(2 * i + r, 2 * (i ^ (2 + r)) + r) for i in range(n) for r in range(2)]
    )
    stat_rows = -(-(experts + 1) // 8) * 8

    chain = [0] + [distance[0], *distance[:0:-1]]
    block = jax.ShapeDtypeStruct((cap, width), BF16)
    weights = [w_gate[0], w_up[0]]
    hidden, gained, squares, first_rows, gate, up = vmem_call(
        functools.partial(attend_kernel, n, chain[1]),
        [
            jax.ShapeDtypeStruct((tokens, width), F32),
            jax.ShapeDtypeStruct((tokens, width), BF16),
            jax.ShapeDtypeStruct((tokens, LANES), F32),
            block,
        ]
        + [like(x) for x in weights],
        [where, side],
        [queries, stream, gain, target, own_kv, near_kv, swap(near_kv, "rep")]
        + [far_kv, swap(far_kv, "rep")],
        remote=weights,
        scratch=[
            pltpu.VMEM((n * tokens, HEAD_SIZE), BF16),
            pltpu.VMEM((n * tokens, HEAD_SIZE), BF16),
            pltpu.SemaphoreType.DMA((2,)),
        ],
    )
    others = [j for j in range(n) if j != chain[1]]
    *rows, stats, down = vmem_call(
        functools.partial(rows_kernel, others),
        [block] * (n - 1) + [jax.ShapeDtypeStruct((stat_rows, tokens), F32), like(w_down[0])],
        [where],
        [gained, squares, router_rows, target],
        remote=[w_down[0]],
        scratch=[pltpu.SemaphoreType.DMA],
    )
    rows = {chain[1]: first_rows, **dict(zip(others, rows))}
    arrived = {j: exchange(rows[j], j) for j in distance}
    arrived[0] = rows[0]

    extra = -(-stat_rows // 16) * 16
    state = {}
    made = {"last": hidden, "stats": stats, "partial": hidden}

    def run(body, out_shape, scalars, arrays, held=True):
        outs = vmem_call(body, out_shape, scalars, arrays, after=[made["last"]], held=held)
        made["last"] = outs[0] if isinstance(outs, (tuple, list)) else outs
        return outs

    def stat_part(j):
        return (1, [made["stats"]], [like(stats)], extra) if j == 1 else (0, [], [], 0)

    def up_step(j):
        flag, given, made_too, more = stat_part(j)
        keep, first, second = run(
            functools.partial(up_kernel, flag),
            [
                jax.ShapeDtypeStruct((cap, wide), F32),
                jax.ShapeDtypeStruct((cap, hid // 2), BF16),
                jax.ShapeDtypeStruct((cap + more, hid // 2 + LANES), BF16),
            ],
            [side],
            [gate, up, gain] + given + [arrived[j]],
        )
        state[j] = (keep, swap(first, "rep"), swap(second, "rep"))

    def add_step(j):
        flag, given, made_too, more = stat_part(j)
        both, send, *rest = run(
            functools.partial(add_kernel, flag),
            [jax.ShapeDtypeStruct((cap, wide), F32), jax.ShapeDtypeStruct((cap + more, wide), BF16)]
            + made_too,
            [],
            given + list(state[j]),
        )
        if rest:
            made["stats"] = rest[0]
        state[j] = (both, swap(send, "section"))

    def inner_step(j):
        flag, given, made_too, more = stat_part(j)
        inner, *rest = run(
            functools.partial(inner_kernel, features, flag),
            [jax.ShapeDtypeStruct((cap, hid // 2), BF16)] + made_too,
            [],
            given + list(state[j]),
        )
        if rest:
            made["stats"] = rest[0]
        state[j] = (inner, swap(inner, "rep"))

    def down_step(j):
        answer = run(down_kernel, jax.ShapeDtypeStruct((cap, width), BF16), [side], [down, *state[j]])
        state[j] = exchange(answer, j) if j else answer

    def gates_step():
        made["weights"] = run(
            functools.partial(gates_kernel, cap, features),
            [jax.ShapeDtypeStruct((2 * tokens, cap), BF16)] * n,
            [where],
            [made["stats"], ids_rows, target],
        )

    def mix_step(blocks, dtype=F32, held=True):
        made["partial"] = run(
            functools.partial(mix_kernel, len(blocks)),
            jax.ShapeDtypeStruct((tokens, width), dtype),
            [],
            [made["partial"]] + [made["weights"][j] for j in blocks] + [state[j] for j in blocks],
            held=held,
        )

    steps = dict(u=up_step, a=add_step, i=inner_step, d=down_step, m=lambda j: mix_step([j]))
    plan = (
        *("u0", "a0", "u1", "i0", "a1", "u2", "a2", "u3", "i1", "d1"),
        *("d0", "a3", "i2", "g", "d2", "m0", "i3", "m1", "d3", "m2"),
    )
    for name in plan:
        if name == "g":
            gates_step()
        elif int(name[1]) < n - (name[0] == "m"):
            steps[name[0]](chain[int(name[1])])
    early = [chain[int(name[1])] for name in plan if name[0] == "m" and int(name[1]) < n - 1]
    mix_step([j for j in chain if j not in early], BF16, held=False)
    return made["partial"]


def capacity_of(tokens, top, n):
    return min(tokens, max(2, 5 * tokens * top // (4 * n)))


def score_update(running, query_matrix, query_pos, key_block, value_block, key_anchor):
    run_max, run_sum, run_acc = running
    key_len = key_block.shape[0]
    scores = jnp.einsum(
        "tha,pa->htp", query_matrix, key_block, preferred_element_type=jnp.float32
    ) * (1.0 / math.sqrt(HEAD_SIZE))
    key_pos = key_anchor + jnp.arange(key_len, dtype=jnp.int32)
    visible = query_pos[:, None] >= key_pos[None, :]
    scores = jnp.where(visible, scores, HIDDEN_MASK)
    new_max = jnp.maximum(run_max, jnp.max(scores, axis=-1))
    expo = jnp.where(visible, jnp.exp(scores - new_max[..., None]), 0.0)
    factor = jnp.exp(run_max - new_max)
    new_sum = run_sum * factor + jnp.sum(expo, axis=-1)
    weights = expo.astype(jnp.bfloat16)
    new_acc = run_acc * factor[..., None] + jnp.einsum(
        "htp,pa->hta", weights, value_block, preferred_element_type=jnp.float32
    )
    return (new_max, new_sum, new_acc)


def absorb_rows(running, query_matrix, query_pos, key_rows, value_rows, anchor):
    piece_len = key_rows.shape[0]
    if piece_len > 512 and piece_len % 512 == 0:
        blocks = piece_len // 512
        key_tiles = key_rows.reshape(blocks, 512, key_rows.shape[1])
        value_tiles = value_rows.reshape(blocks, 512, value_rows.shape[1])
        anchors = anchor + 512 * jnp.arange(blocks, dtype=jnp.int32)

        def advance(state_now, tile):
            return (
                score_update(state_now, query_matrix, query_pos, tile[0], tile[1], tile[2]),
                None,
            )

        running, ignored = lax.scan(advance, running, (key_tiles, value_tiles, anchors))
        return running
    return score_update(running, query_matrix, query_pos, key_rows, value_rows, anchor)


def general(
    stream,
    query_proj,
    key_proj,
    value_projected,
    expert_ids,
    expert_home,
    router,
    norm_gain,
    w_gate,
    w_up,
    w_down,
):
    tok_rows, local_width = stream.shape
    top_count = expert_ids.shape[1]
    columns = lax.axis_size("ctx")
    features = local_width * lax.axis_size(("section", "rep"))
    capacity = capacity_of(tok_rows, top_count, columns)
    place = lax.axis_index("ctx")
    feature_index = lax.axis_index(("section", "rep"))
    heads_dev = local_width // HEAD_SIZE
    group_width = features // key_proj.shape[1]
    kv_head = feature_index * heads_dev // group_width
    query_matrix = query_proj.reshape(tok_rows, heads_dev, HEAD_SIZE)
    query_pos = place * tok_rows + jnp.arange(tok_rows, dtype=jnp.int32)
    initial = (
        jnp.full((heads_dev, tok_rows), HIDDEN_MASK, jnp.float32),
        jnp.zeros((heads_dev, tok_rows), jnp.float32),
        jnp.zeros((heads_dev, tok_rows, HEAD_SIZE), jnp.float32),
    )
    key_single = lax.dynamic_slice_in_dim(key_proj, kv_head * HEAD_SIZE, HEAD_SIZE, 1)
    value_single = lax.dynamic_slice_in_dim(value_projected, kv_head * HEAD_SIZE, HEAD_SIZE, 1)
    run_max, run_sum, run_acc = absorb_rows(
        initial,
        query_matrix,
        query_pos,
        lax.all_gather(key_single, "ctx", axis=0, tiled=True),
        lax.all_gather(value_single, "ctx", axis=0, tiled=True),
        jnp.int32(0),
    )
    attended = jnp.transpose(run_acc / run_sum[..., None], (1, 0, 2)).reshape(tok_rows, local_width)
    hidden = stream.astype(jnp.float32) + attended
    total_sq = lax.psum(jnp.sum(hidden * hidden, axis=-1), ("section", "rep"))
    scale_rows = lax.rsqrt(total_sq / features + EPSILON)
    normed = (hidden * scale_rows[:, None] * norm_gain.astype(jnp.float32)[None, :]).astype(
        jnp.bfloat16
    )
    logits = lax.psum(dot(normed, router), ("section", "rep"))
    experts_all = logits.shape[1]
    one_hot = expert_ids[:, :, None] == jnp.arange(experts_all, dtype=jnp.int32)[None, None, :]
    picked = jnp.sum(jnp.where(one_hot, logits[:, None, :], 0.0), axis=-1)
    squashed = jax.nn.sigmoid(picked)
    gates = squashed / jnp.sum(squashed, axis=-1, keepdims=True)
    target = jnp.sum(jnp.where(one_hot, expert_home[None, None, :], 0), axis=-1)
    named = target[:, :, None] == jnp.arange(columns, dtype=jnp.int32)[None, None, :]
    member = jnp.any(named, axis=1).astype(jnp.bfloat16)
    before = jnp.tril(jnp.ones((tok_rows, tok_rows), jnp.bfloat16), -1)
    rank = dot(before, member).astype(jnp.int32)
    rank = jnp.sum(jnp.where(named, rank[:, None, :], 0), axis=-1)
    slot_index = (target * capacity + rank).reshape(-1)
    placing = slot_index[None, :] == jnp.arange(columns * capacity, dtype=jnp.int32)[:, None]
    placing = jnp.any(placing.reshape(columns * capacity, tok_rows, top_count), axis=-1).astype(
        jnp.bfloat16
    )
    outgoing = dot(placing, normed).astype(jnp.bfloat16)
    outgoing = outgoing.reshape(columns, capacity, local_width)
    received = lax.all_to_all(outgoing, "ctx", split_axis=0, concat_axis=0, tiled=True)
    flat_rows = received.reshape(-1, local_width)
    gate_part = dot(flat_rows, w_gate[0])
    up_part = dot(flat_rows, w_up[0])
    gate_full = lax.psum(gate_part.astype(jnp.bfloat16), ("section", "rep")).astype(jnp.float32)
    up_full = lax.psum(up_part.astype(jnp.bfloat16), ("section", "rep")).astype(jnp.float32)
    inner = (jax.nn.silu(gate_full) * up_full).astype(jnp.bfloat16)
    answer = dot(inner, w_down[0]).astype(jnp.bfloat16)
    returned = lax.all_to_all(
        answer.reshape(received.shape), "ctx", split_axis=0, concat_axis=0, tiled=True
    )
    flat_back = returned.reshape(columns * capacity, local_width)
    picked_rows = flat_back[slot_index].reshape(tok_rows, top_count, local_width)
    mixed = jnp.sum(gates[:, :, None] * picked_rows.astype(jnp.float32), axis=1)
    return (hidden + mixed).astype(jnp.bfloat16)


def solution(mesh):
    size = dict(mesh.shape)
    pairs = size["section"] == 2 and size["rep"] == 2
    short = size["ctx"] == 4
    placed = (
        P(("group", "ctx"), ("section", "rep")),
        P(("group", "ctx"), ("section", "rep")),
        P(("group", "ctx"), None),
        P(("group", "ctx"), None),
        P(("group", "ctx"), None),
        P(),
        P(("section", "rep"), None),
        P(("section", "rep")),
        P("ctx", ("section", "rep"), None),
        P("ctx", ("section", "rep"), None),
        P("ctx", None, ("section", "rep")),
    )
    return jax.shard_map(
        direct if pairs and short else general,
        mesh=mesh,
        in_specs=placed,
        out_specs=P(("group", "ctx"), ("section", "rep")),
        check_vma=False,
    )
```

```python
import functools
import math

import jax
import jax.numpy as jnp
from jax import lax
from jax.experimental import pallas as pl
from jax.experimental.pallas import tpu as pltpu
from jax.sharding import PartitionSpec as P

HEAD_SIZE = 128
LANES = 128
EPSILON = 1e-06
HIDDEN_MASK = -1e30
VMEM_LIMIT = 16 * 1024 * 1024

F32 = jnp.float32
BF16 = jnp.bfloat16
NT = (((1,), (1,)), ((), ()))


def dot(a, b):
    return jnp.dot(a, b, preferred_element_type=F32)


def dot_nt(a, b):
    return lax.dot_general(a, b, NT, preferred_element_type=F32)


def vmem_call(body, out_shape, scalars, arrays, after=(), scratch=(), remote=(), held=True):
    multi = isinstance(out_shape, (tuple, list))
    n_out = len(out_shape) if multi else 1
    n_given = len(scalars) + len(remote) + len(arrays)
    whole = pl.BlockSpec(memory_space=pltpu.VMEM)
    anywhere = pl.BlockSpec(memory_space=pl.ANY)

    def placed(x):
        return pltpu.VMEM(x.shape, x.dtype) if held else x

    def kernel(*refs):
        body(*refs[:n_given], *refs[n_given + len(after) :])

    kernel.__name__ = getattr(body, "func", body).__name__
    return pl.pallas_call(
        kernel,
        out_shape=[placed(x) for x in out_shape] if multi else placed(out_shape),
        in_specs=[pl.BlockSpec(memory_space=pltpu.SMEM)] * len(scalars)
        + [pl.BlockSpec(memory_space=pltpu.HBM)] * len(remote)
        + [whole] * len(arrays)
        + [anywhere] * len(after),
        out_specs=[whole] * n_out if multi else whole,
        scratch_shapes=list(scratch),
        compiler_params=pltpu.CompilerParams(vmem_limit_bytes=VMEM_LIMIT),
        cost_estimate=pl.CostEstimate(flops=1, bytes_accessed=1, transcendentals=0),
    )(
        *scalars,
        *[pltpu.with_memory_space_constraint(x, pltpu.HBM) for x in remote],
        *[pltpu.with_memory_space_constraint(x, pltpu.VMEM) for x in arrays],
        *after,
    )


def carry(copies):
    for copy in copies:
        copy.start()
    for copy in copies:
        copy.wait()


def prepare_kernel(head_ref, rep_ref, key_in, value_in, kv_ref, part_ref, sems):
    columns = pl.ds(pl.multiple_of(head_ref[0] * HEAD_SIZE, HEAD_SIZE), HEAD_SIZE)
    carry(
        [
            pltpu.make_async_copy(
                ref.at[:, columns], kv_ref.at[:, pl.ds(i * HEAD_SIZE, HEAD_SIZE)], sems.at[i]
            )
            for i, ref in enumerate((key_in, value_in))
        ]
    )
    for i in range(2):

        @pl.when(rep_ref[0] == i)
        def _():
            part_ref[...] = kv_ref[:, i * HEAD_SIZE : (i + 1) * HEAD_SIZE]


def fetch_kernel(experts, *refs):
    count = (len(refs) - 4) // 2
    sources, home_in, targets, (target_ref, home_ref, sems) = (
        refs[:count],
        refs[count],
        refs[count + 1 : 2 * count + 1],
        refs[2 * count + 1 :],
    )
    pairs = [(home_in, home_ref), *zip(sources, targets)]
    carry([pltpu.make_async_copy(a, b, sems.at[i]) for i, (a, b) in enumerate(pairs)])
    ids = targets[-1][...]
    target = jnp.zeros(ids.shape, jnp.int32)
    for expert in range(experts):
        target = jnp.where(ids == expert, home_ref[0:1, expert : expert + 1], target)
    target_ref[...] = target


def attend_kernel(n, first, place_ref, rep_ref, gate_in, up_in, q_ref, stream_ref, gain_ref, target_ref, kv_ref, *rest):
    (near_mine, near_theirs, far_mine, far_theirs), rest = rest[:4], rest[4:]
    hidden_ref, gained, squares_ref, first_ref, *weight_refs, k_all, v_all, sems = rest
    pairs = zip((gate_in, up_in), weight_refs)
    copies = [pltpu.make_async_copy(a, b, sems.at[i]) for i, (a, b) in enumerate(pairs)]
    for copy in copies:
        copy.start()
    place = place_ref[0]
    tokens = q_ref.shape[0]
    heads = q_ref.shape[1] // HEAD_SIZE
    row = lax.broadcasted_iota(jnp.int32, (tokens, tokens), 0)
    col = lax.broadcasted_iota(jnp.int32, (tokens, tokens), 1)
    pieces = [jnp.where(row >= col, 0.0, HIDDEN_MASK)]
    rep = rep_ref[0]
    for block, (ref, offset) in enumerate(
        ((kv_ref, 0), (None, 1), (far_mine, 2 + rep), (far_theirs, 3 - rep))
    ):
        rows = slice(block * tokens, (block + 1) * tokens)
        if ref is not None:
            k_all[rows, :] = ref[:, :HEAD_SIZE]
            v_all[rows, :] = ref[:, HEAD_SIZE:]
        if block:
            seen = jnp.where(jnp.bitwise_xor(place, offset) < place, 0.0, HIDDEN_MASK)
            pieces.append(jnp.full((tokens, tokens), seen, F32))

    @pl.when(rep == 0)
    def _():
        k_all[tokens : 2 * tokens, :] = near_mine[...]
        v_all[tokens : 2 * tokens, :] = near_theirs[...]

    @pl.when(rep == 1)
    def _():
        k_all[tokens : 2 * tokens, :] = near_theirs[...]
        v_all[tokens : 2 * tokens, :] = near_mine[...]

    bias = jnp.concatenate(pieces, axis=1)
    stacked = jnp.concatenate(
        [q_ref[:, h * HEAD_SIZE : (h + 1) * HEAD_SIZE] for h in range(heads)], axis=0
    )
    scored = dot_nt(stacked, k_all[...])
    squares = jnp.zeros((tokens, 1), F32)
    for head in range(heads):
        cols = slice(head * HEAD_SIZE, (head + 1) * HEAD_SIZE)
        scores = scored[head * tokens : (head + 1) * tokens, :] * (1.0 / math.sqrt(HEAD_SIZE)) + bias
        expo = jnp.exp(scores - jnp.max(scores, axis=-1, keepdims=True))
        total = jnp.sum(expo, axis=-1, keepdims=True)
        attended = dot(expo.astype(BF16), v_all[...]) / total
        hidden = stream_ref[:, cols].astype(F32) + attended
        hidden_ref[:, cols] = hidden
        squares = squares + jnp.sum(hidden * hidden, axis=-1, keepdims=True)
        gained[:, cols] = (hidden * gain_ref[head : head + 1, :].astype(F32)).astype(BF16)
    squares_ref[...] = jnp.broadcast_to(squares, squares_ref.shape)
    place_rows(place, target_ref, gained[...], [first], [first_ref])
    for copy in copies:
        copy.wait()


def place_rows(place, target_ref, values, blocks, row_refs):
    tokens = values.shape[0]
    earlier = (
        lax.broadcasted_iota(jnp.int32, (tokens, tokens), 0)
        < lax.broadcasted_iota(jnp.int32, (tokens, tokens), 1)
    ).astype(F32).astype(BF16)
    slot = lax.broadcasted_iota(jnp.int32, (row_refs[0].shape[0], tokens), 0)
    for j, row_ref in zip(blocks, row_refs):
        member = jnp.sum((target_ref[...] == jnp.bitwise_xor(place, j)).astype(F32), axis=0, keepdims=True)
        rank = dot(jnp.broadcast_to(member, (8, tokens)).astype(BF16), earlier)[0:1, :]
        rank = jnp.where(member > 0.5, rank, -1.0).astype(jnp.int32)
        placing = (slot == rank).astype(F32).astype(BF16)
        row_ref[...] = dot(placing, values).astype(BF16)


def rows_kernel(blocks, place_ref, down_in, gained_ref, squares_ref, router_ref, target_ref, *refs):
    row_refs, (stats_ref, down_ref, sem) = refs[: len(blocks)], refs[len(blocks) :]
    copy = pltpu.make_async_copy(down_in, down_ref, sem)
    copy.start()
    values = gained_ref[...]
    place_rows(place_ref[0], target_ref, values, blocks, row_refs)
    squares_row = jnp.transpose(squares_ref[...])
    height = stats_ref.shape[0]
    stats_ref[...] = jnp.concatenate(
        [dot_nt(router_ref[...], values), squares_row[: height - router_ref.shape[0], :]], axis=0
    )
    copy.wait()


def split_pair(x):
    high = x.astype(BF16).astype(F32)
    lane = lax.broadcasted_iota(jnp.int32, x.shape, 1)
    return jnp.where(lane < LANES // 2, high, x - high).astype(BF16)


def join_pair(ref, rows, start):
    return jnp.sum(ref[rows, start:].astype(F32), axis=-1, keepdims=True) * (2.0 / LANES)


def put_stats(ref, base, stats):
    height, tokens = stats.shape
    ref[base:, :] = jnp.zeros((ref.shape[0] - base, ref.shape[1]), BF16)
    terms = []
    for i in range(3):
        term = stats.astype(BF16)
        stats = stats - term.astype(F32)
        terms.append(term.astype(F32))
    pad = jnp.zeros((ref.shape[0] - base - height, 3 * tokens), F32)
    ref[base:, : 3 * tokens] = jnp.concatenate(
        [jnp.concatenate(terms, axis=1), pad], axis=0
    ).astype(BF16)


def get_stats(ref, base, like):
    height, tokens = like.shape
    parts = ref[base:, : 3 * tokens].astype(F32)[:height]
    return parts[:, :tokens] + parts[:, tokens : 2 * tokens] + parts[:, 2 * tokens :]


def up_kernel(with_stats, rep_ref, gate_ref, up_ref, gain_ref, *rest):
    rows_ref, keep_ref, first_ref, second_ref = rest[-4:]
    count = rows_ref.shape[0]
    half = gate_ref.shape[1] // 2
    mine = pl.multiple_of(rep_ref[0] * half, LANES)
    other = pl.multiple_of((1 - rep_ref[0]) * half, LANES)
    rows = rows_ref[...]
    squares = jnp.zeros((count, LANES), F32)
    for i in range(gain_ref.shape[0]):
        plain = rows[:, i * LANES : (i + 1) * LANES].astype(F32) / gain_ref[i : i + 1, :].astype(F32)
        squares = squares + plain * plain
    squares = jnp.broadcast_to(jnp.sum(squares, axis=-1, keepdims=True), (count, LANES))
    first_ref[...] = dot(rows, gate_ref[:, pl.ds(other, half)]).astype(BF16)
    second_ref[:count, :half] = dot(rows, up_ref[:, pl.ds(other, half)]).astype(BF16)
    second_ref[:count, half:] = split_pair(squares)
    keep_ref[:, :half] = dot(rows, gate_ref[:, pl.ds(mine, half)])
    keep_ref[:, half : 2 * half] = dot(rows, up_ref[:, pl.ds(mine, half)])
    keep_ref[:, 2 * half :] = squares
    if with_stats:
        put_stats(second_ref, count, rest[0][...])


def add_kernel(with_stats, *refs):
    keep_ref, first_ref, second_ref, sum_ref, send_ref = refs[with_stats : with_stats + 5]
    count = keep_ref.shape[0]
    wide = keep_ref.shape[1] - LANES
    half = first_ref.shape[1]
    for start, ref in ((0, first_ref), (half, second_ref)):
        both = keep_ref[:, start : start + half] + ref[:count, :half].astype(F32)
        sum_ref[:, start : start + half] = both
        send_ref[:count, start : start + half] = both.astype(BF16)
    squares = keep_ref[:, wide:] + join_pair(second_ref, slice(0, count), half)
    sum_ref[:, wide:] = squares
    send_ref[:count, wide:] = split_pair(squares)
    if with_stats:
        stats_ref, total_ref = refs[0], refs[-1]
        stats = stats_ref[...] + get_stats(second_ref, count, stats_ref)
        total_ref[...] = stats
        put_stats(send_ref, count, stats)


def inner_kernel(features, with_stats, *refs):
    sum_ref, got_ref, inner_ref = refs[with_stats : with_stats + 3]
    count = sum_ref.shape[0]
    wide = sum_ref.shape[1] - LANES
    half = wide // 2
    squares = sum_ref[:, wide : wide + 1] + join_pair(got_ref, slice(0, count), wide)
    scale = lax.rsqrt(squares * (1.0 / features) + EPSILON)
    gate = (sum_ref[:, :half] + got_ref[:count, :half].astype(F32)) * scale
    up = (sum_ref[:, half:wide] + got_ref[:count, half:wide].astype(F32)) * scale
    inner_ref[...] = (gate * jax.nn.sigmoid(gate) * up).astype(BF16)
    if with_stats:
        stats_ref, total_ref = refs[0], refs[-1]
        total_ref[...] = stats_ref[...] + get_stats(got_ref, count, stats_ref)


def down_kernel(rep_ref, down_ref, mine_ref, other_ref, out_ref, inner):
    half = mine_ref.shape[1]
    for i in range(2):

        @pl.when(rep_ref[0] == i)
        def _():
            inner[:, i * half : (i + 1) * half] = mine_ref[...]
            inner[:, (1 - i) * half : (2 - i) * half] = other_ref[...]

    out_ref[...] = dot(inner[...], down_ref[...]).astype(BF16)


def gates_kernel(cap, features, place_ref, stats_ref, ids_ref, target_ref, *weight_refs):
    place = place_ref[0]
    top, tokens = ids_ref.shape
    stats = jnp.transpose(stats_ref[...])
    height = stats.shape[1]
    scale = lax.rsqrt(stats[:, height - 1 :] * (1.0 / features) + EPSILON)
    logits = stats * scale
    both = jnp.concatenate(
        [ids_ref[...], target_ref[...], jnp.zeros((8 - 2 * top, tokens), jnp.int32)], axis=0
    )
    both = jnp.transpose(both.astype(F32)).astype(jnp.int32)
    kinds = lax.broadcasted_iota(jnp.int32, stats.shape, 1)
    squashed = [
        jax.nn.sigmoid(
            jnp.sum(jnp.where(kinds == both[:, k : k + 1], logits, 0.0), axis=-1, keepdims=True)
        )
        for k in range(top)
    ]
    whole = functools.reduce(lambda a, b: a + b, squashed)
    blocks = jnp.bitwise_xor(lax.broadcasted_iota(jnp.int32, (tokens, LANES), 1), place)
    named = [both[:, top + k : top + k + 1] == blocks for k in range(top)]
    member = functools.reduce(lambda a, b: a + b, [x.astype(F32) for x in named])
    later = (
        lax.broadcasted_iota(jnp.int32, (tokens, tokens), 0)
        > lax.broadcasted_iota(jnp.int32, (tokens, tokens), 1)
    ).astype(F32).astype(BF16)
    rank = dot(later, member.astype(BF16))
    slot = lax.broadcasted_iota(jnp.int32, (tokens, cap), 1)
    for j, weights_ref in enumerate(weight_refs):
        weights = jnp.zeros((tokens, cap), F32)
        for k in range(top):
            at = jnp.where(named[k][:, j : j + 1], rank[:, j : j + 1], -1.0).astype(jnp.int32)
            weights = weights + jnp.where(slot == at, squashed[k] / whole, 0.0)
        high = weights.astype(BF16)
        weights_ref[:tokens, :] = high
        weights_ref[tokens:, :] = (weights - high.astype(F32)).astype(BF16)


def mix_kernel(count, partial_ref, *rest):
    weights, answers, out_ref = rest[:count], rest[count : 2 * count], rest[-1]
    tokens = partial_ref.shape[0]
    total = partial_ref[...]
    for weights_ref, answer_ref in zip(weights, answers):
        mixed = dot(weights_ref[...], answer_ref[...])
        total = total + (mixed[:tokens] + mixed[tokens:])
    out_ref[...] = total.astype(out_ref.dtype)


def swap(x, axis):
    return lax.ppermute(x, axis, [(0, 1), (1, 0)])


def direct(
    stream,
    query_proj,
    key_proj,
    value_projected,
    expert_ids,
    expert_home,
    router,
    norm_gain,
    w_gate,
    w_up,
    w_down,
):
    tokens, width = stream.shape
    top = expert_ids.shape[1]
    n = lax.axis_size("ctx")
    features = width * lax.axis_size(("section", "rep"))
    experts = router.shape[1]
    hid = w_gate.shape[2]
    wide = hid + LANES
    cap = capacity_of(tokens, top, n)
    where = lax.axis_index("ctx").astype(jnp.int32).reshape(1)
    side = lax.axis_index("rep").astype(jnp.int32).reshape(1)
    heads = width // HEAD_SIZE
    group_width = features // key_proj.shape[1]
    kv_head = (lax.axis_index(("section", "rep")) * heads // group_width).astype(jnp.int32).reshape(1)

    def exchange(x, j):
        return lax.ppermute(x, "ctx", [(i, i ^ j) for i in range(n)])

    def like(x):
        return jax.ShapeDtypeStruct(x.shape, x.dtype)

    own_kv, part = vmem_call(
        prepare_kernel,
        [jax.ShapeDtypeStruct((tokens, w * HEAD_SIZE), BF16) for w in (2, 1)],
        [kv_head, side],
        [],
        remote=[key_proj, value_projected],
        scratch=[pltpu.SemaphoreType.DMA((2,))],
    )
    sources = [query_proj, stream, norm_gain.reshape(width // LANES, LANES), router.T, expert_ids.T]
    queries, stream, gain, router_rows, ids_rows, target = vmem_call(
        functools.partial(fetch_kernel, experts),
        [like(x) for x in sources] + [jax.ShapeDtypeStruct((top, tokens), jnp.int32)],
        [],
        [],
        remote=[*sources, expert_home.reshape(1, experts)],
        after=[part],
        scratch=[pltpu.VMEM((1, experts), jnp.int32), pltpu.SemaphoreType.DMA((6,))],
    )
    distance = sorted(range(1, n), key=lambda j: (j < n // 2, j))
    near_kv = exchange(part, 1)
    far_kv = lax.ppermute(
        own_kv, ("ctx", "rep"), [(2 * i + r, 2 * (i ^ (2 + r)) + r) for i in range(n) for r in range(2)]
    )
    stat_rows = -(-(experts + 1) // 8) * 8

    chain = [0] + [distance[0], *distance[:0:-1]]
    block = jax.ShapeDtypeStruct((cap, width), BF16)
    weights = [w_gate[0], w_up[0]]
    hidden, gained, squares, first_rows, gate, up = vmem_call(
        functools.partial(attend_kernel, n, chain[1]),
        [
            jax.ShapeDtypeStruct((tokens, width), F32),
            jax.ShapeDtypeStruct((tokens, width), BF16),
            jax.ShapeDtypeStruct((tokens, LANES), F32),
            block,
        ]
        + [like(x) for x in weights],
        [where, side],
        [queries, stream, gain, target, own_kv, near_kv, swap(near_kv, "rep")]
        + [far_kv, swap(far_kv, "rep")],
        remote=weights,
        scratch=[
            pltpu.VMEM((n * tokens, HEAD_SIZE), BF16),
            pltpu.VMEM((n * tokens, HEAD_SIZE), BF16),
            pltpu.SemaphoreType.DMA((2,)),
        ],
    )
    others = [j for j in range(n) if j != chain[1]]
    *rows, stats, down = vmem_call(
        functools.partial(rows_kernel, others),
        [block] * (n - 1) + [jax.ShapeDtypeStruct((stat_rows, tokens), F32), like(w_down[0])],
        [where],
        [gained, squares, router_rows, target],
        remote=[w_down[0]],
        scratch=[pltpu.SemaphoreType.DMA],
    )
    rows = {chain[1]: first_rows, **dict(zip(others, rows))}
    arrived = {j: exchange(rows[j], j) for j in distance}
    arrived[0] = rows[0]

    extra = -(-stat_rows // 16) * 16
    state = {}
    made = {"last": hidden, "stats": stats, "partial": hidden}

    def run(body, out_shape, scalars, arrays, scratch=(), held=True):
        outs = vmem_call(
            body, out_shape, scalars, arrays, after=[made["last"]], scratch=scratch, held=held
        )
        made["last"] = outs[0] if isinstance(outs, (tuple, list)) else outs
        return outs

    def stat_part(j):
        return (1, [made["stats"]], [like(stats)], extra) if j == 1 else (0, [], [], 0)

    def up_step(j):
        flag, given, made_too, more = stat_part(j)
        keep, first, second = run(
            functools.partial(up_kernel, flag),
            [
                jax.ShapeDtypeStruct((cap, wide), F32),
                jax.ShapeDtypeStruct((cap, hid // 2), BF16),
                jax.ShapeDtypeStruct((cap + more, hid // 2 + LANES), BF16),
            ],
            [side],
            [gate, up, gain] + given + [arrived[j]],
        )
        state[j] = (keep, swap(first, "rep"), swap(second, "rep"))

    def add_step(j):
        flag, given, made_too, more = stat_part(j)
        both, send, *rest = run(
            functools.partial(add_kernel, flag),
            [jax.ShapeDtypeStruct((cap, wide), F32), jax.ShapeDtypeStruct((cap + more, wide), BF16)]
            + made_too,
            [],
            given + list(state[j]),
        )
        if rest:
            made["stats"] = rest[0]
        state[j] = (both, swap(send, "section"))

    def inner_step(j):
        flag, given, made_too, more = stat_part(j)
        inner, *rest = run(
            functools.partial(inner_kernel, features, flag),
            [jax.ShapeDtypeStruct((cap, hid // 2), BF16)] + made_too,
            [],
            given + list(state[j]),
        )
        if rest:
            made["stats"] = rest[0]
        state[j] = (inner, swap(inner, "rep"))

    def down_step(j):
        answer = run(
            down_kernel,
            jax.ShapeDtypeStruct((cap, width), BF16),
            [side],
            [down, *state[j]],
            scratch=[pltpu.VMEM((cap, hid), BF16)],
        )
        state[j] = exchange(answer, j) if j else answer

    def gates_step():
        made["weights"] = run(
            functools.partial(gates_kernel, cap, features),
            [jax.ShapeDtypeStruct((2 * tokens, cap), BF16)] * n,
            [where],
            [made["stats"], ids_rows, target],
        )

    def mix_step(blocks, dtype=F32, held=True):
        made["partial"] = run(
            functools.partial(mix_kernel, len(blocks)),
            jax.ShapeDtypeStruct((tokens, width), dtype),
            [],
            [made["partial"]] + [made["weights"][j] for j in blocks] + [state[j] for j in blocks],
            held=held,
        )

    steps = dict(u=up_step, a=add_step, i=inner_step, d=down_step, m=lambda j: mix_step([j]))
    plan = (
        *("u0", "a0", "u1", "i0", "a1", "u2", "a2", "u3", "i1", "d0"),
        *("d1", "a3", "i2", "d2", "g", "m0", "i3", "m1", "d3", "m2"),
    )
    for name in plan:
        if name == "g":
            gates_step()
        elif int(name[1]) < n - (name[0] == "m"):
            steps[name[0]](chain[int(name[1])])
    early = [chain[int(name[1])] for name in plan if name[0] == "m" and int(name[1]) < n - 1]
    mix_step([j for j in chain if j not in early], BF16, held=False)
    return made["partial"]


def capacity_of(tokens, top, n):
    return min(tokens, max(2, 5 * tokens * top // (4 * n)))


def score_update(running, query_matrix, query_pos, key_block, value_block, key_anchor):
    run_max, run_sum, run_acc = running
    key_len = key_block.shape[0]
    scores = jnp.einsum(
        "tha,pa->htp", query_matrix, key_block, preferred_element_type=jnp.float32
    ) * (1.0 / math.sqrt(HEAD_SIZE))
    key_pos = key_anchor + jnp.arange(key_len, dtype=jnp.int32)
    visible = query_pos[:, None] >= key_pos[None, :]
    scores = jnp.where(visible, scores, HIDDEN_MASK)
    new_max = jnp.maximum(run_max, jnp.max(scores, axis=-1))
    expo = jnp.where(visible, jnp.exp(scores - new_max[..., None]), 0.0)
    factor = jnp.exp(run_max - new_max)
    new_sum = run_sum * factor + jnp.sum(expo, axis=-1)
    weights = expo.astype(jnp.bfloat16)
    new_acc = run_acc * factor[..., None] + jnp.einsum(
        "htp,pa->hta", weights, value_block, preferred_element_type=jnp.float32
    )
    return (new_max, new_sum, new_acc)


def absorb_rows(running, query_matrix, query_pos, key_rows, value_rows, anchor):
    piece_len = key_rows.shape[0]
    if piece_len > 512 and piece_len % 512 == 0:
        blocks = piece_len // 512
        key_tiles = key_rows.reshape(blocks, 512, key_rows.shape[1])
        value_tiles = value_rows.reshape(blocks, 512, value_rows.shape[1])
        anchors = anchor + 512 * jnp.arange(blocks, dtype=jnp.int32)

        def advance(state_now, tile):
            return (
                score_update(state_now, query_matrix, query_pos, tile[0], tile[1], tile[2]),
                None,
            )

        running, ignored = lax.scan(advance, running, (key_tiles, value_tiles, anchors))
        return running
    return score_update(running, query_matrix, query_pos, key_rows, value_rows, anchor)


def general(
    stream,
    query_proj,
    key_proj,
    value_projected,
    expert_ids,
    expert_home,
    router,
    norm_gain,
    w_gate,
    w_up,
    w_down,
):
    tok_rows, local_width = stream.shape
    top_count = expert_ids.shape[1]
    columns = lax.axis_size("ctx")
    features = local_width * lax.axis_size(("section", "rep"))
    capacity = capacity_of(tok_rows, top_count, columns)
    place = lax.axis_index("ctx")
    feature_index = lax.axis_index(("section", "rep"))
    heads_dev = local_width // HEAD_SIZE
    group_width = features // key_proj.shape[1]
    kv_head = feature_index * heads_dev // group_width
    query_matrix = query_proj.reshape(tok_rows, heads_dev, HEAD_SIZE)
    query_pos = place * tok_rows + jnp.arange(tok_rows, dtype=jnp.int32)
    initial = (
        jnp.full((heads_dev, tok_rows), HIDDEN_MASK, jnp.float32),
        jnp.zeros((heads_dev, tok_rows), jnp.float32),
        jnp.zeros((heads_dev, tok_rows, HEAD_SIZE), jnp.float32),
    )
    key_single = lax.dynamic_slice_in_dim(key_proj, kv_head * HEAD_SIZE, HEAD_SIZE, 1)
    value_single = lax.dynamic_slice_in_dim(value_projected, kv_head * HEAD_SIZE, HEAD_SIZE, 1)
    run_max, run_sum, run_acc = absorb_rows(
        initial,
        query_matrix,
        query_pos,
        lax.all_gather(key_single, "ctx", axis=0, tiled=True),
        lax.all_gather(value_single, "ctx", axis=0, tiled=True),
        jnp.int32(0),
    )
    attended = jnp.transpose(run_acc / run_sum[..., None], (1, 0, 2)).reshape(tok_rows, local_width)
    hidden = stream.astype(jnp.float32) + attended
    total_sq = lax.psum(jnp.sum(hidden * hidden, axis=-1), ("section", "rep"))
    scale_rows = lax.rsqrt(total_sq / features + EPSILON)
    normed = (hidden * scale_rows[:, None] * norm_gain.astype(jnp.float32)[None, :]).astype(
        jnp.bfloat16
    )
    logits = lax.psum(dot(normed, router), ("section", "rep"))
    experts_all = logits.shape[1]
    one_hot = expert_ids[:, :, None] == jnp.arange(experts_all, dtype=jnp.int32)[None, None, :]
    picked = jnp.sum(jnp.where(one_hot, logits[:, None, :], 0.0), axis=-1)
    squashed = jax.nn.sigmoid(picked)
    gates = squashed / jnp.sum(squashed, axis=-1, keepdims=True)
    target = jnp.sum(jnp.where(one_hot, expert_home[None, None, :], 0), axis=-1)
    named = target[:, :, None] == jnp.arange(columns, dtype=jnp.int32)[None, None, :]
    member = jnp.any(named, axis=1).astype(jnp.bfloat16)
    before = jnp.tril(jnp.ones((tok_rows, tok_rows), jnp.bfloat16), -1)
    rank = dot(before, member).astype(jnp.int32)
    rank = jnp.sum(jnp.where(named, rank[:, None, :], 0), axis=-1)
    slot_index = (target * capacity + rank).reshape(-1)
    placing = slot_index[None, :] == jnp.arange(columns * capacity, dtype=jnp.int32)[:, None]
    placing = jnp.any(placing.reshape(columns * capacity, tok_rows, top_count), axis=-1).astype(
        jnp.bfloat16
    )
    outgoing = dot(placing, normed).astype(jnp.bfloat16)
    outgoing = outgoing.reshape(columns, capacity, local_width)
    received = lax.all_to_all(outgoing, "ctx", split_axis=0, concat_axis=0, tiled=True)
    flat_rows = received.reshape(-1, local_width)
    gate_part = dot(flat_rows, w_gate[0])
    up_part = dot(flat_rows, w_up[0])
    gate_full = lax.psum(gate_part.astype(jnp.bfloat16), ("section", "rep")).astype(jnp.float32)
    up_full = lax.psum(up_part.astype(jnp.bfloat16), ("section", "rep")).astype(jnp.float32)
    inner = (jax.nn.silu(gate_full) * up_full).astype(jnp.bfloat16)
    answer = dot(inner, w_down[0]).astype(jnp.bfloat16)
    returned = lax.all_to_all(
        answer.reshape(received.shape), "ctx", split_axis=0, concat_axis=0, tiled=True
    )
    flat_back = returned.reshape(columns * capacity, local_width)
    picked_rows = flat_back[slot_index].reshape(tok_rows, top_count, local_width)
    mixed = jnp.sum(gates[:, :, None] * picked_rows.astype(jnp.float32), axis=1)
    return (hidden + mixed).astype(jnp.bfloat16)


def solution(mesh):
    size = dict(mesh.shape)
    pairs = size["section"] == 2 and size["rep"] == 2
    short = size["ctx"] == 4
    placed = (
        P(("group", "ctx"), ("section", "rep")),
        P(("group", "ctx"), ("section", "rep")),
        P(("group", "ctx"), None),
        P(("group", "ctx"), None),
        P(("group", "ctx"), None),
        P(),
        P(("section", "rep"), None),
        P(("section", "rep")),
        P("ctx", ("section", "rep"), None),
        P("ctx", ("section", "rep"), None),
        P("ctx", None, ("section", "rep")),
    )
    return jax.shard_map(
        direct if pairs and short else general,
        mesh=mesh,
        in_specs=placed,
        out_specs=P(("group", "ctx"), ("section", "rep")),
        check_vma=False,
    )
```

```python
import functools
import math

import jax
import jax.numpy as jnp
from jax import lax
from jax.experimental import pallas as pl
from jax.experimental.pallas import tpu as pltpu
from jax.sharding import PartitionSpec as P

HEAD_SIZE = 128
LANES = 128
EPSILON = 1e-06
HIDDEN_MASK = -1e30
VMEM_LIMIT = 16 * 1024 * 1024

F32 = jnp.float32
BF16 = jnp.bfloat16
NT = (((1,), (1,)), ((), ()))


def dot(a, b):
    return jnp.dot(a, b, preferred_element_type=F32)


def dot_nt(a, b):
    return lax.dot_general(a, b, NT, preferred_element_type=F32)


def vmem_call(body, out_shape, scalars, arrays, after=(), scratch=(), remote=(), held=True):
    multi = isinstance(out_shape, (tuple, list))
    n_out = len(out_shape) if multi else 1
    n_given = len(scalars) + len(remote) + len(arrays)
    whole = pl.BlockSpec(memory_space=pltpu.VMEM)
    anywhere = pl.BlockSpec(memory_space=pl.ANY)

    def placed(x):
        return pltpu.VMEM(x.shape, x.dtype) if held else x

    def kernel(*refs):
        body(*refs[:n_given], *refs[n_given + len(after) :])

    kernel.__name__ = getattr(body, "func", body).__name__
    return pl.pallas_call(
        kernel,
        out_shape=[placed(x) for x in out_shape] if multi else placed(out_shape),
        in_specs=[pl.BlockSpec(memory_space=pltpu.SMEM)] * len(scalars)
        + [pl.BlockSpec(memory_space=pltpu.HBM)] * len(remote)
        + [whole] * len(arrays)
        + [anywhere] * len(after),
        out_specs=[whole] * n_out if multi else (whole if held else anywhere),
        scratch_shapes=list(scratch),
        compiler_params=pltpu.CompilerParams(vmem_limit_bytes=VMEM_LIMIT),
        cost_estimate=pl.CostEstimate(flops=1, bytes_accessed=1, transcendentals=0),
    )(
        *scalars,
        *[pltpu.with_memory_space_constraint(x, pltpu.HBM) for x in remote],
        *[pltpu.with_memory_space_constraint(x, pltpu.VMEM) for x in arrays],
        *after,
    )


def carry(copies):
    for copy in copies:
        copy.start()
    for copy in copies:
        copy.wait()


def prepare_kernel(head_ref, rep_ref, key_in, value_in, kv_ref, part_ref, sems):
    columns = pl.ds(pl.multiple_of(head_ref[0] * HEAD_SIZE, HEAD_SIZE), HEAD_SIZE)
    carry(
        [
            pltpu.make_async_copy(
                ref.at[:, columns], kv_ref.at[:, pl.ds(i * HEAD_SIZE, HEAD_SIZE)], sems.at[i]
            )
            for i, ref in enumerate((key_in, value_in))
        ]
    )
    for i in range(2):

        @pl.when(rep_ref[0] == i)
        def _():
            part_ref[...] = kv_ref[:, i * HEAD_SIZE : (i + 1) * HEAD_SIZE]


def fetch_kernel(experts, *refs):
    count = (len(refs) - 4) // 2
    sources, home_in, targets, (target_ref, home_ref, sems) = (
        refs[:count],
        refs[count],
        refs[count + 1 : 2 * count + 1],
        refs[2 * count + 1 :],
    )
    pairs = [(home_in, home_ref), *zip(sources, targets)]
    carry([pltpu.make_async_copy(a, b, sems.at[i]) for i, (a, b) in enumerate(pairs)])
    ids = targets[-1][...]
    target = jnp.zeros(ids.shape, jnp.int32)
    for expert in range(experts):
        target = jnp.where(ids == expert, home_ref[0:1, expert : expert + 1], target)
    target_ref[...] = target


def attend_kernel(n, first, place_ref, rep_ref, gate_in, up_in, q_ref, stream_ref, gain_ref, target_ref, kv_ref, *rest):
    (near_mine, near_theirs, far_mine, far_theirs), rest = rest[:4], rest[4:]
    hidden_ref, gained, squares_ref, first_ref, *weight_refs, k_all, v_all, sems = rest
    pairs = zip((gate_in, up_in), weight_refs)
    copies = [pltpu.make_async_copy(a, b, sems.at[i]) for i, (a, b) in enumerate(pairs)]
    for copy in copies:
        copy.start()
    place = place_ref[0]
    tokens = q_ref.shape[0]
    heads = q_ref.shape[1] // HEAD_SIZE
    row = lax.broadcasted_iota(jnp.int32, (tokens, tokens), 0)
    col = lax.broadcasted_iota(jnp.int32, (tokens, tokens), 1)
    pieces = [jnp.where(row >= col, 0.0, HIDDEN_MASK)]
    rep = rep_ref[0]
    for block, (ref, offset) in enumerate(
        ((kv_ref, 0), (None, 1), (far_mine, 2 + rep), (far_theirs, 3 - rep))
    ):
        rows = slice(block * tokens, (block + 1) * tokens)
        if ref is not None:
            k_all[rows, :] = ref[:, :HEAD_SIZE]
            v_all[rows, :] = ref[:, HEAD_SIZE:]
        if block:
            seen = jnp.where(jnp.bitwise_xor(place, offset) < place, 0.0, HIDDEN_MASK)
            pieces.append(jnp.full((tokens, tokens), seen, F32))

    @pl.when(rep == 0)
    def _():
        k_all[tokens : 2 * tokens, :] = near_mine[...]
        v_all[tokens : 2 * tokens, :] = near_theirs[...]

    @pl.when(rep == 1)
    def _():
        k_all[tokens : 2 * tokens, :] = near_theirs[...]
        v_all[tokens : 2 * tokens, :] = near_mine[...]

    bias = jnp.concatenate(pieces, axis=1)
    stacked = jnp.concatenate(
        [q_ref[:, h * HEAD_SIZE : (h + 1) * HEAD_SIZE] for h in range(heads)], axis=0
    )
    scored = dot_nt(stacked, k_all[...])
    squares = jnp.zeros((tokens, 1), F32)
    for head in range(heads):
        cols = slice(head * HEAD_SIZE, (head + 1) * HEAD_SIZE)
        scores = scored[head * tokens : (head + 1) * tokens, :] * (1.0 / math.sqrt(HEAD_SIZE)) + bias
        expo = jnp.exp(scores - jnp.max(scores, axis=-1, keepdims=True))
        total = jnp.sum(expo, axis=-1, keepdims=True)
        attended = dot(expo.astype(BF16), v_all[...]) / total
        hidden = stream_ref[:, cols].astype(F32) + attended
        hidden_ref[:, cols] = hidden
        squares = squares + jnp.sum(hidden * hidden, axis=-1, keepdims=True)
        gained[:, cols] = (hidden * gain_ref[head : head + 1, :].astype(F32)).astype(BF16)
    squares_ref[...] = jnp.broadcast_to(squares, squares_ref.shape)
    place_rows(place, target_ref, gained[...], [first], [first_ref])
    for copy in copies:
        copy.wait()


def place_rows(place, target_ref, values, blocks, row_refs):
    tokens = values.shape[0]
    earlier = (
        lax.broadcasted_iota(jnp.int32, (tokens, tokens), 0)
        < lax.broadcasted_iota(jnp.int32, (tokens, tokens), 1)
    ).astype(F32).astype(BF16)
    slot = lax.broadcasted_iota(jnp.int32, (row_refs[0].shape[0], tokens), 0)
    for j, row_ref in zip(blocks, row_refs):
        member = jnp.sum((target_ref[...] == jnp.bitwise_xor(place, j)).astype(F32), axis=0, keepdims=True)
        rank = dot(jnp.broadcast_to(member, (8, tokens)).astype(BF16), earlier)[0:1, :]
        rank = jnp.where(member > 0.5, rank, -1.0).astype(jnp.int32)
        placing = (slot == rank).astype(F32).astype(BF16)
        row_ref[...] = dot(placing, values).astype(BF16)


def rows_kernel(blocks, place_ref, down_in, gained_ref, squares_ref, router_ref, target_ref, *refs):
    row_refs, (stats_ref, down_ref, sem) = refs[: len(blocks)], refs[len(blocks) :]
    copy = pltpu.make_async_copy(down_in, down_ref, sem)
    copy.start()
    values = gained_ref[...]
    place_rows(place_ref[0], target_ref, values, blocks, row_refs)
    squares_row = jnp.transpose(squares_ref[...])
    height = stats_ref.shape[0]
    stats_ref[...] = jnp.concatenate(
        [dot_nt(router_ref[...], values), squares_row[: height - router_ref.shape[0], :]], axis=0
    )
    copy.wait()


def split_pair(x):
    high = x.astype(BF16).astype(F32)
    lane = lax.broadcasted_iota(jnp.int32, x.shape, 1)
    return jnp.where(lane < LANES // 2, high, x - high).astype(BF16)


def join_pair(ref, rows, start):
    return jnp.sum(ref[rows, start:].astype(F32), axis=-1, keepdims=True) * (2.0 / LANES)


def put_stats(ref, base, stats):
    height, tokens = stats.shape
    ref[base:, :] = jnp.zeros((ref.shape[0] - base, ref.shape[1]), BF16)
    terms = []
    for i in range(3):
        term = stats.astype(BF16)
        stats = stats - term.astype(F32)
        terms.append(term.astype(F32))
    pad = jnp.zeros((ref.shape[0] - base - height, 3 * tokens), F32)
    ref[base:, : 3 * tokens] = jnp.concatenate(
        [jnp.concatenate(terms, axis=1), pad], axis=0
    ).astype(BF16)


def get_stats(ref, base, like):
    height, tokens = like.shape
    parts = ref[base:, : 3 * tokens].astype(F32)[:height]
    return parts[:, :tokens] + parts[:, tokens : 2 * tokens] + parts[:, 2 * tokens :]


def up_kernel(with_stats, rep_ref, gate_ref, up_ref, gain_ref, *rest):
    rows_ref, keep_ref, first_ref, second_ref = rest[-4:]
    count = rows_ref.shape[0]
    half = gate_ref.shape[1] // 2
    mine = pl.multiple_of(rep_ref[0] * half, LANES)
    other = pl.multiple_of((1 - rep_ref[0]) * half, LANES)
    rows = rows_ref[...]
    squares = jnp.zeros((count, LANES), F32)
    for i in range(gain_ref.shape[0]):
        plain = rows[:, i * LANES : (i + 1) * LANES].astype(F32) / gain_ref[i : i + 1, :].astype(F32)
        squares = squares + plain * plain
    squares = jnp.broadcast_to(jnp.sum(squares, axis=-1, keepdims=True), (count, LANES))
    first_ref[...] = dot(rows, gate_ref[:, pl.ds(other, half)]).astype(BF16)
    second_ref[:count, :half] = dot(rows, up_ref[:, pl.ds(other, half)]).astype(BF16)
    second_ref[:count, half:] = split_pair(squares)
    keep_ref[:, :half] = dot(rows, gate_ref[:, pl.ds(mine, half)])
    keep_ref[:, half : 2 * half] = dot(rows, up_ref[:, pl.ds(mine, half)])
    keep_ref[:, 2 * half :] = squares
    if with_stats:
        put_stats(second_ref, count, rest[0][...])


def add_kernel(with_stats, *refs):
    keep_ref, first_ref, second_ref, sum_ref, send_ref = refs[with_stats : with_stats + 5]
    count = keep_ref.shape[0]
    wide = keep_ref.shape[1] - LANES
    half = first_ref.shape[1]
    for start, ref in ((0, first_ref), (half, second_ref)):
        both = keep_ref[:, start : start + half] + ref[:count, :half].astype(F32)
        sum_ref[:, start : start + half] = both
        send_ref[:count, start : start + half] = both.astype(BF16)
    squares = keep_ref[:, wide:] + join_pair(second_ref, slice(0, count), half)
    sum_ref[:, wide:] = squares
    send_ref[:count, wide:] = split_pair(squares)
    if with_stats:
        stats_ref, total_ref = refs[0], refs[-1]
        stats = stats_ref[...] + get_stats(second_ref, count, stats_ref)
        total_ref[...] = stats
        put_stats(send_ref, count, stats)


def inner_kernel(features, with_stats, *refs):
    sum_ref, got_ref, inner_ref = refs[with_stats : with_stats + 3]
    count = sum_ref.shape[0]
    wide = sum_ref.shape[1] - LANES
    half = wide // 2
    squares = sum_ref[:, wide : wide + 1] + join_pair(got_ref, slice(0, count), wide)
    scale = lax.rsqrt(squares * (1.0 / features) + EPSILON)
    gate = (sum_ref[:, :half] + got_ref[:count, :half].astype(F32)) * scale
    up = (sum_ref[:, half:wide] + got_ref[:count, half:wide].astype(F32)) * scale
    inner_ref[...] = (gate * jax.nn.sigmoid(gate) * up).astype(BF16)
    if with_stats:
        stats_ref, total_ref = refs[0], refs[-1]
        total_ref[...] = stats_ref[...] + get_stats(got_ref, count, stats_ref)


def down_kernel(rep_ref, down_ref, mine_ref, other_ref, out_ref, inner):
    half = mine_ref.shape[1]
    for i in range(2):

        @pl.when(rep_ref[0] == i)
        def _():
            inner[:, i * half : (i + 1) * half] = mine_ref[...]
            inner[:, (1 - i) * half : (2 - i) * half] = other_ref[...]

    out_ref[...] = dot(inner[...], down_ref[...]).astype(BF16)


def gates_kernel(cap, features, place_ref, stats_ref, ids_ref, target_ref, *weight_refs):
    place = place_ref[0]
    top, tokens = ids_ref.shape
    stats = jnp.transpose(stats_ref[...])
    height = stats.shape[1]
    scale = lax.rsqrt(stats[:, height - 1 :] * (1.0 / features) + EPSILON)
    logits = stats * scale
    both = jnp.concatenate(
        [ids_ref[...], target_ref[...], jnp.zeros((8 - 2 * top, tokens), jnp.int32)], axis=0
    )
    both = jnp.transpose(both.astype(F32)).astype(jnp.int32)
    kinds = lax.broadcasted_iota(jnp.int32, stats.shape, 1)
    squashed = [
        jax.nn.sigmoid(
            jnp.sum(jnp.where(kinds == both[:, k : k + 1], logits, 0.0), axis=-1, keepdims=True)
        )
        for k in range(top)
    ]
    whole = functools.reduce(lambda a, b: a + b, squashed)
    blocks = jnp.bitwise_xor(lax.broadcasted_iota(jnp.int32, (tokens, LANES), 1), place)
    named = [both[:, top + k : top + k + 1] == blocks for k in range(top)]
    member = functools.reduce(lambda a, b: a + b, [x.astype(F32) for x in named])
    later = (
        lax.broadcasted_iota(jnp.int32, (tokens, tokens), 0)
        > lax.broadcasted_iota(jnp.int32, (tokens, tokens), 1)
    ).astype(F32).astype(BF16)
    rank = dot(later, member.astype(BF16))
    slot = lax.broadcasted_iota(jnp.int32, (tokens, cap), 1)
    for j, weights_ref in enumerate(weight_refs):
        weights = jnp.zeros((tokens, cap), F32)
        for k in range(top):
            at = jnp.where(named[k][:, j : j + 1], rank[:, j : j + 1], -1.0).astype(jnp.int32)
            weights = weights + jnp.where(slot == at, squashed[k] / whole, 0.0)
        high = weights.astype(BF16)
        weights_ref[:tokens, :] = high
        weights_ref[tokens:, :] = (weights - high.astype(F32)).astype(BF16)


def mix_kernel(count, partial_ref, *rest):
    weights, answers, out_ref = rest[:count], rest[count : 2 * count], rest[-1]
    tokens = partial_ref.shape[0]
    total = partial_ref[...]
    for weights_ref, answer_ref in zip(weights, answers):
        mixed = dot(weights_ref[...], answer_ref[...])
        total = total + (mixed[:tokens] + mixed[tokens:])
    out_ref[...] = total.astype(out_ref.dtype)


def last_kernel(count, partial_ref, *rest):
    weights, answers, (out_ref, staged, sems) = rest[:count], rest[count : 2 * count], rest[2 * count :]
    tokens, width = partial_ref.shape
    pieces = sems.shape[0]
    span = width // pieces
    copies = []
    for i in range(pieces):
        cols = slice(i * span, (i + 1) * span)
        total = partial_ref[:, cols]
        for weights_ref, answer_ref in zip(weights, answers):
            mixed = dot(weights_ref[...], answer_ref[:, cols])
            total = total + (mixed[:tokens] + mixed[tokens:])
        staged[:, cols] = total.astype(BF16)
        copies.append(
            pltpu.make_async_copy(
                staged.at[:, pl.ds(i * span, span)], out_ref.at[:, pl.ds(i * span, span)], sems.at[i]
            )
        )
        copies[-1].start()
    for copy in copies:
        copy.wait()


def swap(x, axis):
    return lax.ppermute(x, axis, [(0, 1), (1, 0)])


def direct(
    stream,
    query_proj,
    key_proj,
    value_projected,
    expert_ids,
    expert_home,
    router,
    norm_gain,
    w_gate,
    w_up,
    w_down,
):
    tokens, width = stream.shape
    top = expert_ids.shape[1]
    n = lax.axis_size("ctx")
    features = width * lax.axis_size(("section", "rep"))
    experts = router.shape[1]
    hid = w_gate.shape[2]
    wide = hid + LANES
    cap = capacity_of(tokens, top, n)
    where = lax.axis_index("ctx").astype(jnp.int32).reshape(1)
    side = lax.axis_index("rep").astype(jnp.int32).reshape(1)
    heads = width // HEAD_SIZE
    group_width = features // key_proj.shape[1]
    kv_head = (lax.axis_index(("section", "rep")) * heads // group_width).astype(jnp.int32).reshape(1)

    def exchange(x, j):
        return lax.ppermute(x, "ctx", [(i, i ^ j) for i in range(n)])

    def like(x):
        return jax.ShapeDtypeStruct(x.shape, x.dtype)

    own_kv, part = vmem_call(
        prepare_kernel,
        [jax.ShapeDtypeStruct((tokens, w * HEAD_SIZE), BF16) for w in (2, 1)],
        [kv_head, side],
        [],
        remote=[key_proj, value_projected],
        scratch=[pltpu.SemaphoreType.DMA((2,))],
    )
    sources = [query_proj, stream, norm_gain.reshape(width // LANES, LANES), router.T, expert_ids.T]
    queries, stream, gain, router_rows, ids_rows, target = vmem_call(
        functools.partial(fetch_kernel, experts),
        [like(x) for x in sources] + [jax.ShapeDtypeStruct((top, tokens), jnp.int32)],
        [],
        [],
        remote=[*sources, expert_home.reshape(1, experts)],
        after=[part],
        scratch=[pltpu.VMEM((1, experts), jnp.int32), pltpu.SemaphoreType.DMA((6,))],
    )
    distance = sorted(range(1, n), key=lambda j: (j < n // 2, j))
    near_kv = exchange(part, 1)
    far_kv = lax.ppermute(
        own_kv, ("ctx", "rep"), [(2 * i + r, 2 * (i ^ (2 + r)) + r) for i in range(n) for r in range(2)]
    )
    stat_rows = -(-(experts + 1) // 8) * 8

    chain = [0] + [distance[0], *distance[:0:-1]]
    block = jax.ShapeDtypeStruct((cap, width), BF16)
    weights = [w_gate[0], w_up[0]]
    hidden, gained, squares, first_rows, gate, up = vmem_call(
        functools.partial(attend_kernel, n, chain[1]),
        [
            jax.ShapeDtypeStruct((tokens, width), F32),
            jax.ShapeDtypeStruct((tokens, width), BF16),
            jax.ShapeDtypeStruct((tokens, LANES), F32),
            block,
        ]
        + [like(x) for x in weights],
        [where, side],
        [queries, stream, gain, target, own_kv, near_kv, swap(near_kv, "rep")]
        + [far_kv, swap(far_kv, "rep")],
        remote=weights,
        scratch=[
            pltpu.VMEM((n * tokens, HEAD_SIZE), BF16),
            pltpu.VMEM((n * tokens, HEAD_SIZE), BF16),
            pltpu.SemaphoreType.DMA((2,)),
        ],
    )
    others = [j for j in range(n) if j != chain[1]]
    *rows, stats, down = vmem_call(
        functools.partial(rows_kernel, others),
        [block] * (n - 1) + [jax.ShapeDtypeStruct((stat_rows, tokens), F32), like(w_down[0])],
        [where],
        [gained, squares, router_rows, target],
        remote=[w_down[0]],
        scratch=[pltpu.SemaphoreType.DMA],
    )
    rows = {chain[1]: first_rows, **dict(zip(others, rows))}
    arrived = {j: exchange(rows[j], j) for j in distance}
    arrived[0] = rows[0]

    extra = -(-stat_rows // 16) * 16
    state = {}
    made = {"last": hidden, "stats": stats, "partial": hidden}

    def run(body, out_shape, scalars, arrays, scratch=(), held=True):
        outs = vmem_call(
            body, out_shape, scalars, arrays, after=[made["last"]], scratch=scratch, held=held
        )
        made["last"] = outs[0] if isinstance(outs, (tuple, list)) else outs
        return outs

    def stat_part(j):
        return (1, [made["stats"]], [like(stats)], extra) if j == 1 else (0, [], [], 0)

    def up_step(j):
        flag, given, made_too, more = stat_part(j)
        keep, first, second = run(
            functools.partial(up_kernel, flag),
            [
                jax.ShapeDtypeStruct((cap, wide), F32),
                jax.ShapeDtypeStruct((cap, hid // 2), BF16),
                jax.ShapeDtypeStruct((cap + more, hid // 2 + LANES), BF16),
            ],
            [side],
            [gate, up, gain] + given + [arrived[j]],
        )
        state[j] = (keep, swap(first, "rep"), swap(second, "rep"))

    def add_step(j):
        flag, given, made_too, more = stat_part(j)
        both, send, *rest = run(
            functools.partial(add_kernel, flag),
            [jax.ShapeDtypeStruct((cap, wide), F32), jax.ShapeDtypeStruct((cap + more, wide), BF16)]
            + made_too,
            [],
            given + list(state[j]),
        )
        if rest:
            made["stats"] = rest[0]
        state[j] = (both, swap(send, "section"))

    def inner_step(j):
        flag, given, made_too, more = stat_part(j)
        inner, *rest = run(
            functools.partial(inner_kernel, features, flag),
            [jax.ShapeDtypeStruct((cap, hid // 2), BF16)] + made_too,
            [],
            given + list(state[j]),
        )
        if rest:
            made["stats"] = rest[0]
        state[j] = (inner, swap(inner, "rep"))

    def down_step(j):
        answer = run(
            down_kernel,
            jax.ShapeDtypeStruct((cap, width), BF16),
            [side],
            [down, *state[j]],
            scratch=[pltpu.VMEM((cap, hid), BF16)],
        )
        state[j] = exchange(answer, j) if j else answer

    def gates_step():
        made["weights"] = run(
            functools.partial(gates_kernel, cap, features),
            [jax.ShapeDtypeStruct((2 * tokens, cap), BF16)] * n,
            [where],
            [made["stats"], ids_rows, target],
        )

    def mix_step(blocks, last=False):
        pieces = 2 if width % (2 * LANES) == 0 else 1
        made["partial"] = run(
            functools.partial(last_kernel if last else mix_kernel, len(blocks)),
            jax.ShapeDtypeStruct((tokens, width), BF16 if last else F32),
            [],
            [made["partial"]] + [made["weights"][j] for j in blocks] + [state[j] for j in blocks],
            scratch=[pltpu.VMEM((tokens, width), BF16), pltpu.SemaphoreType.DMA((pieces,))] if last else (),
            held=not last,
        )

    steps = dict(u=up_step, a=add_step, i=inner_step, d=down_step, m=lambda j: mix_step([j]))
    plan = (
        *("u0", "a0", "u1", "i0", "a1", "u2", "a2", "u3", "i1", "d0"),
        *("d1", "a3", "i2", "d2", "g", "m0", "i3", "m1", "d3", "m2"),
    )
    for name in plan:
        if name == "g":
            gates_step()
        elif int(name[1]) < n - (name[0] == "m"):
            steps[name[0]](chain[int(name[1])])
    early = [chain[int(name[1])] for name in plan if name[0] == "m" and int(name[1]) < n - 1]
    mix_step([j for j in chain if j not in early], last=True)
    return made["partial"]


def capacity_of(tokens, top, n):
    return min(tokens, max(2, 5 * tokens * top // (4 * n)))


def score_update(running, query_matrix, query_pos, key_block, value_block, key_anchor):
    run_max, run_sum, run_acc = running
    key_len = key_block.shape[0]
    scores = jnp.einsum(
        "tha,pa->htp", query_matrix, key_block, preferred_element_type=jnp.float32
    ) * (1.0 / math.sqrt(HEAD_SIZE))
    key_pos = key_anchor + jnp.arange(key_len, dtype=jnp.int32)
    visible = query_pos[:, None] >= key_pos[None, :]
    scores = jnp.where(visible, scores, HIDDEN_MASK)
    new_max = jnp.maximum(run_max, jnp.max(scores, axis=-1))
    expo = jnp.where(visible, jnp.exp(scores - new_max[..., None]), 0.0)
    factor = jnp.exp(run_max - new_max)
    new_sum = run_sum * factor + jnp.sum(expo, axis=-1)
    weights = expo.astype(jnp.bfloat16)
    new_acc = run_acc * factor[..., None] + jnp.einsum(
        "htp,pa->hta", weights, value_block, preferred_element_type=jnp.float32
    )
    return (new_max, new_sum, new_acc)


def absorb_rows(running, query_matrix, query_pos, key_rows, value_rows, anchor):
    piece_len = key_rows.shape[0]
    if piece_len > 512 and piece_len % 512 == 0:
        blocks = piece_len // 512
        key_tiles = key_rows.reshape(blocks, 512, key_rows.shape[1])
        value_tiles = value_rows.reshape(blocks, 512, value_rows.shape[1])
        anchors = anchor + 512 * jnp.arange(blocks, dtype=jnp.int32)

        def advance(state_now, tile):
            return (
                score_update(state_now, query_matrix, query_pos, tile[0], tile[1], tile[2]),
                None,
            )

        running, ignored = lax.scan(advance, running, (key_tiles, value_tiles, anchors))
        return running
    return score_update(running, query_matrix, query_pos, key_rows, value_rows, anchor)


def general(
    stream,
    query_proj,
    key_proj,
    value_projected,
    expert_ids,
    expert_home,
    router,
    norm_gain,
    w_gate,
    w_up,
    w_down,
):
    tok_rows, local_width = stream.shape
    top_count = expert_ids.shape[1]
    columns = lax.axis_size("ctx")
    features = local_width * lax.axis_size(("section", "rep"))
    capacity = capacity_of(tok_rows, top_count, columns)
    place = lax.axis_index("ctx")
    feature_index = lax.axis_index(("section", "rep"))
    heads_dev = local_width // HEAD_SIZE
    group_width = features // key_proj.shape[1]
    kv_head = feature_index * heads_dev // group_width
    query_matrix = query_proj.reshape(tok_rows, heads_dev, HEAD_SIZE)
    query_pos = place * tok_rows + jnp.arange(tok_rows, dtype=jnp.int32)
    initial = (
        jnp.full((heads_dev, tok_rows), HIDDEN_MASK, jnp.float32),
        jnp.zeros((heads_dev, tok_rows), jnp.float32),
        jnp.zeros((heads_dev, tok_rows, HEAD_SIZE), jnp.float32),
    )
    key_single = lax.dynamic_slice_in_dim(key_proj, kv_head * HEAD_SIZE, HEAD_SIZE, 1)
    value_single = lax.dynamic_slice_in_dim(value_projected, kv_head * HEAD_SIZE, HEAD_SIZE, 1)
    run_max, run_sum, run_acc = absorb_rows(
        initial,
        query_matrix,
        query_pos,
        lax.all_gather(key_single, "ctx", axis=0, tiled=True),
        lax.all_gather(value_single, "ctx", axis=0, tiled=True),
        jnp.int32(0),
    )
    attended = jnp.transpose(run_acc / run_sum[..., None], (1, 0, 2)).reshape(tok_rows, local_width)
    hidden = stream.astype(jnp.float32) + attended
    total_sq = lax.psum(jnp.sum(hidden * hidden, axis=-1), ("section", "rep"))
    scale_rows = lax.rsqrt(total_sq / features + EPSILON)
    normed = (hidden * scale_rows[:, None] * norm_gain.astype(jnp.float32)[None, :]).astype(
        jnp.bfloat16
    )
    logits = lax.psum(dot(normed, router), ("section", "rep"))
    experts_all = logits.shape[1]
    one_hot = expert_ids[:, :, None] == jnp.arange(experts_all, dtype=jnp.int32)[None, None, :]
    picked = jnp.sum(jnp.where(one_hot, logits[:, None, :], 0.0), axis=-1)
    squashed = jax.nn.sigmoid(picked)
    gates = squashed / jnp.sum(squashed, axis=-1, keepdims=True)
    target = jnp.sum(jnp.where(one_hot, expert_home[None, None, :], 0), axis=-1)
    named = target[:, :, None] == jnp.arange(columns, dtype=jnp.int32)[None, None, :]
    member = jnp.any(named, axis=1).astype(jnp.bfloat16)
    before = jnp.tril(jnp.ones((tok_rows, tok_rows), jnp.bfloat16), -1)
    rank = dot(before, member).astype(jnp.int32)
    rank = jnp.sum(jnp.where(named, rank[:, None, :], 0), axis=-1)
    slot_index = (target * capacity + rank).reshape(-1)
    placing = slot_index[None, :] == jnp.arange(columns * capacity, dtype=jnp.int32)[:, None]
    placing = jnp.any(placing.reshape(columns * capacity, tok_rows, top_count), axis=-1).astype(
        jnp.bfloat16
    )
    outgoing = dot(placing, normed).astype(jnp.bfloat16)
    outgoing = outgoing.reshape(columns, capacity, local_width)
    received = lax.all_to_all(outgoing, "ctx", split_axis=0, concat_axis=0, tiled=True)
    flat_rows = received.reshape(-1, local_width)
    gate_part = dot(flat_rows, w_gate[0])
    up_part = dot(flat_rows, w_up[0])
    gate_full = lax.psum(gate_part.astype(jnp.bfloat16), ("section", "rep")).astype(jnp.float32)
    up_full = lax.psum(up_part.astype(jnp.bfloat16), ("section", "rep")).astype(jnp.float32)
    inner = (jax.nn.silu(gate_full) * up_full).astype(jnp.bfloat16)
    answer = dot(inner, w_down[0]).astype(jnp.bfloat16)
    returned = lax.all_to_all(
        answer.reshape(received.shape), "ctx", split_axis=0, concat_axis=0, tiled=True
    )
    flat_back = returned.reshape(columns * capacity, local_width)
    picked_rows = flat_back[slot_index].reshape(tok_rows, top_count, local_width)
    mixed = jnp.sum(gates[:, :, None] * picked_rows.astype(jnp.float32), axis=1)
    return (hidden + mixed).astype(jnp.bfloat16)


def solution(mesh):
    size = dict(mesh.shape)
    pairs = size["section"] == 2 and size["rep"] == 2
    short = size["ctx"] == 4
    placed = (
        P(("group", "ctx"), ("section", "rep")),
        P(("group", "ctx"), ("section", "rep")),
        P(("group", "ctx"), None),
        P(("group", "ctx"), None),
        P(("group", "ctx"), None),
        P(),
        P(("section", "rep"), None),
        P(("section", "rep")),
        P("ctx", ("section", "rep"), None),
        P("ctx", ("section", "rep"), None),
        P("ctx", None, ("section", "rep")),
    )
    return jax.shard_map(
        direct if pairs and short else general,
        mesh=mesh,
        in_specs=placed,
        out_specs=P(("group", "ctx"), ("section", "rep")),
        check_vma=False,
    )
```

```python
import functools
import math

import jax
import jax.numpy as jnp
from jax import lax
from jax.experimental import pallas as pl
from jax.experimental.pallas import tpu as pltpu
from jax.sharding import PartitionSpec as P

HEAD_SIZE = 128
LANES = 128
EPSILON = 1e-06
HIDDEN_MASK = -1e30
VMEM_LIMIT = 16 * 1024 * 1024

F32 = jnp.float32
BF16 = jnp.bfloat16
NT = (((1,), (1,)), ((), ()))


def dot(a, b):
    return jnp.dot(a, b, preferred_element_type=F32)


def dot_nt(a, b):
    return lax.dot_general(a, b, NT, preferred_element_type=F32)


def vmem_call(body, out_shape, scalars, arrays, after=(), scratch=(), remote=(), held=True):
    multi = isinstance(out_shape, (tuple, list))
    n_out = len(out_shape) if multi else 1
    n_given = len(scalars) + len(remote) + len(arrays)
    whole = pl.BlockSpec(memory_space=pltpu.VMEM)
    anywhere = pl.BlockSpec(memory_space=pl.ANY)

    def placed(x):
        return pltpu.VMEM(x.shape, x.dtype) if held else x

    def kernel(*refs):
        body(*refs[:n_given], *refs[n_given + len(after) :])

    kernel.__name__ = getattr(body, "func", body).__name__
    return pl.pallas_call(
        kernel,
        out_shape=[placed(x) for x in out_shape] if multi else placed(out_shape),
        in_specs=[pl.BlockSpec(memory_space=pltpu.SMEM)] * len(scalars)
        + [pl.BlockSpec(memory_space=pltpu.HBM)] * len(remote)
        + [whole] * len(arrays)
        + [anywhere] * len(after),
        out_specs=[whole] * n_out if multi else whole,
        scratch_shapes=list(scratch),
        compiler_params=pltpu.CompilerParams(vmem_limit_bytes=VMEM_LIMIT),
        cost_estimate=pl.CostEstimate(flops=1, bytes_accessed=1, transcendentals=0),
    )(
        *scalars,
        *[pltpu.with_memory_space_constraint(x, pltpu.HBM) for x in remote],
        *[pltpu.with_memory_space_constraint(x, pltpu.VMEM) for x in arrays],
        *after,
    )


def carry(copies):
    for copy in copies:
        copy.start()
    for copy in copies:
        copy.wait()


def prepare_kernel(head_ref, rep_ref, key_in, value_in, kv_ref, part_ref, sems):
    columns = pl.ds(pl.multiple_of(head_ref[0] * HEAD_SIZE, HEAD_SIZE), HEAD_SIZE)
    carry(
        [
            pltpu.make_async_copy(
                ref.at[:, columns], kv_ref.at[:, pl.ds(i * HEAD_SIZE, HEAD_SIZE)], sems.at[i]
            )
            for i, ref in enumerate((key_in, value_in))
        ]
    )
    for i in range(2):

        @pl.when(rep_ref[0] == i)
        def _():
            part_ref[...] = kv_ref[:, i * HEAD_SIZE : (i + 1) * HEAD_SIZE]


def fetch_kernel(experts, *refs):
    count = (len(refs) - 4) // 2
    sources, home_in, targets, (target_ref, home_ref, sems) = (
        refs[:count],
        refs[count],
        refs[count + 1 : 2 * count + 1],
        refs[2 * count + 1 :],
    )
    pairs = [(home_in, home_ref), *zip(sources, targets)]
    carry([pltpu.make_async_copy(a, b, sems.at[i]) for i, (a, b) in enumerate(pairs)])
    ids = targets[-1][...]
    target = jnp.zeros(ids.shape, jnp.int32)
    for expert in range(experts):
        target = jnp.where(ids == expert, home_ref[0:1, expert : expert + 1], target)
    target_ref[...] = target


def attend_kernel(n, first, place_ref, rep_ref, gate_in, up_in, q_ref, stream_ref, gain_ref, target_ref, kv_ref, *rest):
    (near_mine, near_theirs, far_mine, far_theirs), rest = rest[:4], rest[4:]
    hidden_ref, gained, squares_ref, first_ref, *weight_refs, k_all, v_all, sems = rest
    pairs = zip((gate_in, up_in), weight_refs)
    copies = [pltpu.make_async_copy(a, b, sems.at[i]) for i, (a, b) in enumerate(pairs)]
    for copy in copies:
        copy.start()
    place = place_ref[0]
    tokens = q_ref.shape[0]
    heads = q_ref.shape[1] // HEAD_SIZE
    row = lax.broadcasted_iota(jnp.int32, (tokens, tokens), 0)
    col = lax.broadcasted_iota(jnp.int32, (tokens, tokens), 1)
    pieces = [jnp.where(row >= col, 0.0, HIDDEN_MASK)]
    rep = rep_ref[0]
    for block, (ref, offset) in enumerate(
        ((kv_ref, 0), (None, 1), (far_mine, 2 + rep), (far_theirs, 3 - rep))
    ):
        rows = slice(block * tokens, (block + 1) * tokens)
        if ref is not None:
            k_all[rows, :] = ref[:, :HEAD_SIZE]
            v_all[rows, :] = ref[:, HEAD_SIZE:]
        if block:
            seen = jnp.where(jnp.bitwise_xor(place, offset) < place, 0.0, HIDDEN_MASK)
            pieces.append(jnp.full((tokens, tokens), seen, F32))

    @pl.when(rep == 0)
    def _():
        k_all[tokens : 2 * tokens, :] = near_mine[...]
        v_all[tokens : 2 * tokens, :] = near_theirs[...]

    @pl.when(rep == 1)
    def _():
        k_all[tokens : 2 * tokens, :] = near_theirs[...]
        v_all[tokens : 2 * tokens, :] = near_mine[...]

    bias = jnp.concatenate(pieces, axis=1)
    stacked = jnp.concatenate(
        [q_ref[:, h * HEAD_SIZE : (h + 1) * HEAD_SIZE] for h in range(heads)], axis=0
    )
    scored = dot_nt(stacked, k_all[...])
    squares = jnp.zeros((tokens, 1), F32)
    for head in range(heads):
        cols = slice(head * HEAD_SIZE, (head + 1) * HEAD_SIZE)
        scores = scored[head * tokens : (head + 1) * tokens, :] * (1.0 / math.sqrt(HEAD_SIZE)) + bias
        expo = jnp.exp(scores - jnp.max(scores, axis=-1, keepdims=True))
        total = jnp.sum(expo, axis=-1, keepdims=True)
        attended = dot(expo.astype(BF16), v_all[...]) / total
        hidden = stream_ref[:, cols].astype(F32) + attended
        hidden_ref[:, cols] = hidden
        squares = squares + jnp.sum(hidden * hidden, axis=-1, keepdims=True)
        gained[:, cols] = (hidden * gain_ref[head : head + 1, :].astype(F32)).astype(BF16)
    squares_ref[...] = jnp.broadcast_to(squares, squares_ref.shape)
    place_rows(place, target_ref, gained[...], [first], [first_ref])
    for copy in copies:
        copy.wait()


def place_rows(place, target_ref, values, blocks, row_refs):
    tokens = values.shape[0]
    earlier = (
        lax.broadcasted_iota(jnp.int32, (tokens, tokens), 0)
        < lax.broadcasted_iota(jnp.int32, (tokens, tokens), 1)
    ).astype(F32).astype(BF16)
    slot = lax.broadcasted_iota(jnp.int32, (row_refs[0].shape[0], tokens), 0)
    for j, row_ref in zip(blocks, row_refs):
        member = jnp.sum((target_ref[...] == jnp.bitwise_xor(place, j)).astype(F32), axis=0, keepdims=True)
        rank = dot(jnp.broadcast_to(member, (8, tokens)).astype(BF16), earlier)[0:1, :]
        rank = jnp.where(member > 0.5, rank, -1.0).astype(jnp.int32)
        placing = (slot == rank).astype(F32).astype(BF16)
        row_ref[...] = dot(placing, values).astype(BF16)


def rows_kernel(blocks, place_ref, down_in, gained_ref, squares_ref, router_ref, target_ref, *refs):
    row_refs, (stats_ref, down_ref, sem) = refs[: len(blocks)], refs[len(blocks) :]
    copy = pltpu.make_async_copy(down_in, down_ref, sem)
    copy.start()
    values = gained_ref[...]
    place_rows(place_ref[0], target_ref, values, blocks, row_refs)
    squares_row = jnp.transpose(squares_ref[...])
    height = stats_ref.shape[0]
    stats_ref[...] = jnp.concatenate(
        [dot_nt(router_ref[...], values), squares_row[: height - router_ref.shape[0], :]], axis=0
    )
    copy.wait()


def split_pair(x):
    high = x.astype(BF16).astype(F32)
    lane = lax.broadcasted_iota(jnp.int32, x.shape, 1)
    return jnp.where(lane < LANES // 2, high, x - high).astype(BF16)


def join_pair(ref, rows, start):
    return jnp.sum(ref[rows, start:].astype(F32), axis=-1, keepdims=True) * (2.0 / LANES)


def put_stats(ref, base, stats):
    height, tokens = stats.shape
    ref[base:, :] = jnp.zeros((ref.shape[0] - base, ref.shape[1]), BF16)
    terms = []
    for i in range(3):
        term = stats.astype(BF16)
        stats = stats - term.astype(F32)
        terms.append(term.astype(F32))
    pad = jnp.zeros((ref.shape[0] - base - height, 3 * tokens), F32)
    ref[base:, : 3 * tokens] = jnp.concatenate(
        [jnp.concatenate(terms, axis=1), pad], axis=0
    ).astype(BF16)


def get_stats(ref, base, like):
    height, tokens = like.shape
    parts = ref[base:, : 3 * tokens].astype(F32)[:height]
    return parts[:, :tokens] + parts[:, tokens : 2 * tokens] + parts[:, 2 * tokens :]


def up_kernel(with_stats, rep_ref, gate_ref, up_ref, gain_ref, *rest):
    rows_ref, keep_ref, first_ref, second_ref = rest[-4:]
    count = rows_ref.shape[0]
    half = gate_ref.shape[1] // 2
    mine = pl.multiple_of(rep_ref[0] * half, LANES)
    other = pl.multiple_of((1 - rep_ref[0]) * half, LANES)
    rows = rows_ref[...]
    squares = jnp.zeros((count, LANES), F32)
    for i in range(gain_ref.shape[0]):
        plain = rows[:, i * LANES : (i + 1) * LANES].astype(F32) / gain_ref[i : i + 1, :].astype(F32)
        squares = squares + plain * plain
    squares = jnp.broadcast_to(jnp.sum(squares, axis=-1, keepdims=True), (count, LANES))
    first_ref[...] = dot(rows, gate_ref[:, pl.ds(other, half)]).astype(BF16)
    second_ref[:count, :half] = dot(rows, up_ref[:, pl.ds(other, half)]).astype(BF16)
    second_ref[:count, half:] = split_pair(squares)
    keep_ref[:, :half] = dot(rows, gate_ref[:, pl.ds(mine, half)])
    keep_ref[:, half : 2 * half] = dot(rows, up_ref[:, pl.ds(mine, half)])
    keep_ref[:, 2 * half :] = squares
    if with_stats:
        put_stats(second_ref, count, rest[0][...])


def add_kernel(with_stats, *refs):
    keep_ref, first_ref, second_ref, sum_ref, send_ref = refs[with_stats : with_stats + 5]
    count = keep_ref.shape[0]
    wide = keep_ref.shape[1] - LANES
    half = first_ref.shape[1]
    for start, ref in ((0, first_ref), (half, second_ref)):
        both = keep_ref[:, start : start + half] + ref[:count, :half].astype(F32)
        sum_ref[:, start : start + half] = both
        send_ref[:count, start : start + half] = both.astype(BF16)
    squares = keep_ref[:, wide:] + join_pair(second_ref, slice(0, count), half)
    sum_ref[:, wide:] = squares
    send_ref[:count, wide:] = split_pair(squares)
    if with_stats:
        stats_ref, total_ref = refs[0], refs[-1]
        stats = stats_ref[...] + get_stats(second_ref, count, stats_ref)
        total_ref[...] = stats
        put_stats(send_ref, count, stats)


def inner_kernel(features, with_stats, *refs):
    sum_ref, got_ref, inner_ref = refs[with_stats : with_stats + 3]
    count = sum_ref.shape[0]
    wide = sum_ref.shape[1] - LANES
    half = wide // 2
    squares = sum_ref[:, wide : wide + 1] + join_pair(got_ref, slice(0, count), wide)
    scale = lax.rsqrt(squares * (1.0 / features) + EPSILON)
    gate = (sum_ref[:, :half] + got_ref[:count, :half].astype(F32)) * scale
    up = (sum_ref[:, half:wide] + got_ref[:count, half:wide].astype(F32)) * scale
    inner_ref[...] = (gate * jax.nn.sigmoid(gate) * up).astype(BF16)
    if with_stats:
        stats_ref, total_ref = refs[0], refs[-1]
        total_ref[...] = stats_ref[...] + get_stats(got_ref, count, stats_ref)


def down_kernel(rep_ref, down_ref, mine_ref, other_ref, out_ref, inner):
    half = mine_ref.shape[1]
    for i in range(2):

        @pl.when(rep_ref[0] == i)
        def _():
            inner[:, i * half : (i + 1) * half] = mine_ref[...]
            inner[:, (1 - i) * half : (2 - i) * half] = other_ref[...]

    out_ref[...] = dot(inner[...], down_ref[...]).astype(BF16)


def gates_kernel(cap, features, place_ref, stats_ref, ids_ref, target_ref, *weight_refs):
    place = place_ref[0]
    top, tokens = ids_ref.shape
    stats = jnp.transpose(stats_ref[...])
    height = stats.shape[1]
    scale = lax.rsqrt(stats[:, height - 1 :] * (1.0 / features) + EPSILON)
    logits = stats * scale
    both = jnp.concatenate(
        [ids_ref[...], target_ref[...], jnp.zeros((8 - 2 * top, tokens), jnp.int32)], axis=0
    )
    both = jnp.transpose(both.astype(F32)).astype(jnp.int32)
    kinds = lax.broadcasted_iota(jnp.int32, stats.shape, 1)
    squashed = [
        jax.nn.sigmoid(
            jnp.sum(jnp.where(kinds == both[:, k : k + 1], logits, 0.0), axis=-1, keepdims=True)
        )
        for k in range(top)
    ]
    whole = functools.reduce(lambda a, b: a + b, squashed)
    blocks = jnp.bitwise_xor(lax.broadcasted_iota(jnp.int32, (tokens, LANES), 1), place)
    named = [both[:, top + k : top + k + 1] == blocks for k in range(top)]
    member = functools.reduce(lambda a, b: a + b, [x.astype(F32) for x in named])
    later = (
        lax.broadcasted_iota(jnp.int32, (tokens, tokens), 0)
        > lax.broadcasted_iota(jnp.int32, (tokens, tokens), 1)
    ).astype(F32).astype(BF16)
    rank = dot(later, member.astype(BF16))
    slot = lax.broadcasted_iota(jnp.int32, (tokens, cap), 1)
    for j, weights_ref in enumerate(weight_refs):
        weights = jnp.zeros((tokens, cap), F32)
        for k in range(top):
            at = jnp.where(named[k][:, j : j + 1], rank[:, j : j + 1], -1.0).astype(jnp.int32)
            weights = weights + jnp.where(slot == at, squashed[k] / whole, 0.0)
        high = weights.astype(BF16)
        weights_ref[:tokens, :] = high
        weights_ref[tokens:, :] = (weights - high.astype(F32)).astype(BF16)


def mix_kernel(count, partial_ref, *rest):
    weights, answers, out_ref = rest[:count], rest[count : 2 * count], rest[-1]
    tokens = partial_ref.shape[0]
    total = partial_ref[...]
    for weights_ref, answer_ref in zip(weights, answers):
        mixed = dot(weights_ref[...], answer_ref[...])
        total = total + (mixed[:tokens] + mixed[tokens:])
    out_ref[...] = total.astype(out_ref.dtype)


def swap(x, axis):
    return lax.ppermute(x, axis, [(0, 1), (1, 0)])


def direct(
    stream,
    query_proj,
    key_proj,
    value_projected,
    expert_ids,
    expert_home,
    router,
    norm_gain,
    w_gate,
    w_up,
    w_down,
):
    tokens, width = stream.shape
    top = expert_ids.shape[1]
    n = lax.axis_size("ctx")
    features = width * lax.axis_size(("section", "rep"))
    experts = router.shape[1]
    hid = w_gate.shape[2]
    wide = hid + LANES
    cap = capacity_of(tokens, top, n)
    where = lax.axis_index("ctx").astype(jnp.int32).reshape(1)
    side = lax.axis_index("rep").astype(jnp.int32).reshape(1)
    heads = width // HEAD_SIZE
    group_width = features // key_proj.shape[1]
    kv_head = (lax.axis_index(("section", "rep")) * heads // group_width).astype(jnp.int32).reshape(1)

    def exchange(x, j):
        return lax.ppermute(x, "ctx", [(i, i ^ j) for i in range(n)])

    def like(x):
        return jax.ShapeDtypeStruct(x.shape, x.dtype)

    own_kv, part = vmem_call(
        prepare_kernel,
        [jax.ShapeDtypeStruct((tokens, w * HEAD_SIZE), BF16) for w in (2, 1)],
        [kv_head, side],
        [],
        remote=[key_proj, value_projected],
        scratch=[pltpu.SemaphoreType.DMA((2,))],
    )
    sources = [query_proj, stream, norm_gain.reshape(width // LANES, LANES), router.T, expert_ids.T]
    queries, stream, gain, router_rows, ids_rows, target = vmem_call(
        functools.partial(fetch_kernel, experts),
        [like(x) for x in sources] + [jax.ShapeDtypeStruct((top, tokens), jnp.int32)],
        [],
        [],
        remote=[*sources, expert_home.reshape(1, experts)],
        after=[part],
        scratch=[pltpu.VMEM((1, experts), jnp.int32), pltpu.SemaphoreType.DMA((6,))],
    )
    distance = sorted(range(1, n), key=lambda j: (j < n // 2, j))
    near_kv = exchange(part, 1)
    far_kv = lax.ppermute(
        own_kv, ("ctx", "rep"), [(2 * i + r, 2 * (i ^ (2 + r)) + r) for i in range(n) for r in range(2)]
    )
    stat_rows = -(-(experts + 1) // 8) * 8

    chain = [0] + [distance[0], *distance[:0:-1]]
    block = jax.ShapeDtypeStruct((cap, width), BF16)
    weights = [w_gate[0], w_up[0]]
    hidden, gained, squares, first_rows, gate, up = vmem_call(
        functools.partial(attend_kernel, n, chain[1]),
        [
            jax.ShapeDtypeStruct((tokens, width), F32),
            jax.ShapeDtypeStruct((tokens, width), BF16),
            jax.ShapeDtypeStruct((tokens, LANES), F32),
            block,
        ]
        + [like(x) for x in weights],
        [where, side],
        [queries, stream, gain, target, own_kv, near_kv, swap(near_kv, "rep")]
        + [far_kv, swap(far_kv, "rep")],
        remote=weights,
        scratch=[
            pltpu.VMEM((n * tokens, HEAD_SIZE), BF16),
            pltpu.VMEM((n * tokens, HEAD_SIZE), BF16),
            pltpu.SemaphoreType.DMA((2,)),
        ],
    )
    others = [j for j in range(n) if j != chain[1]]
    *rows, stats, down = vmem_call(
        functools.partial(rows_kernel, others),
        [block] * (n - 1) + [jax.ShapeDtypeStruct((stat_rows, tokens), F32), like(w_down[0])],
        [where],
        [gained, squares, router_rows, target],
        remote=[w_down[0]],
        scratch=[pltpu.SemaphoreType.DMA],
    )
    rows = {chain[1]: first_rows, **dict(zip(others, rows))}
    arrived = {j: exchange(rows[j], j) for j in distance}
    arrived[0] = rows[0]

    extra = -(-stat_rows // 16) * 16
    state = {}
    made = {"last": hidden, "stats": stats, "partial": hidden}

    def run(body, out_shape, scalars, arrays, scratch=(), held=True):
        outs = vmem_call(
            body, out_shape, scalars, arrays, after=[made["last"]], scratch=scratch, held=held
        )
        made["last"] = outs[0] if isinstance(outs, (tuple, list)) else outs
        return outs

    def stat_part(j):
        return (1, [made["stats"]], [like(stats)], extra) if j == 1 else (0, [], [], 0)

    def up_step(j):
        flag, given, made_too, more = stat_part(j)
        keep, first, second = run(
            functools.partial(up_kernel, flag),
            [
                jax.ShapeDtypeStruct((cap, wide), F32),
                jax.ShapeDtypeStruct((cap, hid // 2), BF16),
                jax.ShapeDtypeStruct((cap + more, hid // 2 + LANES), BF16),
            ],
            [side],
            [gate, up, gain] + given + [arrived[j]],
        )
        state[j] = (keep, swap(first, "rep"), swap(second, "rep"))

    def add_step(j):
        flag, given, made_too, more = stat_part(j)
        both, send, *rest = run(
            functools.partial(add_kernel, flag),
            [jax.ShapeDtypeStruct((cap, wide), F32), jax.ShapeDtypeStruct((cap + more, wide), BF16)]
            + made_too,
            [],
            given + list(state[j]),
        )
        if rest:
            made["stats"] = rest[0]
        state[j] = (both, swap(send, "section"))

    def inner_step(j):
        flag, given, made_too, more = stat_part(j)
        inner, *rest = run(
            functools.partial(inner_kernel, features, flag),
            [jax.ShapeDtypeStruct((cap, hid // 2), BF16)] + made_too,
            [],
            given + list(state[j]),
        )
        if rest:
            made["stats"] = rest[0]
        state[j] = (inner, swap(inner, "rep"))

    def down_step(j):
        answer = run(
            down_kernel,
            jax.ShapeDtypeStruct((cap, width), BF16),
            [side],
            [down, *state[j]],
            scratch=[pltpu.VMEM((cap, hid), BF16)],
        )
        state[j] = exchange(answer, j) if j else answer

    def gates_step():
        made["weights"] = run(
            functools.partial(gates_kernel, cap, features),
            [jax.ShapeDtypeStruct((2 * tokens, cap), BF16)] * n,
            [where],
            [made["stats"], ids_rows, target],
        )

    def mix_step(blocks, dtype=F32, held=True):
        made["partial"] = run(
            functools.partial(mix_kernel, len(blocks)),
            jax.ShapeDtypeStruct((tokens, width), dtype),
            [],
            [made["partial"]] + [made["weights"][j] for j in blocks] + [state[j] for j in blocks],
            held=held,
        )

    steps = dict(u=up_step, a=add_step, i=inner_step, d=down_step, m=lambda j: mix_step([j]))
    plan = (
        *("u0", "a0", "u1", "i0", "a1", "u2", "a2", "u3", "i1", "d0"),
        *("d1", "a3", "i2", "d2", "g", "i3", "m0", "m1", "d3", "m2"),
    )
    for name in plan:
        if name == "g":
            gates_step()
        elif int(name[1]) < n - (name[0] == "m"):
            steps[name[0]](chain[int(name[1])])
    early = [chain[int(name[1])] for name in plan if name[0] == "m" and int(name[1]) < n - 1]
    mix_step([j for j in chain if j not in early], BF16, held=False)
    return made["partial"]


def capacity_of(tokens, top, n):
    return min(tokens, max(2, 5 * tokens * top // (4 * n)))


def score_update(running, query_matrix, query_pos, key_block, value_block, key_anchor):
    run_max, run_sum, run_acc = running
    key_len = key_block.shape[0]
    scores = jnp.einsum(
        "tha,pa->htp", query_matrix, key_block, preferred_element_type=jnp.float32
    ) * (1.0 / math.sqrt(HEAD_SIZE))
    key_pos = key_anchor + jnp.arange(key_len, dtype=jnp.int32)
    visible = query_pos[:, None] >= key_pos[None, :]
    scores = jnp.where(visible, scores, HIDDEN_MASK)
    new_max = jnp.maximum(run_max, jnp.max(scores, axis=-1))
    expo = jnp.where(visible, jnp.exp(scores - new_max[..., None]), 0.0)
    factor = jnp.exp(run_max - new_max)
    new_sum = run_sum * factor + jnp.sum(expo, axis=-1)
    weights = expo.astype(jnp.bfloat16)
    new_acc = run_acc * factor[..., None] + jnp.einsum(
        "htp,pa->hta", weights, value_block, preferred_element_type=jnp.float32
    )
    return (new_max, new_sum, new_acc)


def absorb_rows(running, query_matrix, query_pos, key_rows, value_rows, anchor):
    piece_len = key_rows.shape[0]
    if piece_len > 512 and piece_len % 512 == 0:
        blocks = piece_len // 512
        key_tiles = key_rows.reshape(blocks, 512, key_rows.shape[1])
        value_tiles = value_rows.reshape(blocks, 512, value_rows.shape[1])
        anchors = anchor + 512 * jnp.arange(blocks, dtype=jnp.int32)

        def advance(state_now, tile):
            return (
                score_update(state_now, query_matrix, query_pos, tile[0], tile[1], tile[2]),
                None,
            )

        running, ignored = lax.scan(advance, running, (key_tiles, value_tiles, anchors))
        return running
    return score_update(running, query_matrix, query_pos, key_rows, value_rows, anchor)


def general(
    stream,
    query_proj,
    key_proj,
    value_projected,
    expert_ids,
    expert_home,
    router,
    norm_gain,
    w_gate,
    w_up,
    w_down,
):
    tok_rows, local_width = stream.shape
    top_count = expert_ids.shape[1]
    columns = lax.axis_size("ctx")
    features = local_width * lax.axis_size(("section", "rep"))
    capacity = capacity_of(tok_rows, top_count, columns)
    place = lax.axis_index("ctx")
    feature_index = lax.axis_index(("section", "rep"))
    heads_dev = local_width // HEAD_SIZE
    group_width = features // key_proj.shape[1]
    kv_head = feature_index * heads_dev // group_width
    query_matrix = query_proj.reshape(tok_rows, heads_dev, HEAD_SIZE)
    query_pos = place * tok_rows + jnp.arange(tok_rows, dtype=jnp.int32)
    initial = (
        jnp.full((heads_dev, tok_rows), HIDDEN_MASK, jnp.float32),
        jnp.zeros((heads_dev, tok_rows), jnp.float32),
        jnp.zeros((heads_dev, tok_rows, HEAD_SIZE), jnp.float32),
    )
    key_single = lax.dynamic_slice_in_dim(key_proj, kv_head * HEAD_SIZE, HEAD_SIZE, 1)
    value_single = lax.dynamic_slice_in_dim(value_projected, kv_head * HEAD_SIZE, HEAD_SIZE, 1)
    run_max, run_sum, run_acc = absorb_rows(
        initial,
        query_matrix,
        query_pos,
        lax.all_gather(key_single, "ctx", axis=0, tiled=True),
        lax.all_gather(value_single, "ctx", axis=0, tiled=True),
        jnp.int32(0),
    )
    attended = jnp.transpose(run_acc / run_sum[..., None], (1, 0, 2)).reshape(tok_rows, local_width)
    hidden = stream.astype(jnp.float32) + attended
    total_sq = lax.psum(jnp.sum(hidden * hidden, axis=-1), ("section", "rep"))
    scale_rows = lax.rsqrt(total_sq / features + EPSILON)
    normed = (hidden * scale_rows[:, None] * norm_gain.astype(jnp.float32)[None, :]).astype(
        jnp.bfloat16
    )
    logits = lax.psum(dot(normed, router), ("section", "rep"))
    experts_all = logits.shape[1]
    one_hot = expert_ids[:, :, None] == jnp.arange(experts_all, dtype=jnp.int32)[None, None, :]
    picked = jnp.sum(jnp.where(one_hot, logits[:, None, :], 0.0), axis=-1)
    squashed = jax.nn.sigmoid(picked)
    gates = squashed / jnp.sum(squashed, axis=-1, keepdims=True)
    target = jnp.sum(jnp.where(one_hot, expert_home[None, None, :], 0), axis=-1)
    named = target[:, :, None] == jnp.arange(columns, dtype=jnp.int32)[None, None, :]
    member = jnp.any(named, axis=1).astype(jnp.bfloat16)
    before = jnp.tril(jnp.ones((tok_rows, tok_rows), jnp.bfloat16), -1)
    rank = dot(before, member).astype(jnp.int32)
    rank = jnp.sum(jnp.where(named, rank[:, None, :], 0), axis=-1)
    slot_index = (target * capacity + rank).reshape(-1)
    placing = slot_index[None, :] == jnp.arange(columns * capacity, dtype=jnp.int32)[:, None]
    placing = jnp.any(placing.reshape(columns * capacity, tok_rows, top_count), axis=-1).astype(
        jnp.bfloat16
    )
    outgoing = dot(placing, normed).astype(jnp.bfloat16)
    outgoing = outgoing.reshape(columns, capacity, local_width)
    received = lax.all_to_all(outgoing, "ctx", split_axis=0, concat_axis=0, tiled=True)
    flat_rows = received.reshape(-1, local_width)
    gate_part = dot(flat_rows, w_gate[0])
    up_part = dot(flat_rows, w_up[0])
    gate_full = lax.psum(gate_part.astype(jnp.bfloat16), ("section", "rep")).astype(jnp.float32)
    up_full = lax.psum(up_part.astype(jnp.bfloat16), ("section", "rep")).astype(jnp.float32)
    inner = (jax.nn.silu(gate_full) * up_full).astype(jnp.bfloat16)
    answer = dot(inner, w_down[0]).astype(jnp.bfloat16)
    returned = lax.all_to_all(
        answer.reshape(received.shape), "ctx", split_axis=0, concat_axis=0, tiled=True
    )
    flat_back = returned.reshape(columns * capacity, local_width)
    picked_rows = flat_back[slot_index].reshape(tok_rows, top_count, local_width)
    mixed = jnp.sum(gates[:, :, None] * picked_rows.astype(jnp.float32), axis=1)
    return (hidden + mixed).astype(jnp.bfloat16)


def solution(mesh):
    size = dict(mesh.shape)
    pairs = size["section"] == 2 and size["rep"] == 2
    short = size["ctx"] == 4
    placed = (
        P(("group", "ctx"), ("section", "rep")),
        P(("group", "ctx"), ("section", "rep")),
        P(("group", "ctx"), None),
        P(("group", "ctx"), None),
        P(("group", "ctx"), None),
        P(),
        P(("section", "rep"), None),
        P(("section", "rep")),
        P("ctx", ("section", "rep"), None),
        P("ctx", ("section", "rep"), None),
        P("ctx", None, ("section", "rep")),
    )
    return jax.shard_map(
        direct if pairs and short else general,
        mesh=mesh,
        in_specs=placed,
        out_specs=P(("group", "ctx"), ("section", "rep")),
        check_vma=False,
    )
```
